32 devices in a mesh: cls: 4 (over x, core), dom: 8 (over z, y).
Axes of the slice: x: 2, y: 2, z: 4, core: 2. Of those that a mesh axis runs over, the one named last changes fastest.
Arguments:
- particles: bfloat16 [128, 36864], P(('cls', 'dom')), may hold values from -6 to 6
- references: bfloat16 [200, 36864], P('cls'), may hold values from -0.03125 to 0.03125
- candidates: int32 [128, 8], P(('cls', 'dom')), may hold values from 0 to 199, as said below
- offsets: int32 [128, 2], P(('cls', 'dom')), may hold values from -7 to 7
Outputs:
- class_average: bfloat16 [200, 36864], P('cls')
The draws below stay inside these ranges and needn't reach their ends.
Inputs may be any that keep to these rules, and one draw needn't show every extreme that they name: `candidates`: each particle lists 8 distinct classes, 4 of them with each of two class owners, the owner of class c being c // (200 / number of cls groups). Of the 4 particles of one device at most 2 list classes of one owner, and on every device some owner is listed by exactly 2.
All inputs are finite; a program needn't handle non-finite values.
Results may differ from the reference program's by a relative error of at most 0.0074.
Values may be sent and summed in bfloat16 or wider, within the bound.
No kernel may reach another device: no remote copies, remote signals or barrier semaphores. Data moves between devices by JAX's collectives and lax.ppermute only.
A program may use at most 128 MiB of HBM per device.

```python
import math
import jax
import jax.numpy as jnp
from jax import lax

CLASSES = 200
CYCLES = 128
ANGLES = 144
ROT = 36
SHIFTS = 5
CAND = 8
BOX = 256
PART_DEV = 4
CAP = 2
CLS_LOC = 50
PIXV = 36864
PARTICLES = 128
N_CLS = 4


def route_tables(key):
    block_list = PARTICLES // PART_DEV
    half_count = CAND // 2

    def one_block(block_key):
        subkeys = jax.random.split(block_key, 6)
        owner_list = jax.random.permutation(subkeys[0], N_CLS)
        ordering = jax.random.permutation(subkeys[1], PART_DEV)
        first_owner = owner_list[ordering // CAP]
        second_owner = owner_list[2 + ordering % (N_CLS - 2)]
        pick_first = jax.vmap(lambda sub_key: jax.random.permutation(sub_key, CLS_LOC)[:half_count])(jax.random.split(subkeys[2], PART_DEV))
        pick_second = jax.vmap(lambda sub_key: jax.random.permutation(sub_key, CLS_LOC)[:half_count])(jax.random.split(subkeys[3], PART_DEV))
        listed = jnp.concatenate([first_owner[:, None] * CLS_LOC + pick_first, second_owner[:, None] * CLS_LOC + pick_second], axis=1)
        mixing = jax.vmap(lambda sub_key: jax.random.permutation(sub_key, CAND))(jax.random.split(subkeys[4], PART_DEV))
        shuffled = jnp.take_along_axis(listed, mixing, axis=1)
        prior_shift = jax.random.randint(subkeys[5], (PART_DEV, 2), -7, 8, dtype=jnp.int32)
        return (shuffled, prior_shift, listed[:, 0])
    shuffled, prior_shift, leading = jax.vmap(one_block)(jax.random.split(jax.random.fold_in(key, 11), block_list))
    return (shuffled.reshape(PARTICLES, CAND), prior_shift.reshape(PARTICLES, 2))


def reference_field(key):
    base_key = jax.random.fold_in(key, 29)
    field = jnp.clip(jax.random.normal(base_key, (CLASSES, ANGLES, 2, CYCLES), jnp.float32), -6.0, 6.0) * PIXV ** (-0.5)
    return field


def draw_references(key, part):
    return reference_field(key).reshape(CLASSES, PIXV).astype(jnp.bfloat16)


def draw_candidates(key, part):
    return route_tables(key)[0]


def draw_offsets(key, part):
    return route_tables(key)[1]


def draw_particles(key, part):
    base_key = jax.random.fold_in(key, 37)
    values = jnp.clip(jax.random.normal(base_key, (PARTICLES, ANGLES, 2, CYCLES), jnp.float32), -6.0, 6.0)
    return values.reshape(PARTICLES, PIXV).astype(jnp.bfloat16)


def setup_inputs(seed: int = 0) -> dict:
    arg_keys = jax.random.split(jax.random.key(seed), 5)
    particles = draw_particles(jax.random.fold_in(arg_keys[4], 71), 0)
    references = draw_references(jax.random.fold_in(arg_keys[4], 71), 0)
    candidates = draw_candidates(jax.random.fold_in(arg_keys[4], 71), 0)
    offsets = draw_offsets(jax.random.fold_in(arg_keys[4], 71), 0)
    return {"particles": particles, "references": references, "candidates": candidates, "offsets": offsets}


SOFTMAX_WARMTH = 2.0
PRIOR_MASS = 1.0
SHIFT_X_STEPS = (0, 1, -1, 0, 0)
SHIFT_Y_STEPS = (0, 0, 0, 1, -1)


def phase_angles(move_x, move_y):
    theta = 2.0 * math.pi * jnp.arange(ANGLES, dtype=jnp.float32) / ANGLES
    radius = jnp.arange(1, CYCLES + 1, dtype=jnp.float32)
    along = jnp.cos(theta)[:, None] * move_x.astype(jnp.float32)[..., None, None] + jnp.sin(theta)[:, None] * move_y.astype(jnp.float32)[..., None, None]
    return (2.0 * math.pi / BOX) * along * radius


def shift_images(images, phase):
    real_part = images[..., 0, :].astype(jnp.float32)
    imag_part = images[..., 1, :].astype(jnp.float32)
    cosine = jnp.cos(phase)
    sine = jnp.sin(phase)
    return jnp.stack([real_part * cosine + imag_part * sine, imag_part * cosine - real_part * sine], axis=-2).astype(jnp.bfloat16)


def reference(particles, references, candidates, offsets):
    block_width = PIXV // ROT
    turn_index = jnp.arange(ROT, dtype=jnp.int32)
    source_block = (turn_index[:, None] + turn_index[None, :]) % ROT
    steps_x = jnp.array(SHIFT_X_STEPS, dtype=jnp.int32)
    steps_y = jnp.array(SHIFT_Y_STEPS, dtype=jnp.int32)

    def one_particle(carry, element):
        totals, masses = carry
        particle_image, listed, prior_shift = element
        phase = phase_angles(prior_shift[0] + steps_x, prior_shift[1] + steps_y)
        shifted = shift_images(particle_image.reshape(ANGLES, 2, CYCLES)[None], phase)
        shifted = shifted.reshape(SHIFTS, ROT, block_width)
        rotated_images = shifted[:, source_block, :].reshape(SHIFTS * ROT, PIXV)
        selected_candidates = references[listed]
        score_values = SOFTMAX_WARMTH * jnp.dot(rotated_images, selected_candidates.T, preferred_element_type=jnp.float32)
        best_score = jnp.max(score_values)
        exponent = jnp.exp(score_values - best_score)
        weight = (exponent / jnp.sum(exponent)).astype(jnp.bfloat16)
        contrib = jnp.dot(weight.T, rotated_images, preferred_element_type=jnp.float32)
        totals = totals.at[listed].add(contrib)
        masses = masses.at[listed].add(jnp.sum(weight.astype(jnp.float32), axis=0))
        return (totals, masses), None

    initial = (jnp.zeros((CLASSES, PIXV), jnp.float32), jnp.zeros((CLASSES,), jnp.float32))
    (totals, masses), unused = lax.scan(one_particle, initial, (particles, candidates, offsets))
    return (totals / (masses + PRIOR_MASS)[:, None]).astype(jnp.bfloat16)
```

```python
import functools
import math

import jax
import jax.numpy as jnp
import numpy as np
from jax import lax
from jax.experimental import pallas as pl
from jax.experimental.pallas import tpu as pltpu
from jax.sharding import PartitionSpec as P

CYCLES = 128
ANGLES = 144
ROT = 36
SHIFTS = 5
BOX = 256
LANES = 128
SPAN = 40
STEP_ANGLES = ANGLES // ROT
REACH = 8

SOFTMAX_WARMTH = 2.0
PRIOR_MASS = 1.0
NEGATIVE = -1e30
SHIFT_X_STEPS = (0, 1, -1, 0, 0)
SHIFT_Y_STEPS = (0, 0, 0, 1, -1)
META_ROWS = 16
VMEM_LIMIT = 60 * 1024 * 1024


def trig_tables():
    theta = 2.0 * np.pi * np.arange(ANGLES) / ANGLES
    radius = np.arange(1, CYCLES + 1)
    out = np.zeros((4, REACH + 1, STEP_ANGLES, SPAN, CYCLES), np.float32)
    for axis, direction in enumerate((np.cos(theta), np.sin(theta))):
        for t in range(REACH + 1):
            phase = 2.0 * np.pi / BOX * t * direction[:, None] * radius[None, :]
            for part, fn in enumerate((np.cos, np.sin)):
                table = fn(phase).reshape(ROT, STEP_ANGLES, CYCLES).transpose(1, 0, 2)
                out[2 * axis + part, t, :, :ROT] = table[:, ::-1]
    return out.reshape(4, REACH + 1, STEP_ANGLES * SPAN, CYCLES)


def prep_kernel(groups, capacity, local, cand_ref, off_ref, image_ref, out_ref):
    count, listed = cand_ref.shape
    rows = image_ref.shape[1]
    half = listed // 2
    out_ref[:, :, rows:, :] = jnp.zeros((groups, capacity, META_ROWS, LANES), out_ref.dtype)
    cand = [[cand_ref[u, k] for k in range(listed)] for u in range(count)]
    owner = [[lax.div(c, local) for c in row] for row in cand]
    pair = []
    for u in range(count):
        first = owner[u][0]
        second = first
        for k in range(1, listed):
            second = jnp.where(owner[u][k] != first, owner[u][k], second)
        pair.append((first, second))
    lane = lax.broadcasted_iota(jnp.int32, (META_ROWS, LANES), 1)
    for u in range(count):
        rank = []
        for side in range(2):
            value = jnp.int32(0)
            for v in range(u):
                lists = (pair[v][0] == pair[u][side]) | (pair[v][1] == pair[u][side])
                value = value + jnp.where(lists, 1, 0)
            rank.append(value)
        for side in range(2):
            mine, other = pair[u][side], pair[u][1 - side]
            entries = [jnp.int32(1), off_ref[u, 0], off_ref[u, 1], other, rank[1 - side]]
            classes = [jnp.int32(0)] * half
            seen = jnp.int32(0)
            for k in range(listed):
                hit = owner[u][k] == mine
                for j in range(half):
                    classes[j] = jnp.where(hit & (seen == j), cand[u][k] - mine * local, classes[j])
                seen = seen + jnp.where(hit, 1, 0)
            entries += classes
            tile = jnp.zeros((META_ROWS, LANES), jnp.int32)
            for k, value in enumerate(entries):
                tile = jnp.where(lane == k, value, tile)
            out_ref[mine, rank[side], :rows, :] = image_ref[u]
            out_ref[mine, rank[side], rows:, :] = tile.astype(jnp.float32).astype(out_ref.dtype)


def prepare(images, candidates, offsets, groups, local):
    count, rows, _ = images.shape
    capacity = count // 2
    smem = pl.BlockSpec(memory_space=pltpu.SMEM)
    vmem = pl.BlockSpec(memory_space=pltpu.VMEM)
    return pl.pallas_call(
        functools.partial(prep_kernel, groups, capacity, local),
        out_shape=jax.ShapeDtypeStruct((groups, capacity, rows + META_ROWS, LANES), images.dtype),
        in_specs=[smem, smem, vmem],
        out_specs=vmem,
        name="prepare",
    )(candidates, offsets, images)


def load_image(source, rows, raw):
    group = 2 * STEP_ANGLES
    values = source.astype(jnp.float32)
    for block in range(rows // group):
        at = rows - (block + 1) * group
        raw[at : at + group, :] = values[block * group : (block + 1) * group]


def piece(raw, part):
    return raw[pl.ds(part, SPAN, stride=2 * STEP_ANGLES), :]


def axis_phase(table_ref, axis, step, move):
    size = jnp.abs(move)
    sign = jnp.where(move < 0, -1.0, 1.0).astype(jnp.float32)
    at = pl.ds(step * SPAN, SPAN)
    return table_ref[2 * axis, size, at, :], table_ref[2 * axis + 1, size, at, :] * sign


def read_meta(source, meta_vmem, row):
    meta_vmem[pl.ds(row, 1), :] = source.astype(jnp.float32)[0:1, :].astype(jnp.int32)


def score_kernel(
    image_ref, refs_ref, table_ref, weight_ref, stat_ref, raw, moved, picked, sums, meta_vmem, meta, sem
):
    slots = image_ref.shape[0]
    rows = image_ref.shape[1] - META_ROWS
    classes = picked.shape[0] // 48
    raw[...] = jnp.zeros_like(raw)
    moved[...] = jnp.zeros_like(moved)
    picked[...] = jnp.zeros_like(picked)
    sums[...] = jnp.zeros_like(sums)
    for slot in range(slots):
        read_meta(image_ref[slot, rows:, :], meta_vmem, slot)
    copy = pltpu.make_async_copy(meta_vmem, meta, sem)
    copy.start()
    copy.wait()
    lane = lax.broadcasted_iota(jnp.int32, (1, LANES), 1)
    used = SHIFTS * classes

    def one(slot, carry):
        load_image(image_ref[slot, :rows, :], rows, raw)
        filled = meta[slot, 0]
        base_x, base_y = meta[slot, 1], meta[slot, 2]
        for j in range(classes):
            picked[j * 48 : j * 48 + ROT, :] = refs_ref[meta[slot, 5 + j]]
        for step in range(STEP_ANGLES):
            re, im = piece(raw, 2 * step), piece(raw, 2 * step + 1)
            for s in range(SHIFTS):
                cx, sx = axis_phase(table_ref, 0, step, base_x + SHIFT_X_STEPS[s])
                cy, sy = axis_phase(table_ref, 1, step, base_y + SHIFT_Y_STEPS[s])
                cosine = cx * cy - sx * sy
                sine = sx * cy + cx * sy
                left = pl.ds((2 * step) * LANES, LANES)
                right = pl.ds((2 * step + 1) * LANES, LANES)
                pad = jnp.zeros((8, LANES), jnp.float32)
                new_re = jnp.concatenate([re * cosine + im * sine, pad], axis=0)
                new_im = jnp.concatenate([im * cosine - re * sine, pad], axis=0)
                moved[s * LANES : s * LANES + 48, left] = new_re.astype(jnp.bfloat16)
                moved[s * LANES : s * LANES + 48, right] = new_im.astype(jnp.bfloat16)
        pairs = lax.dot_general(
            picked[...], moved[...], (((1,), (1,)), ((), ())), preferred_element_type=jnp.float32
        )
        for s in range(SHIFTS):
            for j in range(classes):
                block = pairs[j * 48 : j * 48 + SPAN, s * LANES : (s + 1) * LANES]
                turned = pltpu.roll(block, 0, 1, stride=1, stride_axis=0)
                sums[pl.ds(s * classes + j, 1), :] = jnp.sum(turned, axis=0, keepdims=True)
        raw_sums = sums[...]
        scores = SOFTMAX_WARMTH * (raw_sums + pltpu.roll(raw_sums, LANES - ROT, 1))
        lanes = lax.broadcasted_iota(jnp.int32, scores.shape, 1)
        lines = lax.broadcasted_iota(jnp.int32, scores.shape, 0)
        valid = (lanes < ROT) & (lines < used) & (filled > 0)
        scores = jnp.where(valid, scores, NEGATIVE)
        peak = jnp.max(jnp.max(scores, axis=0, keepdims=True), axis=1, keepdims=True)
        peak = jnp.where(filled > 0, peak, 0.0)
        weights = jnp.where(valid, jnp.exp(scores - peak), 0.0)
        total = jnp.sum(jnp.sum(weights, axis=0, keepdims=True), axis=1, keepdims=True)
        total = jnp.where(filled > 0, total, 1.0)
        stat_ref[pl.ds(2 * slot, 1), :] = jnp.broadcast_to(peak, (1, LANES))
        stat_ref[pl.ds(2 * slot + 1, 1), :] = jnp.broadcast_to(total, (1, LANES))
        w = [weights[s * classes : (s + 1) * classes] for s in range(SHIFTS)]
        low = w[0] + pltpu.roll(w[1] + w[2], SPAN, 1) + pltpu.roll(w[1] - w[2], 2 * SPAN, 1)
        high = (w[3] + w[4]) + pltpu.roll(w[3] - w[4], SPAN, 1)
        weight_ref[slot, :classes, :] = low
        weight_ref[slot, classes:, :] = high
        return carry

    lax.fori_loop(0, slots, one, 0)


def score(arrived, refs, tables, classes):
    slots, rows, _ = arrived.shape
    vmem = pl.BlockSpec(memory_space=pltpu.VMEM)
    width = refs.shape[2]
    return pl.pallas_call(
        score_kernel,
        out_shape=(
            jax.ShapeDtypeStruct((slots, 2 * classes, LANES), jnp.float32),
            jax.ShapeDtypeStruct((2 * slots, LANES), jnp.float32),
        ),
        in_specs=[vmem, vmem, vmem],
        out_specs=(vmem, vmem),
        scratch_shapes=[
            pltpu.VMEM((2 * STEP_ANGLES * SPAN, LANES), jnp.float32),
            pltpu.VMEM((SHIFTS * LANES, width), jnp.bfloat16),
            pltpu.VMEM((48 * classes, width), jnp.bfloat16),
            pltpu.VMEM((24, LANES), jnp.float32),
            pltpu.VMEM((slots, LANES), jnp.int32),
            pltpu.SMEM((slots, LANES), jnp.int32),
            pltpu.SemaphoreType.DMA,
        ],
        compiler_params=pltpu.CompilerParams(vmem_limit_bytes=VMEM_LIMIT),
        cost_estimate=pl.CostEstimate(flops=10**10, bytes_accessed=10**7, transcendentals=0),
        name="score",
    )(arrived, refs, tables)


def sum_kernel(
    z_size, y_size, wave, *refs
):
    count = z_size * y_size
    image_refs = refs[:count]
    (
        weight_ref, stat_ref, table_ref, place_ref, out_ref,
        images, raw, moved, totals, mass, meta_vmem, meta, image_sem, meta_sem,
    ) = refs[count:]
    slots = image_refs[0].shape[0]
    rows = image_refs[0].shape[1] - META_ROWS
    classes = weight_ref.shape[2] // 2
    local = out_ref.shape[0]
    width = moved.shape[1]
    depth = images.shape[0]
    waves = count // wave
    capacity = slots // stat_ref.shape[0]

    def copies(w):
        return [
            pltpu.make_async_copy(
                image_refs[w * wave + b],
                images.at[w % depth, pl.ds(b * slots, slots)],
                image_sem.at[w % depth, b],
            )
            for b in range(wave)
        ]

    for w in range(min(depth, waves)):
        for copy in copies(w):
            copy.start()
    raw[...] = jnp.zeros_like(raw)
    moved[...] = jnp.zeros_like(moved)
    mass[...] = jnp.zeros_like(mass)
    totals[...] = jnp.zeros_like(totals)
    my_cls, my_z, my_y = place_ref[0], place_ref[1], place_ref[2]
    lane = lax.broadcasted_iota(jnp.int32, (2 * classes, LANES), 1)
    lane_wide = lax.broadcasted_iota(jnp.int32, (SPAN, LANES), 1)

    for w in range(waves):
        for copy in copies(w):
            copy.wait()
        here = images.at[w % depth]
        for i in range(wave * slots):
            read_meta(here[i, rows:, :], meta_vmem, i)
        meta_copy = pltpu.make_async_copy(meta_vmem, meta, meta_sem)
        meta_copy.start()
        meta_copy.wait()

        def one(i, carry):
            b = w * wave + i // slots
            slot = i % slots
            q_z = lax.rem(my_z - lax.rem(b, z_size) + z_size, z_size)
            q_y = lax.rem(my_y - b // z_size + y_size, y_size)
            q = q_z * y_size + q_y
            source = slot // capacity
            other, other_rank = meta[i, 3], meta[i, 4]
            mine = stat_ref[my_cls, q, pl.ds(2 * slot, 2), :]
            theirs = stat_ref[other, q, pl.ds(2 * (source * capacity + other_rank), 2), :]
            peak = jnp.maximum(mine[0:1], theirs[0:1])
            gain = jnp.exp(mine[0:1] - peak)
            factor = gain / (mine[1:2] * gain + theirs[1:2] * jnp.exp(theirs[0:1] - peak))
            weights = weight_ref[q, slot] * factor
            load_image(here[i, :rows, :], rows, raw)
            base_x, base_y = meta[i, 1], meta[i, 2]
            for step in range(STEP_ANGLES):
                re, im = piece(raw, 2 * step), piece(raw, 2 * step + 1)
                cx, sx = axis_phase(table_ref, 0, step, base_x)
                cy, sy = axis_phase(table_ref, 1, step, base_y)
                cosine = cx * cy - sx * sy
                sine = sx * cy + cx * sy
                re, im = re * cosine + im * sine, im * cosine - re * sine
                at = pl.ds(step * SPAN, SPAN)
                c1, s1 = table_ref[0, 1, at, :], table_ref[1, 1, at, :]
                c2, s2 = table_ref[2, 1, at, :], table_ref[3, 1, at, :]
                pad = jnp.zeros((8, LANES), jnp.float32)
                left = pl.ds((2 * step) * LANES, LANES)
                right = pl.ds((2 * step + 1) * LANES, LANES)
                moved[:LANES, left] = jnp.concatenate([re, re * c1, im * s1, pad], axis=0).astype(jnp.bfloat16)
                moved[:LANES, right] = jnp.concatenate([im, im * c1, -re * s1, pad], axis=0).astype(jnp.bfloat16)
                moved[LANES : LANES + 2 * SPAN, left] = jnp.concatenate([re * c2, im * s2], axis=0).astype(jnp.bfloat16)
                moved[LANES : LANES + 2 * SPAN, right] = jnp.concatenate([im * c2, -re * s2], axis=0).astype(
                    jnp.bfloat16
                )
            parts = []
            for k in range(3):
                part = jnp.where((lane >= k * SPAN) & (lane < (k + 1) * SPAN), weights, 0.0)
                parts.append(part + pltpu.roll(part, LANES - ROT, 1))
            blocks = []
            for j in range(classes):
                line = []
                for half in range(2):
                    at = half * classes + j
                    turned = [
                        pltpu.roll(
                            jnp.broadcast_to(parts[k][at : at + 1], (SPAN, LANES)), 1, 1, stride=1, stride_axis=0
                        )
                        for k in range(3 - half)
                    ]
                    tile = jnp.where(lane_wide < SPAN, turned[0], turned[1])
                    if half == 0:
                        tile = jnp.where(lane_wide < 2 * SPAN, tile, turned[2])
                    line.append(tile)
                blocks.append(jnp.concatenate(line, axis=1))
            spread = jnp.concatenate(blocks, axis=0).astype(jnp.bfloat16)
            added = jnp.dot(spread, moved[...], preferred_element_type=jnp.float32)
            plain = jnp.where(lane < 2 * SPAN, weights, 0.0)
            plain_high = jnp.where(lane < SPAN, weights, 0.0)
            for j in range(classes):
                c = meta[i, 5 + j]
                for tile in range(width // LANES):
                    at = pl.ds(pl.multiple_of(tile * local * SPAN + c * SPAN, 8), SPAN)
                    totals[at, :] += added[j * SPAN : (j + 1) * SPAN, tile * LANES : (tile + 1) * LANES]
                mass[pl.ds(c, 1), :] += plain[j : j + 1] + plain_high[classes + j : classes + j + 1]
            return carry

        lax.fori_loop(0, wave * slots, one, 0)
        if w + depth < waves:
            for copy in copies(w + depth):
                copy.start()

    scale = 1.0 / (jnp.sum(mass[:local, :], axis=1, keepdims=True) + PRIOR_MASS)
    for turn in range(ROT):
        for tile in range(width // LANES):
            line = totals[pl.ds(tile * local * SPAN + ROT - 1 - turn, local, stride=SPAN), :]
            out_ref[:, pl.ds(turn * width + tile * LANES, LANES)] = (line * scale).astype(out_ref.dtype)


def class_sum(buffers, weights, stats, tables, place, z_size, y_size, local, width, classes):
    slots, rows, _ = buffers[0].shape
    count = len(buffers)
    wave = math.gcd(count, 8)
    depth = min(2, count // wave)
    vmem = pl.BlockSpec(memory_space=pltpu.VMEM)
    smem = pl.BlockSpec(memory_space=pltpu.SMEM)
    hbm = pl.BlockSpec(memory_space=pl.ANY)
    return pl.pallas_call(
        functools.partial(sum_kernel, z_size, y_size, wave),
        out_shape=jax.ShapeDtypeStruct((local, ROT * width), jnp.bfloat16),
        in_specs=[hbm] * count + [vmem, vmem, vmem, smem],
        out_specs=vmem,
        scratch_shapes=[
            pltpu.VMEM((depth, wave * slots, rows, LANES), jnp.bfloat16),
            pltpu.VMEM((2 * STEP_ANGLES * SPAN, LANES), jnp.float32),
            pltpu.VMEM((2 * LANES, width), jnp.bfloat16),
            pltpu.VMEM((width // LANES * local * SPAN, LANES), jnp.float32),
            pltpu.VMEM((-(-local // 8) * 8, LANES), jnp.float32),
            pltpu.VMEM((wave * slots, LANES), jnp.int32),
            pltpu.SMEM((wave * slots, LANES), jnp.int32),
            pltpu.SemaphoreType.DMA((depth, wave)),
            pltpu.SemaphoreType.DMA,
        ],
        compiler_params=pltpu.CompilerParams(vmem_limit_bytes=VMEM_LIMIT),
        cost_estimate=pl.CostEstimate(flops=2 * 10**10, bytes_accessed=10**7, transcendentals=0),
        name="class_sum",
    )(*buffers, weights, stats, tables, place)


def shards(z_size, y_size, particles, references, candidates, offsets):
    groups = lax.axis_size("cls")
    doms = lax.axis_size("dom")
    count, width = particles.shape
    local = references.shape[0]
    classes = candidates.shape[1] // 2
    block_width = width // ROT
    slots = groups * (count // 2)
    tables = jnp.asarray(trig_tables())
    images = particles.reshape(count, width // LANES, LANES)
    outgoing = prepare(images, candidates, offsets, groups, local)
    arrived = lax.all_to_all(outgoing, "cls", split_axis=0, concat_axis=0, tiled=True)
    arrived = arrived.reshape(slots, width // LANES + META_ROWS, LANES)
    refs = references.reshape(local, ROT, block_width)

    def along(dz, dy):
        return [
            (z * y_size + y, (z + dz) % z_size * y_size + (y + dy) % y_size)
            for z in range(z_size)
            for y in range(y_size)
        ]

    ring = [arrived]
    for _ in range(z_size - 1):
        ring.append(lax.ppermute(ring[-1], "dom", along(1, 0)))
    buffers = list(ring)
    for _ in range(y_size - 1):
        ring = [lax.ppermute(part, "dom", along(0, 1)) for part in ring]
        buffers += ring

    weights, stats = score(arrived, refs, tables, classes)
    weights = lax.all_to_all(
        jnp.broadcast_to(weights[None], (doms, *weights.shape)), "dom", split_axis=0, concat_axis=0, tiled=True
    )
    stats = lax.all_to_all(
        jnp.broadcast_to(stats[None], (groups * doms, *stats.shape)),
        ("cls", "dom"),
        split_axis=0,
        concat_axis=0,
        tiled=True,
    )
    stats = stats.reshape(groups, doms, *stats.shape[1:])
    dom = lax.axis_index("dom")
    place = jnp.stack([lax.axis_index("cls"), dom // y_size, dom % y_size]).astype(jnp.int32)
    return class_sum(buffers, weights, stats, tables, place, z_size, y_size, local, block_width, classes)


def solution(mesh):
    coords = [device.coords for device in mesh.devices.flat]
    z_size = len({c[2] for c in coords})
    y_size = len({c[1] for c in coords})
    in_specs = (
        P(("cls", "dom"), None),
        P("cls", None),
        P(("cls", "dom"), None),
        P(("cls", "dom"), None),
    )
    out_specs = P("cls", None)
    return jax.shard_map(
        functools.partial(shards, z_size, y_size),
        mesh=mesh,
        in_specs=in_specs,
        out_specs=out_specs,
        check_vma=False,
    )
```

```python
import functools
import math

import jax
import jax.numpy as jnp
import numpy as np
from jax import lax
from jax.experimental import pallas as pl
from jax.experimental.pallas import tpu as pltpu
from jax.sharding import PartitionSpec as P

CYCLES = 128
ANGLES = 144
ROT = 36
SHIFTS = 5
BOX = 256
LANES = 128
SPAN = 40
STEP_ANGLES = ANGLES // ROT
PIECES = 2 * STEP_ANGLES
IMAGE_ROWS = PIECES * SPAN
REACH = 7

SOFTMAX_WARMTH = 2.0
PRIOR_MASS = 1.0
NEGATIVE = -1e30
META_ROWS = 16
VMEM_LIMIT = 60 * 1024 * 1024
DOM, OWNER, SLOT, CLASS = 0, 1, 3, 5
FILLED, OTHER, OTHER_SLOT = 0, 1, 2


def trig_tables():
    theta = 2.0 * np.pi * np.arange(ANGLES) / ANGLES
    radius = np.arange(1, CYCLES + 1)
    out = np.zeros((4, REACH + 1, STEP_ANGLES, SPAN, CYCLES), np.float32)
    for axis, direction in enumerate((np.cos(theta), np.sin(theta))):
        for t in range(REACH + 1):
            phase = 2.0 * np.pi / BOX * t * direction[:, None] * radius[None, :]
            for part, fn in enumerate((np.cos, np.sin)):
                table = fn(phase).reshape(ROT, STEP_ANGLES, CYCLES).transpose(1, 0, 2)
                out[2 * axis + part, t, :, :ROT] = table[:, ::-1]
    return out.reshape(4, REACH + 1, STEP_ANGLES * SPAN, CYCLES)


def axis_phase(table_ref, axis, step, move):
    size = jnp.abs(move)
    sign = jnp.where(move < 0, -1.0, 1.0).astype(jnp.float32)
    at = pl.ds(step * SPAN, SPAN)
    return table_ref[2 * axis, size, at, :], table_ref[2 * axis + 1, size, at, :] * sign


def prep_kernel(local, place_ref, near_ref, far_ref, image_near, image_far, table_ref, mine_ref, rest_ref, raw):
    count = near_ref.shape[0]
    listed = near_ref.shape[1] - 2
    rows = image_near.shape[1]
    half = listed // 2
    share = count // 2
    my_cls, my_dom = place_ref[0], place_ref[1]
    core = lax.rem(my_cls, 2)
    raw[...] = jnp.zeros_like(raw)
    lane = lax.broadcasted_iota(jnp.int32, (META_ROWS, LANES), 1)
    for far in range(2):
        record, image_ref = (far_ref, image_far) if far else (near_ref, image_near)
        source_core = 1 - core if far else core
        source = my_cls - core + source_core
        cand = [[record[u, k] for k in range(listed)] for u in range(count)]
        owner = [[lax.div(c, local) for c in row] for row in cand]
        pair = []
        for u in range(count):
            first = owner[u][0]
            second = first
            for k in range(1, listed):
                second = jnp.where(owner[u][k] != first, owner[u][k], second)
            pair.append((first, second))
        for u in range(count):
            entries = [my_dom, pair[u][0], pair[u][1]]
            for side in range(2):
                value = source * (count // 2)
                for v in range(u):
                    lists = (pair[v][0] == pair[u][side]) | (pair[v][1] == pair[u][side])
                    value = value + jnp.where(lists, 1, 0)
                entries.append(value)
            for side in range(2):
                classes = [jnp.int32(0)] * half
                seen = jnp.int32(0)
                for k in range(listed):
                    hit = owner[u][k] == pair[u][side]
                    for j in range(half):
                        classes[j] = jnp.where(hit & (seen == j), cand[u][k] - pair[u][side] * local, classes[j])
                    seen = seen + jnp.where(hit, 1, 0)
                entries += classes
            tile = jnp.zeros((META_ROWS, LANES), jnp.int32)
            for k, value in enumerate(entries):
                tile = jnp.where(lane == k, value, tile)
            values = image_ref[u].astype(jnp.float32)
            for block in range(rows // PIECES):
                at = rows - (block + 1) * PIECES
                raw[at : at + PIECES, :] = values[block * PIECES : (block + 1) * PIECES]
            moved = []
            for step in range(STEP_ANGLES):
                re = raw[pl.ds(2 * step, SPAN, stride=PIECES), :]
                im = raw[pl.ds(2 * step + 1, SPAN, stride=PIECES), :]
                cx, sx = axis_phase(table_ref, 0, step, record[u, listed])
                cy, sy = axis_phase(table_ref, 1, step, record[u, listed + 1])
                cosine = cx * cy - sx * sy
                sine = sx * cy + cx * sy
                moved += [re * cosine + im * sine, im * cosine - re * sine]
            moved = jnp.concatenate(moved, axis=0).astype(mine_ref.dtype)
            tile = tile.astype(jnp.float32).astype(mine_ref.dtype)
            at = source_core * share + u % share
            role = u // share

            @pl.when(core == role)
            def _():
                mine_ref[at, :IMAGE_ROWS, :] = moved
                mine_ref[at, IMAGE_ROWS:, :] = tile

            @pl.when(core != role)
            def _():
                rest_ref[at, :IMAGE_ROWS, :] = moved
                rest_ref[at, IMAGE_ROWS:, :] = tile


SMEM_SPEC = pl.BlockSpec(memory_space=pltpu.SMEM)
VMEM_SPEC = pl.BlockSpec(memory_space=pltpu.VMEM)
HBM_SPEC = pl.BlockSpec(memory_space=pl.ANY)


def prepare(place, near, far, image_near, image_far, tables, local):
    count = near.shape[0]
    shape = jax.ShapeDtypeStruct((count, IMAGE_ROWS + META_ROWS, LANES), image_near.dtype)
    return pl.pallas_call(
        functools.partial(prep_kernel, local),
        out_shape=(shape, shape),
        in_specs=[SMEM_SPEC] * 3 + [VMEM_SPEC] * 3,
        out_specs=(VMEM_SPEC, VMEM_SPEC),
        scratch_shapes=[pltpu.VMEM((IMAGE_ROWS, LANES), jnp.float32)],
        compiler_params=pltpu.CompilerParams(vmem_limit_bytes=VMEM_LIMIT),
        name="prepare",
    )(place, near, far, image_near, image_far, tables)


def read_meta(source, meta_vmem, row):
    meta_vmem[pl.ds(row, 1), :] = source.astype(jnp.float32)[0:1, :].astype(jnp.int32)


def move_metas(meta_vmem, meta, sem):
    copy = pltpu.make_async_copy(meta_vmem, meta, sem)
    copy.start()
    copy.wait()


def side_of(meta, i, my_cls):
    return jnp.where(meta[i, OWNER] == my_cls, 0, 1)


def collect(meta, active, total, my_cls):
    def look(i, n):
        mine = (meta[i, OWNER] == my_cls) | (meta[i, OWNER + 1] == my_cls)
        active[n] = i
        return n + jnp.where(mine, 1, 0)

    return lax.fori_loop(0, total, look, jnp.int32(0))


def step_pieces(values, table_ref, step):
    re = values[2 * step * SPAN : (2 * step + 1) * SPAN]
    im = values[(2 * step + 1) * SPAN : (2 * step + 2) * SPAN]
    at = pl.ds(step * SPAN, SPAN)
    return re, im, [table_ref[k, 1, at, :] for k in range(4)]


def store_moved(moved, step, part, blocks):
    at = pl.ds((2 * step + part) * LANES, LANES)
    pad = jnp.zeros((8, LANES), jnp.float32)
    moved[:LANES, at] = jnp.concatenate([*blocks[:3], pad], axis=0).astype(jnp.bfloat16)
    moved[LANES : LANES + 2 * SPAN, at] = jnp.concatenate(blocks[3:], axis=0).astype(jnp.bfloat16)


def score_kernel(count, place_ref, *refs):
    image_refs = refs[:count]
    (
        refs_ref, table_ref, weight_ref, stat_ref, partner_ref,
        moved, picked, sums, meta_vmem, meta, sem,
    ) = refs[count:]
    block = image_refs[0].shape[0]
    slots = weight_ref.shape[0]
    classes = picked.shape[0] // 48
    my_cls, my_dom = place_ref[0], place_ref[1]
    moved[...] = jnp.zeros_like(moved)
    picked[...] = jnp.zeros_like(picked)
    weight_ref[...] = jnp.zeros_like(weight_ref)
    stat_ref[...] = jnp.zeros_like(stat_ref)
    sums[...] = jnp.zeros_like(sums)
    for b in range(count):
        for i in range(block):
            read_meta(image_refs[b][i, IMAGE_ROWS:, :], meta_vmem, b * block + i)
    move_metas(meta_vmem, meta, sem)
    for slot in range(slots):
        for k in range(3):
            partner_ref[slot, k] = 0
    lane = lax.broadcasted_iota(jnp.int32, (SPAN, LANES), 1)

    def one(b, i):
        side = side_of(meta, b * block + i, my_cls)
        index = b * block + i
        slot = meta[index, SLOT + side]
        partner_ref[slot, FILLED] = 1
        partner_ref[slot, OTHER] = meta[index, OWNER + 1 - side]
        partner_ref[slot, OTHER_SLOT] = meta[index, SLOT + 1 - side]
        for j in range(classes):
            picked[j * 48 : j * 48 + ROT, :] = refs_ref[meta[index, CLASS + side * classes + j]]
        values = image_refs[b][i, :IMAGE_ROWS, :].astype(jnp.float32)
        for step in range(STEP_ANGLES):
            re, im, (c1, s1, c2, s2) = step_pieces(values, table_ref, step)
            a1, b1, d1, e1 = re * c1, im * s1, im * c1, re * s1
            a2, b2, d2, e2 = re * c2, im * s2, im * c2, re * s2
            store_moved(moved, step, 0, [re, a1 + b1, a1 - b1, a2 + b2, a2 - b2])
            store_moved(moved, step, 1, [im, d1 - e1, d1 + e1, d2 - e2, d2 + e2])
        pairs = lax.dot_general(
            picked[...], moved[...], (((1,), (1,)), ((), ())), preferred_element_type=jnp.float32
        )
        for s in range(SHIFTS):
            half, k = divmod(s, 3)
            for j in range(classes):
                part = pairs[j * 48 : j * 48 + SPAN, half * LANES : (half + 1) * LANES]
                part = jnp.where((lane >= k * SPAN) & (lane < (k + 1) * SPAN), part, 0.0)
                turned = pltpu.roll(part, 0, 1, stride=1, stride_axis=0)
                sums[k, pl.ds(half * classes + j, 1), :] = jnp.sum(turned, axis=0, keepdims=True)
        found = []
        for k in range(3):
            plain = pltpu.roll(sums[k], (LANES - k * SPAN) % LANES, 1) if k else sums[k]
            found.append(SOFTMAX_WARMTH * (plain + pltpu.roll(plain, LANES - ROT, 1)))
        lanes = lax.broadcasted_iota(jnp.int32, found[0].shape, 1)
        lines = lax.broadcasted_iota(jnp.int32, found[0].shape, 0)
        valid = [lanes < ROT, lanes < ROT, (lanes < ROT) & (lines < classes)]
        found = [jnp.where(v, f, NEGATIVE) for v, f in zip(valid, found)]
        peak = jnp.maximum(jnp.maximum(found[0], found[1]), found[2])
        peak = jnp.max(jnp.max(peak, axis=0, keepdims=True), axis=1, keepdims=True)
        w = [jnp.where(v, jnp.exp(f - peak), 0.0) for v, f in zip(valid, found)]
        total = w[0] + w[1] + w[2]
        total = jnp.sum(jnp.sum(total, axis=0, keepdims=True), axis=1, keepdims=True)
        stat_ref[pl.ds(2 * slot, 1), :] = jnp.broadcast_to(peak, (1, LANES))
        stat_ref[pl.ds(2 * slot + 1, 1), :] = jnp.broadcast_to(total, (1, LANES))
        upper = lines < classes
        first = jnp.where(upper, w[0], w[0] + w[1])
        second = jnp.where(upper, w[1] + w[2], w[0] - w[1])
        third = w[1] - w[2]
        third = jnp.where(upper, third, 0.0)
        weight_ref[slot] = first + pltpu.roll(second, SPAN, 1) + pltpu.roll(third, 2 * SPAN, 1)

    for b in range(count):

        def body(i, carry, b=b):
            @pl.when(
                (meta[b * block + i, DOM] == my_dom)
                & ((meta[b * block + i, OWNER] == my_cls) | (meta[b * block + i, OWNER + 1] == my_cls))
            )
            def _():
                one(b, i)

            return carry

        lax.fori_loop(0, block, body, 0)


def score(place, buffers, refs, tables, slots, classes):
    count, block = len(buffers), buffers[0].shape[0]
    width = refs.shape[2]
    return pl.pallas_call(
        functools.partial(score_kernel, count),
        out_shape=(
            jax.ShapeDtypeStruct((slots, 2 * classes, LANES), jnp.float32),
            jax.ShapeDtypeStruct((2 * slots, LANES), jnp.float32),
            jax.ShapeDtypeStruct((slots, 3), jnp.int32),
        ),
        in_specs=[SMEM_SPEC] + [VMEM_SPEC] * (count + 2),
        out_specs=(VMEM_SPEC, VMEM_SPEC, SMEM_SPEC),
        scratch_shapes=[
            pltpu.VMEM((2 * LANES, width), jnp.bfloat16),
            pltpu.VMEM((48 * classes, width), jnp.bfloat16),
            pltpu.VMEM((3, 2 * classes, LANES), jnp.float32),
            pltpu.VMEM((count * block, LANES), jnp.int32),
            pltpu.SMEM((count * block, LANES), jnp.int32),
            pltpu.SemaphoreType.DMA,
        ],
        compiler_params=pltpu.CompilerParams(vmem_limit_bytes=VMEM_LIMIT),
        cost_estimate=pl.CostEstimate(flops=10**10, bytes_accessed=10**7, transcendentals=0),
        name="score",
    )(place, *buffers, refs, tables)


def weight_kernel(flip, place_ref, partner_ref, weight_ref, *refs):
    stat_refs, out_ref = refs[:-1], refs[-1]
    slots, lines, _ = weight_ref.shape
    my_cls = place_ref[0]
    done = []
    for slot in range(slots):
        other, other_slot = partner_ref[slot, OTHER], partner_ref[slot, OTHER_SLOT]
        at = pl.ds(2 * other_slot, 2)
        if flip:
            mine = stat_refs[0][2 * slot : 2 * slot + 2, :]
            theirs = mine
            for k in range(1, len(stat_refs)):
                theirs = jnp.where(jnp.bitwise_xor(other, my_cls) == k, stat_refs[k][at, :], theirs)
        else:
            mine = stat_refs[0][my_cls, 2 * slot : 2 * slot + 2, :]
            theirs = stat_refs[0][other, at, :]
        peak = jnp.maximum(mine[0:1], theirs[0:1])
        gain = jnp.exp(mine[0:1] - peak)
        mass = mine[1:2] * gain + theirs[1:2] * jnp.exp(theirs[0:1] - peak)
        factor = gain / jnp.where(partner_ref[slot, FILLED] > 0, mass, 1.0)
        done.append(weight_ref[slot] * factor)
    out_ref[...] = jnp.concatenate(done, axis=0).astype(out_ref.dtype)


def normalise(flip, place, partners, weights, stats):
    slots, lines, _ = weights.shape
    return pl.pallas_call(
        functools.partial(weight_kernel, flip),
        out_shape=jax.ShapeDtypeStruct((slots * lines, LANES), jnp.bfloat16),
        in_specs=[SMEM_SPEC] * 2 + [VMEM_SPEC] * (1 + len(stats)),
        out_specs=VMEM_SPEC,
        name="normalise",
    )(place, partners, weights, *stats)


def sum_kernel(relative, z_size, y_size, lines, count, n_weights, place_ref, *refs):
    image_refs = refs[:count]
    weight_refs = refs[count : count + n_weights]
    (
        table_ref, out_ref, images, weights, moved, totals, mass, meta_vmem, meta, active, image_sem, meta_sem,
    ) = refs[count + n_weights :]
    local = out_ref.shape[0]
    width = moved.shape[2]
    depth, wave = images.shape[0], images.shape[1]
    size = image_refs[0].shape[0]
    per_row = weight_refs[0].shape[0]
    classes = lines // 2
    waves = count * size // wave

    def copies(w):
        if size <= wave:
            each = wave // size
            return [
                pltpu.make_async_copy(
                    image_refs[w * each + b], images.at[w % depth, pl.ds(b * size, size)], image_sem.at[w % depth, b]
                )
                for b in range(each)
            ]
        return [
            pltpu.make_async_copy(
                image_refs[0].at[pl.ds(w * wave, wave)], images.at[w % depth], image_sem.at[w % depth, 0]
            )
        ]

    for w in range(min(depth, waves)):
        for copy in copies(w):
            copy.start()
    moved[...] = jnp.zeros_like(moved)
    mass[...] = jnp.zeros_like(mass)
    totals[...] = jnp.zeros_like(totals)
    for b in range(n_weights):
        weights[b * per_row : (b + 1) * per_row, :] = weight_refs[b][...].astype(jnp.float32)
    my_cls, my_dom = place_ref[0], place_ref[1]
    my_z, my_y = lax.div(my_dom, y_size), lax.rem(my_dom, y_size)
    lane = lax.broadcasted_iota(jnp.int32, (lines, LANES), 1)
    lane_wide = lax.broadcasted_iota(jnp.int32, (SPAN, LANES), 1)

    for w in range(waves):
        for copy in copies(w):
            copy.wait()
        here = images.at[w % depth]
        for i in range(wave):
            read_meta(here[i, IMAGE_ROWS:, :], meta_vmem, i)
        move_metas(meta_vmem, meta, meta_sem)
        number = collect(meta, active, wave, my_cls)

        def prepare_one(i, share, buffer):
            side = side_of(meta, i, my_cls)
            q = meta[i, DOM]
            if relative:
                d_z = lax.rem(my_z - lax.div(q, y_size) + z_size, z_size)
                d_y = lax.rem(my_y - lax.rem(q, y_size) + y_size, y_size)
                q = d_y * z_size + d_z
            at = pl.multiple_of(q * per_row + meta[i, SLOT + side] * lines, lines)
            mine = weights[pl.ds(at, lines), :] * share
            values = here[i, :IMAGE_ROWS, :].astype(jnp.float32)
            for step in range(STEP_ANGLES):
                re, im, (c1, s1, c2, s2) = step_pieces(values, table_ref, step)
                store_moved(moved.at[buffer], step, 0, [re, re * c1, im * s1, re * c2, im * s2])
                store_moved(moved.at[buffer], step, 1, [im, im * c1, -re * s1, im * c2, -re * s2])
            parts = []
            for k in range(3):
                part = jnp.where((lane >= k * SPAN) & (lane < (k + 1) * SPAN), mine, 0.0)
                parts.append(part + pltpu.roll(part, LANES - ROT, 1))
            blocks = []
            for j in range(classes):
                line = []
                for half in range(2):
                    at = half * classes + j
                    turned = [
                        pltpu.roll(
                            jnp.broadcast_to(parts[k][at : at + 1], (SPAN, LANES)), 1, 1, stride=1, stride_axis=0
                        )
                        for k in range(3 - half)
                    ]
                    tile = jnp.where(lane_wide < SPAN, turned[0], turned[1])
                    if half == 0:
                        tile = jnp.where(lane_wide < 2 * SPAN, tile, turned[2])
                    line.append(tile)
                blocks.append(jnp.concatenate(line, axis=1))
            spread = jnp.concatenate(blocks, axis=0).astype(jnp.bfloat16)
            plain = jnp.where(lane < 2 * SPAN, mine, 0.0)
            plain_high = jnp.where(lane < SPAN, mine, 0.0)
            masses = [plain[j : j + 1] + plain_high[classes + j : classes + j + 1] for j in range(classes)]
            chosen = [meta[i, CLASS + side * classes + j] for j in range(classes)]
            return spread, masses, chosen

        def add_one(added, masses, chosen):
            for j in range(classes):
                c = chosen[j]
                for tile in range(width // LANES):
                    at = pl.ds(pl.multiple_of(tile * local * SPAN + c * SPAN, 8), SPAN)
                    totals[at, :] += added[j * SPAN : (j + 1) * SPAN, tile * LANES : (tile + 1) * LANES]
                mass[pl.ds(c, 1), :] += masses[j]

        def two(step, carry):
            first = active[2 * step]
            second_at = 2 * step + 1
            second = active[jnp.minimum(second_at, number - 1)]
            share = jnp.where(second_at < number, 1.0, 0.0).astype(jnp.float32)
            one_spread, one_mass, one_chosen = prepare_one(first, 1.0, 0)
            two_spread, two_mass, two_chosen = prepare_one(second, share, 1)
            one_added = jnp.dot(one_spread, moved[0], preferred_element_type=jnp.float32)
            two_added = jnp.dot(two_spread, moved[1], preferred_element_type=jnp.float32)
            add_one(one_added, one_mass, one_chosen)
            add_one(two_added, two_mass, two_chosen)
            return carry

        lax.fori_loop(0, lax.div(number + 1, 2), two, 0)
        if w + depth < waves:
            for copy in copies(w + depth):
                copy.start()

    scale = 1.0 / (jnp.sum(mass[:local, :], axis=1, keepdims=True) + PRIOR_MASS)
    for turn in range(ROT):
        for tile in range(width // LANES):
            line = totals[pl.ds(tile * local * SPAN + ROT - 1 - turn, local, stride=SPAN), :]
            out_ref[:, pl.ds(turn * width + tile * LANES, LANES)] = (line * scale).astype(out_ref.dtype)


def class_sum(place, buffers, weights, tables, relative, z_size, y_size, local, width, lines):
    count, size = len(buffers), buffers[0].shape[0]
    total = count * size
    wave = math.gcd(total, 128)
    depth = min(2, total // wave)
    return pl.pallas_call(
        functools.partial(sum_kernel, relative, z_size, y_size, lines, count, len(weights)),
        out_shape=jax.ShapeDtypeStruct((local, ROT * width), jnp.bfloat16),
        in_specs=[SMEM_SPEC] + [HBM_SPEC] * count + [VMEM_SPEC] * (len(weights) + 1),
        out_specs=VMEM_SPEC,
        scratch_shapes=[
            pltpu.VMEM((depth, wave, IMAGE_ROWS + META_ROWS, LANES), jnp.bfloat16),
            pltpu.VMEM((len(weights) * weights[0].shape[0], LANES), jnp.float32),
            pltpu.VMEM((2, 2 * LANES, width), jnp.bfloat16),
            pltpu.VMEM((width // LANES * local * SPAN, LANES), jnp.float32),
            pltpu.VMEM((-(-local // 8) * 8, LANES), jnp.float32),
            pltpu.VMEM((wave, LANES), jnp.int32),
            pltpu.SMEM((wave, LANES), jnp.int32),
            pltpu.SMEM((wave + 1,), jnp.int32),
            pltpu.SemaphoreType.DMA((depth, max(1, wave // size))),
            pltpu.SemaphoreType.DMA,
        ],
        compiler_params=pltpu.CompilerParams(vmem_limit_bytes=VMEM_LIMIT),
        cost_estimate=pl.CostEstimate(flops=2 * 10**10, bytes_accessed=10**7, transcendentals=0),
        name="class_sum",
    )(place, *buffers, *weights, tables)


def shards(x_size, y_size, z_size, particles, references, candidates, offsets):
    groups = lax.axis_size("cls")
    doms = lax.axis_size("dom")
    count, width = particles.shape
    local = references.shape[0]
    classes = candidates.shape[1] // 2
    block_width = width // ROT
    slots = groups * (count // 2)
    tables = jnp.asarray(trig_tables())
    place = jnp.stack([lax.axis_index("cls"), lax.axis_index("dom")]).astype(jnp.int32)

    def moves(goal):
        out = []
        for cls in range(groups):
            for dom in range(doms):
                x, core, z, y = goal(cls // 2, cls % 2, dom // y_size, dom % y_size)
                to = ((x % x_size) * 2 + core) * doms + (z % z_size) * y_size + y % y_size
                out.append((cls * doms + dom, to))
        return out

    def send(value, goal):
        return lax.ppermute(value, ("cls", "dom"), moves(goal))

    swap = functools.partial(send, goal=lambda x, c, z, y: (x, 1 - c, z, y))
    along_z = functools.partial(send, goal=lambda x, c, z, y: (x, c, z + 1, y))
    early = functools.partial(send, goal=lambda x, c, z, y: (x + 1 - c, c, z, y + c))
    late = functools.partial(send, goal=lambda x, c, z, y: (x + c, c, z, y + 1 - c))

    images = particles.reshape(count, width // LANES, LANES)
    record = jnp.concatenate([candidates, offsets], axis=1)
    mine, rest = prepare(place, record, swap(record), images, swap(images), tables, local)
    refs = references.reshape(local, ROT, block_width)
    tuned = x_size == 2 and y_size == 2
    if tuned:
        first_early, first_late = early(mine), late(mine)
        row = [mine, rest, first_early, first_late, swap(first_early), swap(first_late)]
        ring = [mine]
        for _ in range(z_size - 1):
            ring.append(along_z(ring[-1]))
        second = [first_early] + [early(part) for part in ring[1:]]
        third = [first_late] + [late(part) for part in ring[1:] + second]
        received = ring[1:] + second[1:] + third[1:]
        buffers = row + received + [swap(part) for part in received]
    else:
        row = [lax.all_gather(mine, "cls", axis=0, tiled=True)]
        buffers = [lax.all_gather(row[0], "dom", axis=0, tiled=True)]

    weights, stats, partners = score(place, row, refs, tables, slots, classes)
    if tuned:
        stats = [
            stats,
            swap(stats),
            send(stats, lambda x, c, z, y: (x + 1, c, z, y)),
            send(stats, lambda x, c, z, y: (x + 1, 1 - c, z, y)),
        ]
    else:
        stats = [lax.all_gather(stats, "cls", axis=0, tiled=False)]
    weights = normalise(tuned, place, partners, weights, stats)
    if tuned:
        weights = [
            weights if dz == dy == 0 else send(weights, lambda x, c, z, y, dz=dz, dy=dy: (x, c, z + dz, y + dy))
            for dy in range(y_size)
            for dz in range(z_size)
        ]
    else:
        weights = [lax.all_gather(weights, "dom", axis=0, tiled=True)]
    return class_sum(
        place, buffers, weights, tables, tuned, z_size, y_size, local, block_width, 2 * classes
    )


def solution(mesh):
    coords = [device.coords for device in mesh.devices.flat]
    sizes = [len({c[axis] for c in coords}) for axis in range(3)]
    in_specs = (
        P(("cls", "dom"), None),
        P("cls", None),
        P(("cls", "dom"), None),
        P(("cls", "dom"), None),
    )
    out_specs = P("cls", None)
    return jax.shard_map(
        functools.partial(shards, *sizes),
        mesh=mesh,
        in_specs=in_specs,
        out_specs=out_specs,
        check_vma=False,
    )
```

```python
import functools
import math

import jax
import jax.numpy as jnp
import numpy as np
from jax import lax
from jax.experimental import pallas as pl
from jax.experimental.pallas import tpu as pltpu
from jax.sharding import PartitionSpec as P

CYCLES = 128
ANGLES = 144
ROT = 36
SHIFTS = 5
BOX = 256
LANES = 128
SPAN = 40
STEP_ANGLES = ANGLES // ROT
PIECES = 2 * STEP_ANGLES
IMAGE_ROWS = PIECES * SPAN
REACH = 7

SOFTMAX_WARMTH = 2.0
PRIOR_MASS = 1.0
NEGATIVE = -1e30
META_ROWS = 16
VMEM_LIMIT = 60 * 1024 * 1024
DOM, OWNER, SLOT, CLASS = 0, 1, 3, 5
FILLED, OTHER, OTHER_SLOT = 0, 1, 2


def trig_tables():
    theta = 2.0 * np.pi * np.arange(ANGLES) / ANGLES
    radius = np.arange(1, CYCLES + 1)
    out = np.zeros((4, REACH + 1, STEP_ANGLES, SPAN, CYCLES), np.float32)
    for axis, direction in enumerate((np.cos(theta), np.sin(theta))):
        for t in range(REACH + 1):
            phase = 2.0 * np.pi / BOX * t * direction[:, None] * radius[None, :]
            for part, fn in enumerate((np.cos, np.sin)):
                table = fn(phase).reshape(ROT, STEP_ANGLES, CYCLES).transpose(1, 0, 2)
                out[2 * axis + part, t, :, :ROT] = table[:, ::-1]
    return out.reshape(4, REACH + 1, STEP_ANGLES * SPAN, CYCLES)


def axis_phase(table_ref, axis, step, move):
    size = jnp.abs(move)
    sign = jnp.where(move < 0, -1.0, 1.0).astype(jnp.float32)
    at = pl.ds(step * SPAN, SPAN)
    return table_ref[2 * axis, size, at, :], table_ref[2 * axis + 1, size, at, :] * sign


def prep_kernel(local, place_ref, near_ref, far_ref, image_near, image_far, table_ref, mine_ref, rest_ref, raw):
    count = near_ref.shape[0]
    listed = near_ref.shape[1] - 2
    rows = image_near.shape[1]
    half = listed // 2
    share = count // 2
    my_cls, my_dom = place_ref[0], place_ref[1]
    core = lax.rem(my_cls, 2)
    raw[...] = jnp.zeros_like(raw)
    lane = lax.broadcasted_iota(jnp.int32, (META_ROWS, LANES), 1)
    for far in range(2):
        record, image_ref = (far_ref, image_far) if far else (near_ref, image_near)
        source_core = 1 - core if far else core
        source = my_cls - core + source_core
        cand = [[record[u, k] for k in range(listed)] for u in range(count)]
        owner = [[lax.div(c, local) for c in row] for row in cand]
        pair = []
        for u in range(count):
            first = owner[u][0]
            second = first
            for k in range(1, listed):
                second = jnp.where(owner[u][k] != first, owner[u][k], second)
            pair.append((first, second))
        for u in range(count):
            entries = [my_dom, pair[u][0], pair[u][1]]
            for side in range(2):
                value = source * (count // 2)
                for v in range(u):
                    lists = (pair[v][0] == pair[u][side]) | (pair[v][1] == pair[u][side])
                    value = value + jnp.where(lists, 1, 0)
                entries.append(value)
            for side in range(2):
                classes = [jnp.int32(0)] * half
                seen = jnp.int32(0)
                for k in range(listed):
                    hit = owner[u][k] == pair[u][side]
                    for j in range(half):
                        classes[j] = jnp.where(hit & (seen == j), cand[u][k] - pair[u][side] * local, classes[j])
                    seen = seen + jnp.where(hit, 1, 0)
                entries += classes
            tile = jnp.zeros((META_ROWS, LANES), jnp.int32)
            for k, value in enumerate(entries):
                tile = jnp.where(lane == k, value, tile)
            values = image_ref[u].astype(jnp.float32)
            for block in range(rows // PIECES):
                at = rows - (block + 1) * PIECES
                raw[at : at + PIECES, :] = values[block * PIECES : (block + 1) * PIECES]
            moved = []
            for step in range(STEP_ANGLES):
                re = raw[pl.ds(2 * step, SPAN, stride=PIECES), :]
                im = raw[pl.ds(2 * step + 1, SPAN, stride=PIECES), :]
                cx, sx = axis_phase(table_ref, 0, step, record[u, listed])
                cy, sy = axis_phase(table_ref, 1, step, record[u, listed + 1])
                cosine = cx * cy - sx * sy
                sine = sx * cy + cx * sy
                moved += [re * cosine + im * sine, im * cosine - re * sine]
            moved = jnp.concatenate(moved, axis=0).astype(mine_ref.dtype)
            tile = tile.astype(jnp.float32).astype(mine_ref.dtype)
            at = source_core * share + u % share
            role = u // share

            @pl.when(core == role)
            def _():
                mine_ref[at, :IMAGE_ROWS, :] = moved
                mine_ref[at, IMAGE_ROWS:, :] = tile

            @pl.when(core != role)
            def _():
                rest_ref[at, :IMAGE_ROWS, :] = moved
                rest_ref[at, IMAGE_ROWS:, :] = tile


SMEM_SPEC = pl.BlockSpec(memory_space=pltpu.SMEM)
VMEM_SPEC = pl.BlockSpec(memory_space=pltpu.VMEM)
HBM_SPEC = pl.BlockSpec(memory_space=pl.ANY)


def prepare(place, near, far, image_near, image_far, tables, local):
    count = near.shape[0]
    shape = jax.ShapeDtypeStruct((count, IMAGE_ROWS + META_ROWS, LANES), image_near.dtype)
    return pl.pallas_call(
        functools.partial(prep_kernel, local),
        out_shape=(shape, shape),
        in_specs=[SMEM_SPEC] * 3 + [VMEM_SPEC] * 3,
        out_specs=(VMEM_SPEC, VMEM_SPEC),
        scratch_shapes=[pltpu.VMEM((IMAGE_ROWS, LANES), jnp.float32)],
        compiler_params=pltpu.CompilerParams(vmem_limit_bytes=VMEM_LIMIT),
        name="prepare",
    )(place, near, far, image_near, image_far, tables)


def read_meta(source, meta_vmem, row):
    meta_vmem[pl.ds(row, 1), :] = source.astype(jnp.float32)[0:1, :].astype(jnp.int32)


def move_metas(meta_vmem, meta, sem):
    copy = pltpu.make_async_copy(meta_vmem, meta, sem)
    copy.start()
    copy.wait()


def side_of(meta, i, my_cls):
    return jnp.where(meta[i, OWNER] == my_cls, 0, 1)


def collect(meta, active, total, my_cls):
    def look(i, n):
        mine = (meta[i, OWNER] == my_cls) | (meta[i, OWNER + 1] == my_cls)
        active[n] = i
        return n + jnp.where(mine, 1, 0)

    return lax.fori_loop(0, total, look, jnp.int32(0))


def step_pieces(values, table_ref, step):
    re = values[2 * step * SPAN : (2 * step + 1) * SPAN]
    im = values[(2 * step + 1) * SPAN : (2 * step + 2) * SPAN]
    at = pl.ds(step * SPAN, SPAN)
    return re, im, [table_ref[k, at, :] for k in range(4)]


def store_moved(moved, step, part, blocks):
    at = pl.ds((2 * step + part) * LANES, LANES)
    pad = jnp.zeros((8, LANES), jnp.float32)
    moved[:LANES, at] = jnp.concatenate([*blocks[:3], pad], axis=0).astype(jnp.bfloat16)
    moved[LANES : LANES + 2 * SPAN, at] = jnp.concatenate(blocks[3:], axis=0).astype(jnp.bfloat16)


def score_kernel(count, waits, place_ref, *refs):
    image_refs = refs[:count]
    (
        refs_ref, table_ref, weight_ref, stat_ref, partner_ref,
        moved, picked, sums, meta_vmem, meta, sem,
    ) = refs[count + waits :]
    block = image_refs[0].shape[0]
    slots = weight_ref.shape[0]
    classes = picked.shape[0] // 48
    my_cls, my_dom = place_ref[0], place_ref[1]
    moved[...] = jnp.zeros_like(moved)
    picked[...] = jnp.zeros_like(picked)
    weight_ref[...] = jnp.zeros_like(weight_ref)
    stat_ref[...] = jnp.zeros_like(stat_ref)
    sums[...] = jnp.zeros_like(sums)
    for b in range(count):
        for i in range(block):
            read_meta(image_refs[b][i, IMAGE_ROWS:, :], meta_vmem, b * block + i)
    move_metas(meta_vmem, meta, sem)
    for slot in range(slots):
        for k in range(3):
            partner_ref[slot, k] = 0
    lane = lax.broadcasted_iota(jnp.int32, (SPAN, LANES), 1)

    def one(b, i):
        side = side_of(meta, b * block + i, my_cls)
        index = b * block + i
        slot = meta[index, SLOT + side]
        partner_ref[slot, FILLED] = 1
        partner_ref[slot, OTHER] = meta[index, OWNER + 1 - side]
        partner_ref[slot, OTHER_SLOT] = meta[index, SLOT + 1 - side]
        for j in range(classes):
            picked[j * 48 : j * 48 + ROT, :] = refs_ref[meta[index, CLASS + side * classes + j]]
        values = image_refs[b][i, :IMAGE_ROWS, :].astype(jnp.float32)
        for step in range(STEP_ANGLES):
            re, im, (c1, s1, c2, s2) = step_pieces(values, table_ref, step)
            a1, b1, d1, e1 = re * c1, im * s1, im * c1, re * s1
            a2, b2, d2, e2 = re * c2, im * s2, im * c2, re * s2
            store_moved(moved, step, 0, [re, a1 + b1, a1 - b1, a2 + b2, a2 - b2])
            store_moved(moved, step, 1, [im, d1 - e1, d1 + e1, d2 - e2, d2 + e2])
        pairs = lax.dot_general(
            picked[...], moved[...], (((1,), (1,)), ((), ())), preferred_element_type=jnp.float32
        )
        for s in range(SHIFTS):
            half, k = divmod(s, 3)
            for j in range(classes):
                part = pairs[j * 48 : j * 48 + SPAN, half * LANES : (half + 1) * LANES]
                part = jnp.where((lane >= k * SPAN) & (lane < (k + 1) * SPAN), part, 0.0)
                turned = pltpu.roll(part, 0, 1, stride=1, stride_axis=0)
                sums[k, pl.ds(half * classes + j, 1), :] = jnp.sum(turned, axis=0, keepdims=True)
        found = []
        for k in range(3):
            plain = pltpu.roll(sums[k], (LANES - k * SPAN) % LANES, 1) if k else sums[k]
            found.append(SOFTMAX_WARMTH * (plain + pltpu.roll(plain, LANES - ROT, 1)))
        lanes = lax.broadcasted_iota(jnp.int32, found[0].shape, 1)
        lines = lax.broadcasted_iota(jnp.int32, found[0].shape, 0)
        valid = [lanes < ROT, lanes < ROT, (lanes < ROT) & (lines < classes)]
        found = [jnp.where(v, f, NEGATIVE) for v, f in zip(valid, found)]
        peak = jnp.maximum(jnp.maximum(found[0], found[1]), found[2])
        peak = jnp.max(jnp.max(peak, axis=0, keepdims=True), axis=1, keepdims=True)
        w = [jnp.where(v, jnp.exp(f - peak), 0.0) for v, f in zip(valid, found)]
        total = w[0] + w[1] + w[2]
        total = jnp.sum(jnp.sum(total, axis=0, keepdims=True), axis=1, keepdims=True)
        stat_ref[pl.ds(2 * slot, 1), :] = jnp.broadcast_to(peak, (1, LANES))
        stat_ref[pl.ds(2 * slot + 1, 1), :] = jnp.broadcast_to(total, (1, LANES))
        upper = lines < classes
        first = jnp.where(upper, w[0], w[0] + w[1])
        second = jnp.where(upper, w[1] + w[2], w[0] - w[1])
        third = w[1] - w[2]
        third = jnp.where(upper, third, 0.0)
        weight_ref[slot] = first + pltpu.roll(second, SPAN, 1) + pltpu.roll(third, 2 * SPAN, 1)

    for b in range(count):

        def body(i, carry, b=b):
            @pl.when(
                (meta[b * block + i, DOM] == my_dom)
                & ((meta[b * block + i, OWNER] == my_cls) | (meta[b * block + i, OWNER + 1] == my_cls))
            )
            def _():
                one(b, i)

            return carry

        lax.fori_loop(0, block, body, 0)


def score(place, buffers, refs, tables, slots, classes, after):
    count, block = len(buffers), buffers[0].shape[0]
    width = refs.shape[2]
    return pl.pallas_call(
        functools.partial(score_kernel, count, len(after)),
        out_shape=(
            jax.ShapeDtypeStruct((slots, 2 * classes, LANES), jnp.float32),
            jax.ShapeDtypeStruct((2 * slots, LANES), jnp.float32),
            jax.ShapeDtypeStruct((slots, 3), jnp.int32),
        ),
        in_specs=[SMEM_SPEC] + [VMEM_SPEC] * count + [HBM_SPEC] * len(after) + [VMEM_SPEC] * 2,
        out_specs=(VMEM_SPEC, VMEM_SPEC, SMEM_SPEC),
        scratch_shapes=[
            pltpu.VMEM((2 * LANES, width), jnp.bfloat16),
            pltpu.VMEM((48 * classes, width), jnp.bfloat16),
            pltpu.VMEM((3, 2 * classes, LANES), jnp.float32),
            pltpu.VMEM((count * block, LANES), jnp.int32),
            pltpu.SMEM((count * block, LANES), jnp.int32),
            pltpu.SemaphoreType.DMA,
        ],
        compiler_params=pltpu.CompilerParams(vmem_limit_bytes=VMEM_LIMIT),
        cost_estimate=pl.CostEstimate(flops=10**10, bytes_accessed=10**7, transcendentals=0),
        name="score",
    )(place, *buffers, *after, refs, tables)


def weight_kernel(flip, place_ref, partner_ref, weight_ref, *refs):
    stat_refs, out_ref = refs[:-1], refs[-1]
    slots, lines, _ = weight_ref.shape
    my_cls = place_ref[0]
    done = []
    for slot in range(slots):
        other, other_slot = partner_ref[slot, OTHER], partner_ref[slot, OTHER_SLOT]
        at = pl.ds(2 * other_slot, 2)
        if flip:
            mine = stat_refs[0][2 * slot : 2 * slot + 2, :]
            theirs = mine
            for k in range(1, len(stat_refs)):
                theirs = jnp.where(jnp.bitwise_xor(other, my_cls) == k, stat_refs[k][at, :], theirs)
        else:
            mine = stat_refs[0][my_cls, 2 * slot : 2 * slot + 2, :]
            theirs = stat_refs[0][other, at, :]
        peak = jnp.maximum(mine[0:1], theirs[0:1])
        gain = jnp.exp(mine[0:1] - peak)
        mass = mine[1:2] * gain + theirs[1:2] * jnp.exp(theirs[0:1] - peak)
        factor = gain / jnp.where(partner_ref[slot, FILLED] > 0, mass, 1.0)
        done.append(weight_ref[slot] * factor)
    out_ref[...] = jnp.concatenate(done, axis=0).astype(out_ref.dtype)


def normalise(flip, place, partners, weights, stats):
    slots, lines, _ = weights.shape
    return pl.pallas_call(
        functools.partial(weight_kernel, flip),
        out_shape=jax.ShapeDtypeStruct((slots * lines, LANES), jnp.bfloat16),
        in_specs=[SMEM_SPEC] * 2 + [VMEM_SPEC] * (1 + len(stats)),
        out_specs=VMEM_SPEC,
        name="normalise",
    )(place, partners, weights, *stats)


def sum_kernel(weight_rows, relative, z_size, y_size, lines, local, width, count, n_weights, first, last, place_ref, *refs):
    refs = list(refs)
    image_refs = [refs.pop(0) for _ in range(count)]
    weight_refs = [refs.pop(0) for _ in range(n_weights)]
    table_ref = refs.pop(0)
    given = None if first else [refs.pop(0), refs.pop(0)]
    out_ref = refs.pop(0) if last else None
    if not last:
        totals, mass = refs.pop(0), refs.pop(0)
    images, weights, moved, meta_vmem, meta, active, image_sem, meta_sem = refs[:8]
    if last:
        totals, mass = refs[8:10]
    given_sem = refs[-1]
    depth, wave = images.shape[0], images.shape[1]
    per_row = weight_rows
    chunk = weight_refs[0].shape[0]
    classes = lines // 2
    waves = sum(ref.shape[0] for ref in image_refs) // wave

    def copies(w):
        out, at = [], 0
        for b, ref in enumerate(image_refs):
            size = ref.shape[0]
            low, high = max(at, w * wave), min(at + size, (w + 1) * wave)
            if low < high:
                source = ref.at[pl.ds(low - at, high - low)]
                target = images.at[w % depth, pl.ds(low - w * wave, high - low)]
                out.append(pltpu.make_async_copy(source, target, image_sem.at[w % depth, b]))
            at += size
        return out

    for w in range(min(depth, waves)):
        for copy in copies(w):
            copy.start()
    if first:
        mass[...] = jnp.zeros_like(mass)
        totals[...] = jnp.zeros_like(totals)
    else:
        held = [pltpu.make_async_copy(g, t, given_sem.at[k]) for k, (g, t) in enumerate(zip(given, (totals, mass)))]
        for copy in held:
            copy.start()
    moved[...] = jnp.zeros_like(moved)
    for b in range(n_weights):
        weights[b * chunk : (b + 1) * chunk, :] = weight_refs[b][...].astype(jnp.float32)
    my_cls, my_dom = place_ref[0], place_ref[1]
    my_z, my_y = lax.div(my_dom, y_size), lax.rem(my_dom, y_size)
    lane = lax.broadcasted_iota(jnp.int32, (lines, LANES), 1)
    lane_wide = lax.broadcasted_iota(jnp.int32, (SPAN, LANES), 1)

    for w in range(waves):
        for copy in copies(w):
            copy.wait()
        here = images.at[w % depth]
        for i in range(wave):
            read_meta(here[i, IMAGE_ROWS:, :], meta_vmem, i)
        move_metas(meta_vmem, meta, meta_sem)
        number = collect(meta, active, wave, my_cls)
        if w == 0 and not first:
            for copy in held:
                copy.wait()

        def prepare_one(i, share, buffer):
            side = side_of(meta, i, my_cls)
            q = meta[i, DOM]
            if relative:
                d_z = lax.rem(my_z - lax.div(q, y_size) + z_size, z_size)
                d_y = lax.rem(my_y - lax.rem(q, y_size) + y_size, y_size)
                q = d_z * y_size + d_y
            at = pl.multiple_of(q * per_row + meta[i, SLOT + side] * lines, lines)
            mine = weights[pl.ds(at, lines), :] * share
            values = here[i, :IMAGE_ROWS, :].astype(jnp.float32)
            for step in range(STEP_ANGLES):
                re, im, (c1, s1, c2, s2) = step_pieces(values, table_ref, step)
                store_moved(moved.at[buffer], step, 0, [re, re * c1, im * s1, re * c2, im * s2])
                store_moved(moved.at[buffer], step, 1, [im, im * c1, -re * s1, im * c2, -re * s2])
            parts = []
            for k in range(3):
                part = jnp.where((lane >= k * SPAN) & (lane < (k + 1) * SPAN), mine, 0.0)
                parts.append(part + pltpu.roll(part, LANES - ROT, 1))
            blocks = []
            for j in range(classes):
                line = []
                for half in range(2):
                    at = half * classes + j
                    turned = [
                        pltpu.roll(
                            jnp.broadcast_to(parts[k][at : at + 1], (SPAN, LANES)), 1, 1, stride=1, stride_axis=0
                        )
                        for k in range(3 - half)
                    ]
                    tile = jnp.where(lane_wide < SPAN, turned[0], turned[1])
                    if half == 0:
                        tile = jnp.where(lane_wide < 2 * SPAN, tile, turned[2])
                    line.append(tile)
                blocks.append(jnp.concatenate(line, axis=1))
            spread = jnp.concatenate(blocks, axis=0).astype(jnp.bfloat16)
            plain = jnp.where(lane < 2 * SPAN, mine, 0.0)
            plain_high = jnp.where(lane < SPAN, mine, 0.0)
            masses = [plain[j : j + 1] + plain_high[classes + j : classes + j + 1] for j in range(classes)]
            chosen = [meta[i, CLASS + side * classes + j] for j in range(classes)]
            return spread, masses, chosen

        def add_one(added, masses, chosen):
            for j in range(classes):
                c = chosen[j]
                for tile in range(width // LANES):
                    at = pl.ds(pl.multiple_of(tile * local * SPAN + c * SPAN, 8), SPAN)
                    totals[at, :] += added[j * SPAN : (j + 1) * SPAN, tile * LANES : (tile + 1) * LANES]
                mass[pl.ds(c, 1), :] += masses[j]

        def two(step, carry):
            first = active[2 * step]
            second_at = 2 * step + 1
            second = active[jnp.minimum(second_at, number - 1)]
            share = jnp.where(second_at < number, 1.0, 0.0).astype(jnp.float32)
            one_spread, one_mass, one_chosen = prepare_one(first, 1.0, 0)
            two_spread, two_mass, two_chosen = prepare_one(second, share, 1)
            one_added = jnp.dot(one_spread, moved[0], preferred_element_type=jnp.float32)
            two_added = jnp.dot(two_spread, moved[1], preferred_element_type=jnp.float32)
            add_one(one_added, one_mass, one_chosen)
            add_one(two_added, two_mass, two_chosen)
            return carry

        lax.fori_loop(0, lax.div(number + 1, 2), two, 0)
        if w + depth < waves:
            for copy in copies(w + depth):
                copy.start()

    if not last:
        return
    scale = 1.0 / (jnp.sum(mass[:local, :], axis=1, keepdims=True) + PRIOR_MASS)
    for turn in range(ROT):
        for tile in range(width // LANES):
            line = totals[pl.ds(tile * local * SPAN + ROT - 1 - turn, local, stride=SPAN), :]
            out_ref[:, pl.ds(turn * width + tile * LANES, LANES)] = (line * scale).astype(out_ref.dtype)


def class_sum(place, buffers, weights, tables, given, last, relative, z_size, y_size, local, width, lines, weight_rows):
    count = len(buffers)
    total = sum(buffer.shape[0] for buffer in buffers)
    wave = total if total <= 128 else math.gcd(total, 128)
    depth = min(2, total // wave)
    totals = (width // LANES * local * SPAN, LANES)
    mass = (-(-local // 8) * 8, LANES)
    first = given is None
    out = jax.ShapeDtypeStruct((local, ROT * width), jnp.bfloat16)
    held = tuple(jax.ShapeDtypeStruct(shape, jnp.float32) for shape in (totals, mass))
    scratch = [
        pltpu.VMEM((depth, wave, IMAGE_ROWS + META_ROWS, LANES), jnp.bfloat16),
        pltpu.VMEM((len(weights) * weights[0].shape[0], LANES), jnp.float32),
        pltpu.VMEM((2, 2 * LANES, width), jnp.bfloat16),
        pltpu.VMEM((wave, LANES), jnp.int32),
        pltpu.SMEM((wave, LANES), jnp.int32),
        pltpu.SMEM((wave + 1,), jnp.int32),
        pltpu.SemaphoreType.DMA((depth, count)),
        pltpu.SemaphoreType.DMA,
    ]
    if last:
        scratch += [pltpu.VMEM(totals, jnp.float32), pltpu.VMEM(mass, jnp.float32)]
    scratch += [pltpu.SemaphoreType.DMA((2,))]
    return pl.pallas_call(
        functools.partial(
            sum_kernel, weight_rows, relative, z_size, y_size, lines, local, width, count, len(weights), first, last
        ),
        out_shape=out if last else held,
        in_specs=[SMEM_SPEC]
        + [HBM_SPEC] * count
        + [VMEM_SPEC] * (len(weights) + 1)
        + ([] if first else [HBM_SPEC] * 2),
        out_specs=VMEM_SPEC if last else (VMEM_SPEC, VMEM_SPEC),
        scratch_shapes=scratch,
        compiler_params=pltpu.CompilerParams(vmem_limit_bytes=VMEM_LIMIT),
        cost_estimate=pl.CostEstimate(flops=total * 2 * 10**8, bytes_accessed=10**7, transcendentals=0),
        name="class_sum",
    )(place, *buffers, *weights, tables, *([] if first else given))


def shards(x_size, y_size, z_size, particles, references, candidates, offsets):
    groups = lax.axis_size("cls")
    doms = lax.axis_size("dom")
    count, width = particles.shape
    local = references.shape[0]
    classes = candidates.shape[1] // 2
    block_width = width // ROT
    slots = groups * (count // 2)
    tables = trig_tables()
    place = jnp.stack([lax.axis_index("cls"), lax.axis_index("dom")]).astype(jnp.int32)

    def moves(goal):
        out = []
        for cls in range(groups):
            for dom in range(doms):
                x, core, z, y = goal(cls // 2, cls % 2, dom // y_size, dom % y_size)
                to = ((x % x_size) * 2 + core) * doms + (z % z_size) * y_size + y % y_size
                out.append((cls * doms + dom, to))
        return out

    def send(value, goal):
        return lax.ppermute(value, ("cls", "dom"), moves(goal))

    swap = functools.partial(send, goal=lambda x, c, z, y: (x, 1 - c, z, y))
    along_z = functools.partial(send, goal=lambda x, c, z, y: (x, c, z + 1, y))
    back_z = functools.partial(send, goal=lambda x, c, z, y: (x, c, z - 1, y))
    early = functools.partial(send, goal=lambda x, c, z, y: (x + 1 - c, c, z, y + c))
    late = functools.partial(send, goal=lambda x, c, z, y: (x + c, c, z, y + 1 - c))

    images = particles.reshape(count, width // LANES, LANES)
    record = jnp.concatenate([candidates, offsets], axis=1)
    mine, rest = prepare(place, record, swap(record), images, swap(images), jnp.asarray(tables), local)
    refs = references.reshape(local, ROT, block_width)
    steps = jnp.asarray(tables[:, 1])
    tuned = x_size == 2 and y_size == 2 and z_size == 4
    if tuned:
        e0, l0, z1 = early(mine), late(mine), along_z(mine)
        e0, l0, z1, refs = lax.optimization_barrier((e0, l0, z1, refs))
        row = [mine, rest, e0, l0, swap(e0), swap(l0)]
        e1, l1, z2, f0 = early(z1), late(z1), along_z(z1), late(e0)
        z3 = back_z(lax.optimization_barrier((mine, z1))[0])
    else:
        row = [lax.all_gather(mine, "cls", axis=0, tiled=True)]
        parts = [[lax.all_gather(row[0], "dom", axis=0, tiled=True)]]

    weights, stats, partners = score(place, row, refs, steps, slots, classes, [z1] if tuned else [])
    if tuned:
        stats = [
            stats,
            swap(stats),
            send(stats, lambda x, c, z, y: (x + 1, c, z, y)),
            send(stats, lambda x, c, z, y: (x + 1, 1 - c, z, y)),
        ]
        weights, z2, z3, e1, l1, f0 = lax.optimization_barrier((weights, z2, z3, e1, l1, f0))
        z23 = jnp.concatenate([z2, z3])
        e23, f1 = early(z23), late(e1)
        weights = normalise(tuned, place, partners, weights, stats)
        pair = jnp.concatenate([weights, send(weights, lambda x, c, z, y: (x, c, z, y + 1))])
        pair, e23, f1, z23 = lax.optimization_barrier((pair, e23, f1, z23))
        weights = [pair] + [send(pair, lambda x, c, z, y, dz=dz: (x, c, z + dz, y)) for dz in range(1, z_size)]
        l23, f23 = late(z23), late(e23)
        middle = [z1, e1, l1, f0, f1, e23]
        parts = [row + middle + [z23] + [swap(block) for block in [z1, z2, z3, *middle[1:]]], [l23, f23]]
    else:
        stats = [lax.all_gather(stats, "cls", axis=0, tiled=False)]
        weights = normalise(tuned, place, partners, weights, stats)
        weights = [lax.all_gather(weights, "dom", axis=0, tiled=True)]
    held = None
    for k, part in enumerate(parts):
        if k:
            *part, _ = lax.optimization_barrier((*part, held[1]))
            part = part + [swap(block) for block in part]
        held = class_sum(
            place, part, weights, steps, held, k == len(parts) - 1, tuned, z_size, y_size, local, block_width, 2 * classes, slots * 2 * classes
        )
    return held


def solution(mesh):
    coords = [device.coords for device in mesh.devices.flat]
    sizes = [len({c[axis] for c in coords}) for axis in range(3)]
    in_specs = (
        P(("cls", "dom"), None),
        P("cls", None),
        P(("cls", "dom"), None),
        P(("cls", "dom"), None),
    )
    out_specs = P("cls", None)
    return jax.shard_map(
        functools.partial(shards, *sizes),
        mesh=mesh,
        in_specs=in_specs,
        out_specs=out_specs,
        check_vma=False,
    )
```

```python
import functools
import math

import jax
import jax.numpy as jnp
import numpy as np
from jax import lax
from jax.experimental import pallas as pl
from jax.experimental.pallas import tpu as pltpu
from jax.sharding import PartitionSpec as P

CYCLES = 128
ANGLES = 144
ROT = 36
SHIFTS = 5
BOX = 256
LANES = 128
SPAN = 40
STEP_ANGLES = ANGLES // ROT
PIECES = 2 * STEP_ANGLES
IMAGE_ROWS = PIECES * SPAN
REACH = 7

SOFTMAX_WARMTH = 2.0
PRIOR_MASS = 1.0
NEGATIVE = -1e30
META_ROWS = 16
VMEM_LIMIT = 60 * 1024 * 1024
DOM, OWNER, SLOT, CLASS = 0, 1, 3, 5
FILLED, OTHER, OTHER_SLOT = 0, 1, 2


def trig_tables():
    theta = 2.0 * np.pi * np.arange(ANGLES) / ANGLES
    radius = np.arange(1, CYCLES + 1)
    out = np.zeros((4, REACH + 1, STEP_ANGLES, SPAN, CYCLES), np.float32)
    for axis, direction in enumerate((np.cos(theta), np.sin(theta))):
        for t in range(REACH + 1):
            phase = 2.0 * np.pi / BOX * t * direction[:, None] * radius[None, :]
            for part, fn in enumerate((np.cos, np.sin)):
                table = fn(phase).reshape(ROT, STEP_ANGLES, CYCLES).transpose(1, 0, 2)
                out[2 * axis + part, t, :, :ROT] = table[:, ::-1]
    return out.reshape(4, REACH + 1, STEP_ANGLES * SPAN, CYCLES)


def axis_phase(table_ref, axis, step, move):
    size = jnp.abs(move)
    sign = jnp.where(move < 0, -1.0, 1.0).astype(jnp.float32)
    at = pl.ds(step * SPAN, SPAN)
    return table_ref[2 * axis, size, at, :], table_ref[2 * axis + 1, size, at, :] * sign


def prep_kernel(local, place_ref, near_ref, far_ref, image_near, image_far, table_ref, mine_ref, rest_ref, raw):
    count = near_ref.shape[0]
    listed = near_ref.shape[1] - 2
    rows = image_near.shape[1]
    half = listed // 2
    share = count // 2
    my_cls, my_dom = place_ref[0], place_ref[1]
    core = lax.rem(my_cls, 2)
    raw[...] = jnp.zeros_like(raw)
    lane = lax.broadcasted_iota(jnp.int32, (META_ROWS, LANES), 1)
    for far in range(2):
        record, image_ref = (far_ref, image_far) if far else (near_ref, image_near)
        source_core = 1 - core if far else core
        source = my_cls - core + source_core
        cand = [[record[u, k] for k in range(listed)] for u in range(count)]
        owner = [[lax.div(c, local) for c in row] for row in cand]
        pair = []
        for u in range(count):
            first = owner[u][0]
            second = first
            for k in range(1, listed):
                second = jnp.where(owner[u][k] != first, owner[u][k], second)
            pair.append((first, second))
        for u in range(count):
            entries = [my_dom, pair[u][0], pair[u][1]]
            for side in range(2):
                value = source * (count // 2)
                for v in range(u):
                    lists = (pair[v][0] == pair[u][side]) | (pair[v][1] == pair[u][side])
                    value = value + jnp.where(lists, 1, 0)
                entries.append(value)
            for side in range(2):
                classes = [jnp.int32(0)] * half
                seen = jnp.int32(0)
                for k in range(listed):
                    hit = owner[u][k] == pair[u][side]
                    for j in range(half):
                        classes[j] = jnp.where(hit & (seen == j), cand[u][k] - pair[u][side] * local, classes[j])
                    seen = seen + jnp.where(hit, 1, 0)
                entries += classes
            tile = jnp.zeros((META_ROWS, LANES), jnp.int32)
            for k, value in enumerate(entries):
                tile = jnp.where(lane == k, value, tile)
            values = image_ref[u].astype(jnp.float32)
            for block in range(rows // PIECES):
                at = rows - (block + 1) * PIECES
                raw[at : at + PIECES, :] = values[block * PIECES : (block + 1) * PIECES]
            moved = []
            for step in range(STEP_ANGLES):
                re = raw[pl.ds(2 * step, SPAN, stride=PIECES), :]
                im = raw[pl.ds(2 * step + 1, SPAN, stride=PIECES), :]
                cx, sx = axis_phase(table_ref, 0, step, record[u, listed])
                cy, sy = axis_phase(table_ref, 1, step, record[u, listed + 1])
                cosine = cx * cy - sx * sy
                sine = sx * cy + cx * sy
                moved += [re * cosine + im * sine, im * cosine - re * sine]
            moved = jnp.concatenate(moved, axis=0).astype(mine_ref.dtype)
            tile = tile.astype(jnp.float32).astype(mine_ref.dtype)
            at = source_core * share + u % share
            role = u // share

            @pl.when(core == role)
            def _():
                mine_ref[at, :IMAGE_ROWS, :] = moved
                mine_ref[at, IMAGE_ROWS:, :] = tile

            @pl.when(core != role)
            def _():
                rest_ref[at, :IMAGE_ROWS, :] = moved
                rest_ref[at, IMAGE_ROWS:, :] = tile


SMEM_SPEC = pl.BlockSpec(memory_space=pltpu.SMEM)
VMEM_SPEC = pl.BlockSpec(memory_space=pltpu.VMEM)
HBM_SPEC = pl.BlockSpec(memory_space=pl.ANY)


def prepare(place, near, far, image_near, image_far, tables, local):
    count = near.shape[0]
    shape = jax.ShapeDtypeStruct((count, IMAGE_ROWS + META_ROWS, LANES), image_near.dtype)
    return pl.pallas_call(
        functools.partial(prep_kernel, local),
        out_shape=(shape, shape),
        in_specs=[SMEM_SPEC] * 3 + [VMEM_SPEC] * 3,
        out_specs=(VMEM_SPEC, VMEM_SPEC),
        scratch_shapes=[pltpu.VMEM((IMAGE_ROWS, LANES), jnp.float32)],
        compiler_params=pltpu.CompilerParams(vmem_limit_bytes=VMEM_LIMIT),
        name="prepare",
    )(place, near, far, image_near, image_far, tables)


def read_meta(source, meta_vmem, row):
    meta_vmem[pl.ds(row, 1), :] = source.astype(jnp.float32)[0:1, :].astype(jnp.int32)


def move_metas(meta_vmem, meta, sem):
    copy = pltpu.make_async_copy(meta_vmem, meta, sem)
    copy.start()
    copy.wait()


def side_of(meta, i, my_cls):
    return jnp.where(meta[i, OWNER] == my_cls, 0, 1)


def collect(meta, active, total, my_cls):
    def look(i, n):
        mine = (meta[i, OWNER] == my_cls) | (meta[i, OWNER + 1] == my_cls)
        active[n] = i
        return n + jnp.where(mine, 1, 0)

    return lax.fori_loop(0, total, look, jnp.int32(0), unroll=4)


def step_pieces(values, table_ref, step):
    re = values[2 * step * SPAN : (2 * step + 1) * SPAN]
    im = values[(2 * step + 1) * SPAN : (2 * step + 2) * SPAN]
    at = pl.ds(step * SPAN, SPAN)
    return re, im, [table_ref[k, at, :] for k in range(4)]


def store_moved(moved, step, part, blocks):
    at = pl.ds((2 * step + part) * LANES, LANES)
    pad = jnp.zeros((8, LANES), jnp.float32)
    moved[:LANES, at] = jnp.concatenate([*blocks[:3], pad], axis=0).astype(jnp.bfloat16)
    moved[LANES : LANES + 2 * SPAN, at] = jnp.concatenate(blocks[3:], axis=0).astype(jnp.bfloat16)


def score_kernel(count, given, place_ref, *refs):
    image_refs = refs[:count]
    (
        refs_ref, table_ref, weight_ref, stat_ref, partner_ref,
        moved, picked, sums, meta_vmem, meta, sem,
    ) = refs[count + given :]
    before = refs[count : count + given]
    block = image_refs[0].shape[0]
    slots = weight_ref.shape[0]
    classes = picked.shape[0] // 48
    my_cls, my_dom = place_ref[0], place_ref[1]
    moved[...] = jnp.zeros_like(moved)
    picked[...] = jnp.zeros_like(picked)
    if given:
        weight_ref[...] = before[0][...]
        stat_ref[...] = before[1][...]
    else:
        weight_ref[...] = jnp.zeros_like(weight_ref)
        stat_ref[...] = jnp.zeros_like(stat_ref)
    sums[...] = jnp.zeros_like(sums)
    for b in range(count):
        for i in range(block):
            read_meta(image_refs[b][i, IMAGE_ROWS:, :], meta_vmem, b * block + i)
    move_metas(meta_vmem, meta, sem)
    for slot in range(slots):
        for k in range(3):
            partner_ref[slot, k] = before[2][slot, k] if given else 0
    lane = lax.broadcasted_iota(jnp.int32, (SPAN, LANES), 1)

    def one(b, i):
        side = side_of(meta, b * block + i, my_cls)
        index = b * block + i
        slot = meta[index, SLOT + side]
        partner_ref[slot, FILLED] = 1
        partner_ref[slot, OTHER] = meta[index, OWNER + 1 - side]
        partner_ref[slot, OTHER_SLOT] = meta[index, SLOT + 1 - side]
        for j in range(classes):
            picked[j * 48 : j * 48 + ROT, :] = refs_ref[meta[index, CLASS + side * classes + j]]
        values = image_refs[b][i, :IMAGE_ROWS, :].astype(jnp.float32)
        for step in range(STEP_ANGLES):
            re, im, (c1, s1, c2, s2) = step_pieces(values, table_ref, step)
            a1, b1, d1, e1 = re * c1, im * s1, im * c1, re * s1
            a2, b2, d2, e2 = re * c2, im * s2, im * c2, re * s2
            store_moved(moved, step, 0, [re, a1 + b1, a1 - b1, a2 + b2, a2 - b2])
            store_moved(moved, step, 1, [im, d1 - e1, d1 + e1, d2 - e2, d2 + e2])
        pairs = lax.dot_general(
            picked[...], moved[...], (((1,), (1,)), ((), ())), preferred_element_type=jnp.float32
        )
        for s in range(SHIFTS):
            half, k = divmod(s, 3)
            for j in range(classes):
                part = pairs[j * 48 : j * 48 + SPAN, half * LANES : (half + 1) * LANES]
                part = jnp.where((lane >= k * SPAN) & (lane < (k + 1) * SPAN), part, 0.0)
                turned = pltpu.roll(part, 0, 1, stride=1, stride_axis=0)
                sums[k, pl.ds(half * classes + j, 1), :] = jnp.sum(turned, axis=0, keepdims=True)
        found = []
        for k in range(3):
            plain = pltpu.roll(sums[k], (LANES - k * SPAN) % LANES, 1) if k else sums[k]
            found.append(SOFTMAX_WARMTH * (plain + pltpu.roll(plain, LANES - ROT, 1)))
        lanes = lax.broadcasted_iota(jnp.int32, found[0].shape, 1)
        lines = lax.broadcasted_iota(jnp.int32, found[0].shape, 0)
        valid = [lanes < ROT, lanes < ROT, (lanes < ROT) & (lines < classes)]
        found = [jnp.where(v, f, NEGATIVE) for v, f in zip(valid, found)]
        peak = jnp.maximum(jnp.maximum(found[0], found[1]), found[2])
        peak = jnp.max(jnp.max(peak, axis=0, keepdims=True), axis=1, keepdims=True)
        w = [jnp.where(v, jnp.exp(f - peak), 0.0) for v, f in zip(valid, found)]
        total = w[0] + w[1] + w[2]
        total = jnp.sum(jnp.sum(total, axis=0, keepdims=True), axis=1, keepdims=True)
        stat_ref[pl.ds(2 * slot, 1), :] = jnp.broadcast_to(peak, (1, LANES))
        stat_ref[pl.ds(2 * slot + 1, 1), :] = jnp.broadcast_to(total, (1, LANES))
        upper = lines < classes
        first = jnp.where(upper, w[0], w[0] + w[1])
        second = jnp.where(upper, w[1] + w[2], w[0] - w[1])
        third = w[1] - w[2]
        third = jnp.where(upper, third, 0.0)
        weight_ref[slot] = first + pltpu.roll(second, SPAN, 1) + pltpu.roll(third, 2 * SPAN, 1)

    for b in range(count):

        def body(i, carry, b=b):
            @pl.when(
                (meta[b * block + i, DOM] == my_dom)
                & ((meta[b * block + i, OWNER] == my_cls) | (meta[b * block + i, OWNER + 1] == my_cls))
            )
            def _():
                one(b, i)

            return carry

        lax.fori_loop(0, block, body, 0)


def score(place, buffers, refs, tables, slots, classes, before=()):
    count, block = len(buffers), buffers[0].shape[0]
    width = refs.shape[2]
    return pl.pallas_call(
        functools.partial(score_kernel, count, len(before)),
        out_shape=(
            jax.ShapeDtypeStruct((slots, 2 * classes, LANES), jnp.float32),
            jax.ShapeDtypeStruct((2 * slots, LANES), jnp.float32),
            jax.ShapeDtypeStruct((slots, 3), jnp.int32),
        ),
        in_specs=[SMEM_SPEC] + [VMEM_SPEC] * count + [VMEM_SPEC, VMEM_SPEC, SMEM_SPEC][: len(before)] + [VMEM_SPEC] * 2,
        out_specs=(VMEM_SPEC, VMEM_SPEC, SMEM_SPEC),
        scratch_shapes=[
            pltpu.VMEM((2 * LANES, width), jnp.bfloat16),
            pltpu.VMEM((48 * classes, width), jnp.bfloat16),
            pltpu.VMEM((3, 2 * classes, LANES), jnp.float32),
            pltpu.VMEM((count * block, LANES), jnp.int32),
            pltpu.SMEM((count * block, LANES), jnp.int32),
            pltpu.SemaphoreType.DMA,
        ],
        compiler_params=pltpu.CompilerParams(vmem_limit_bytes=VMEM_LIMIT),
        cost_estimate=pl.CostEstimate(flops=5 * 10**9, bytes_accessed=10**7, transcendentals=0),
        name="score",
    )(place, *buffers, *before, refs, tables)


def weight_kernel(flip, place_ref, partner_ref, weight_ref, *refs):
    stat_refs, out_ref = refs[:-1], refs[-1]
    slots, lines, _ = weight_ref.shape
    my_cls = place_ref[0]
    done = []
    for slot in range(slots):
        other, other_slot = partner_ref[slot, OTHER], partner_ref[slot, OTHER_SLOT]
        at = pl.ds(2 * other_slot, 2)
        if flip:
            mine = stat_refs[0][2 * slot : 2 * slot + 2, :]
            theirs = mine
            for k in range(1, len(stat_refs)):
                theirs = jnp.where(jnp.bitwise_xor(other, my_cls) == k, stat_refs[k][at, :], theirs)
        else:
            mine = stat_refs[0][my_cls, 2 * slot : 2 * slot + 2, :]
            theirs = stat_refs[0][other, at, :]
        peak = jnp.maximum(mine[0:1], theirs[0:1])
        gain = jnp.exp(mine[0:1] - peak)
        mass = mine[1:2] * gain + theirs[1:2] * jnp.exp(theirs[0:1] - peak)
        factor = gain / jnp.where(partner_ref[slot, FILLED] > 0, mass, 1.0)
        done.append(weight_ref[slot] * factor)
    out_ref[...] = jnp.concatenate(done, axis=0).astype(out_ref.dtype)


def normalise(flip, place, partners, weights, stats):
    slots, lines, _ = weights.shape
    return pl.pallas_call(
        functools.partial(weight_kernel, flip),
        out_shape=jax.ShapeDtypeStruct((slots * lines, LANES), jnp.bfloat16),
        in_specs=[SMEM_SPEC] * 2 + [VMEM_SPEC] * (1 + len(stats)),
        out_specs=VMEM_SPEC,
        name="normalise",
    )(place, partners, weights, *stats)


def sum_kernel(weight_rows, relative, z_size, y_size, lines, local, width, count, n_weights, first, last, place_ref, *refs):
    refs = list(refs)
    image_refs = [refs.pop(0) for _ in range(count)]
    weight_refs = [refs.pop(0) for _ in range(n_weights)]
    table_ref = refs.pop(0)
    given = None if first else [refs.pop(0), refs.pop(0)]
    out_ref = refs.pop(0) if last else None
    if not last:
        totals, mass = refs.pop(0), refs.pop(0)
    images, weights, moved_a, moved_b, spread_a, spread_b, meta_vmem, meta, active, image_sem, meta_sem = refs[:11]
    if last:
        totals, mass = refs[11:13]
    given_sem = refs[-1]
    depth, wave = images.shape[0], images.shape[1]
    per_row = weight_rows
    chunk = weight_refs[0].shape[0]
    classes = lines // 2
    waves = sum(ref.shape[0] for ref in image_refs) // wave

    def copies(w):
        out, at = [], 0
        for b, ref in enumerate(image_refs):
            size = ref.shape[0]
            low, high = max(at, w * wave), min(at + size, (w + 1) * wave)
            if low < high:
                source = ref.at[pl.ds(low - at, high - low)]
                target = images.at[w % depth, pl.ds(low - w * wave, high - low)]
                out.append(pltpu.make_async_copy(source, target, image_sem.at[w % depth, b]))
            at += size
        return out

    for w in range(min(depth, waves)):
        for copy in copies(w):
            copy.start()
    if first:
        mass[...] = jnp.zeros_like(mass)
        totals[...] = jnp.zeros_like(totals)
    else:
        held = [pltpu.make_async_copy(g, t, given_sem.at[k]) for k, (g, t) in enumerate(zip(given, (totals, mass)))]
        for copy in held:
            copy.start()
    moved_a[...] = jnp.zeros_like(moved_a)
    moved_b[...] = jnp.zeros_like(moved_b)
    for b in range(n_weights):
        weights[b * chunk : (b + 1) * chunk, :] = weight_refs[b][...].astype(jnp.float32)
    my_cls, my_dom = place_ref[0], place_ref[1]
    my_z, my_y = lax.div(my_dom, y_size), lax.rem(my_dom, y_size)
    lane = lax.broadcasted_iota(jnp.int32, (lines, LANES), 1)
    lane_wide = lax.broadcasted_iota(jnp.int32, (SPAN, LANES), 1)

    for w in range(waves):
        for copy in copies(w):
            copy.wait()
        here = images.at[w % depth]
        for i in range(wave):
            read_meta(here[i, IMAGE_ROWS:, :], meta_vmem, i)
        move_metas(meta_vmem, meta, meta_sem)
        number = collect(meta, active, wave, my_cls)
        if w == 0 and not first:
            for copy in held:
                copy.wait()

        def prepare_one(at, moved, spread):
            i = active[jnp.minimum(at, number - 1)]
            share = jnp.where(at < number, 1.0, 0.0).astype(jnp.float32)
            side = side_of(meta, i, my_cls)
            q = meta[i, DOM]
            if relative:
                d_z = lax.rem(my_z - lax.div(q, y_size) + z_size, z_size)
                d_y = lax.rem(my_y - lax.rem(q, y_size) + y_size, y_size)
                q = d_y * z_size + d_z
            at = pl.multiple_of(q * per_row + meta[i, SLOT + side] * lines, lines)
            mine = weights[pl.ds(at, lines), :] * share
            values = here[i, :IMAGE_ROWS, :].astype(jnp.float32)
            for step in range(STEP_ANGLES):
                re, im, (c1, s1, c2, s2) = step_pieces(values, table_ref, step)
                store_moved(moved, step, 0, [re, re * c1, im * s1, re * c2, im * s2])
                store_moved(moved, step, 1, [im, im * c1, -re * s1, im * c2, -re * s2])
            parts = []
            for k in range(3):
                part = jnp.where((lane >= k * SPAN) & (lane < (k + 1) * SPAN), mine, 0.0)
                parts.append(part + pltpu.roll(part, LANES - ROT, 1))
            blocks = []
            for j in range(classes):
                line = []
                for half in range(2):
                    at = half * classes + j
                    turned = [
                        pltpu.roll(
                            jnp.broadcast_to(parts[k][at : at + 1], (SPAN, LANES)), 1, 1, stride=1, stride_axis=0
                        )
                        for k in range(3 - half)
                    ]
                    tile = jnp.where(lane_wide < SPAN, turned[0], turned[1])
                    if half == 0:
                        tile = jnp.where(lane_wide < 2 * SPAN, tile, turned[2])
                    line.append(tile)
                blocks.append(jnp.concatenate(line, axis=1))
            spread[...] = jnp.concatenate(blocks, axis=0).astype(jnp.bfloat16)
            plain = jnp.where(lane < 2 * SPAN, mine, 0.0)
            plain_high = jnp.where(lane < SPAN, mine, 0.0)
            for j in range(classes):
                c = meta[i, CLASS + side * classes + j]
                mass[pl.ds(c, 1), :] += plain[j : j + 1] + plain_high[classes + j : classes + j + 1]

        def add_one(at, added):
            i = active[jnp.minimum(at, number - 1)]
            side = side_of(meta, i, my_cls)
            for j in range(classes):
                c = meta[i, CLASS + side * classes + j]
                for tile in range(width // LANES):
                    to = pl.ds(pl.multiple_of(tile * local * SPAN + c * SPAN, 8), SPAN)
                    totals[to, :] += added[j * SPAN : (j + 1) * SPAN, tile * LANES : (tile + 1) * LANES]

        def two(step, carry):
            at = 2 * step
            added = jnp.dot(spread_a[...], moved_a[...], preferred_element_type=jnp.float32)
            prepare_one(at + 1, moved_b, spread_b)
            add_one(at, added)
            added = jnp.dot(spread_b[...], moved_b[...], preferred_element_type=jnp.float32)
            prepare_one(at + 2, moved_a, spread_a)
            add_one(at + 1, added)
            return carry

        @pl.when(number > 0)
        def _():
            prepare_one(0, moved_a, spread_a)

        lax.fori_loop(0, lax.div(number + 1, 2), two, 0)
        if w + depth < waves:
            for copy in copies(w + depth):
                copy.start()

    if not last:
        return
    scale = 1.0 / (jnp.sum(mass[:local, :], axis=1, keepdims=True) + PRIOR_MASS)
    for turn in range(ROT):
        for tile in range(width // LANES):
            line = totals[pl.ds(tile * local * SPAN + ROT - 1 - turn, local, stride=SPAN), :]
            out_ref[:, pl.ds(turn * width + tile * LANES, LANES)] = (line * scale).astype(out_ref.dtype)


def class_sum(place, buffers, weights, tables, given, last, relative, z_size, y_size, local, width, lines, weight_rows):
    count = len(buffers)
    total = sum(buffer.shape[0] for buffer in buffers)
    wave = total if total <= 128 else math.gcd(total, 128)
    depth = min(2, total // wave)
    totals = (width // LANES * local * SPAN, LANES)
    mass = (-(-local // 8) * 8, LANES)
    first = given is None
    out = jax.ShapeDtypeStruct((local, ROT * width), jnp.bfloat16)
    held = tuple(jax.ShapeDtypeStruct(shape, jnp.float32) for shape in (totals, mass))
    scratch = [
        pltpu.VMEM((depth, wave, IMAGE_ROWS + META_ROWS, LANES), jnp.bfloat16),
        pltpu.VMEM((len(weights) * weights[0].shape[0], LANES), jnp.float32),
        pltpu.VMEM((2 * LANES, width), jnp.bfloat16),
        pltpu.VMEM((2 * LANES, width), jnp.bfloat16),
        pltpu.VMEM((lines // 2 * SPAN, 2 * LANES), jnp.bfloat16),
        pltpu.VMEM((lines // 2 * SPAN, 2 * LANES), jnp.bfloat16),
        pltpu.VMEM((wave, LANES), jnp.int32),
        pltpu.SMEM((wave, LANES), jnp.int32),
        pltpu.SMEM((wave + 1,), jnp.int32),
        pltpu.SemaphoreType.DMA((depth, count)),
        pltpu.SemaphoreType.DMA,
    ]
    if last:
        scratch += [pltpu.VMEM(totals, jnp.float32), pltpu.VMEM(mass, jnp.float32)]
    scratch += [pltpu.SemaphoreType.DMA((2,))]
    return pl.pallas_call(
        functools.partial(
            sum_kernel, weight_rows, relative, z_size, y_size, lines, local, width, count, len(weights), first, last
        ),
        out_shape=out if last else held,
        in_specs=[SMEM_SPEC]
        + [HBM_SPEC] * count
        + [VMEM_SPEC] * (len(weights) + 1)
        + ([] if first else [HBM_SPEC] * 2),
        out_specs=VMEM_SPEC if last else (VMEM_SPEC, VMEM_SPEC),
        scratch_shapes=scratch,
        compiler_params=pltpu.CompilerParams(vmem_limit_bytes=VMEM_LIMIT),
        cost_estimate=pl.CostEstimate(flops=total * 2 * 10**8, bytes_accessed=10**7, transcendentals=0),
        name="class_sum",
    )(place, *buffers, *weights, tables, *([] if first else given))


def shards(x_size, y_size, z_size, particles, references, candidates, offsets):
    groups = lax.axis_size("cls")
    doms = lax.axis_size("dom")
    count, width = particles.shape
    local = references.shape[0]
    classes = candidates.shape[1] // 2
    block_width = width // ROT
    slots = groups * (count // 2)
    tables = trig_tables()
    place = jnp.stack([lax.axis_index("cls"), lax.axis_index("dom")]).astype(jnp.int32)

    def moves(goal):
        out = []
        for cls in range(groups):
            for dom in range(doms):
                x, core, z, y = goal(cls // 2, cls % 2, dom // y_size, dom % y_size)
                to = ((x % x_size) * 2 + core) * doms + (z % z_size) * y_size + y % y_size
                out.append((cls * doms + dom, to))
        return out

    def send(value, goal):
        return lax.ppermute(value, ("cls", "dom"), moves(goal))

    swap = functools.partial(send, goal=lambda x, c, z, y: (x, 1 - c, z, y))
    along_z = functools.partial(send, goal=lambda x, c, z, y: (x, c, z + 1, y))
    back_z = functools.partial(send, goal=lambda x, c, z, y: (x, c, z - 1, y))
    early = functools.partial(send, goal=lambda x, c, z, y: (x + 1 - c, c, z, y + c))
    late = functools.partial(send, goal=lambda x, c, z, y: (x + c, c, z, y + 1 - c))

    images = particles.reshape(count, width // LANES, LANES)
    record = jnp.concatenate([candidates, offsets], axis=1)
    mine, rest = prepare(place, record, swap(record), images, swap(images), jnp.asarray(tables), local)
    refs = lax.optimization_barrier((references, mine))[0].reshape(local, ROT, block_width)
    steps = jnp.asarray(tables[:, 1])
    tuned = x_size == 2 and y_size == 2 and z_size == 4
    if tuned:
        e0, l0, z1 = early(mine), late(mine), along_z(mine)
        found = score(place, [mine, rest], refs, steps, slots, classes)
        *found, e0, l0, z1 = lax.optimization_barrier((*found, e0, l0, z1))
        row = [e0, l0, swap(e0), swap(l0)]
        e1, l1, z2, f0 = early(z1), late(z1), along_z(z1), late(e0)
        z3 = back_z(lax.optimization_barrier((mine, z1))[0])
        weights, stats, partners = score(place, row, refs, steps, slots, classes, found)
        stats = [
            stats,
            swap(stats),
            send(stats, lambda x, c, z, y: (x + 1, c, z, y)),
            send(stats, lambda x, c, z, y: (x + 1, 1 - c, z, y)),
        ]
        z2, z3, e1, l1, f0, *_ = lax.optimization_barrier((z2, z3, e1, l1, f0, *stats))
        z23 = jnp.concatenate([z2, z3])
        f1, e23 = late(e1), early(z23)
        weights = normalise(tuned, place, partners, weights, stats)
        weights = [weights] + [send(weights, lambda x, c, z, y, dz=dz: (x, c, z + dz, y)) for dz in range(1, z_size)]
        weights = jnp.concatenate(weights)
        weights = [weights, send(weights, lambda x, c, z, y: (x, c, z, y + 1))]
        z23, e23, f1, *weights = lax.optimization_barrier((z23, e23, f1, *weights))
        l23, f23 = late(z23), late(e23)
        ready = [z1, e1, l1, f0, f1, e23]
        ready = [mine, rest, *row, z23, *ready, *[swap(block) for block in [z2, z3, *ready]]]
        parts = [ready, [l23, f23]]
    else:
        row = lax.all_gather(mine, "cls", axis=0, tiled=True)
        parts = [[lax.all_gather(row, "dom", axis=0, tiled=True)]]
        weights, stats, partners = score(place, [row], refs, steps, slots, classes)
        stats = [lax.all_gather(stats, "cls", axis=0, tiled=False)]
        weights = normalise(tuned, place, partners, weights, stats)
        weights = [lax.all_gather(weights, "dom", axis=0, tiled=True)]
    held = None
    for k, part in enumerate(parts):
        if k:
            *part, _ = lax.optimization_barrier((*part, held[1]))
            part = part + [swap(block) for block in part]
        held = class_sum(
            place, part, weights, steps, held, k == len(parts) - 1, tuned, z_size, y_size, local, block_width, 2 * classes, slots * 2 * classes
        )
    return held


def solution(mesh):
    coords = [device.coords for device in mesh.devices.flat]
    sizes = [len({c[axis] for c in coords}) for axis in range(3)]
    in_specs = (
        P(("cls", "dom"), None),
        P("cls", None),
        P(("cls", "dom"), None),
        P(("cls", "dom"), None),
    )
    out_specs = P("cls", None)
    return jax.shard_map(
        functools.partial(shards, *sizes),
        mesh=mesh,
        in_specs=in_specs,
        out_specs=out_specs,
        check_vma=False,
    )
```

```python
import functools
import math

import jax
import jax.numpy as jnp
import numpy as np
from jax import lax
from jax.experimental import pallas as pl
from jax.experimental.pallas import tpu as pltpu
from jax.sharding import PartitionSpec as P

CYCLES = 128
ANGLES = 144
ROT = 36
SHIFTS = 5
BOX = 256
LANES = 128
SPAN = 40
STEP_ANGLES = ANGLES // ROT
PIECES = 2 * STEP_ANGLES
IMAGE_ROWS = PIECES * SPAN
REACH = 7

SOFTMAX_WARMTH = 2.0
PRIOR_MASS = 1.0
NEGATIVE = -1e30
META_ROWS = 16
VMEM_LIMIT = 60 * 1024 * 1024
DOM, OWNER, SLOT, CLASS = 0, 1, 3, 5
FILLED, OTHER, OTHER_SLOT = 0, 1, 2


def trig_tables():
    theta = 2.0 * np.pi * np.arange(ANGLES) / ANGLES
    radius = np.arange(1, CYCLES + 1)
    out = np.zeros((4, REACH + 1, STEP_ANGLES, SPAN, CYCLES), np.float32)
    for axis, direction in enumerate((np.cos(theta), np.sin(theta))):
        for t in range(REACH + 1):
            phase = 2.0 * np.pi / BOX * t * direction[:, None] * radius[None, :]
            for part, fn in enumerate((np.cos, np.sin)):
                table = fn(phase).reshape(ROT, STEP_ANGLES, CYCLES).transpose(1, 0, 2)
                out[2 * axis + part, t, :, :ROT] = table[:, ::-1]
    return out.reshape(4, REACH + 1, STEP_ANGLES * SPAN, CYCLES)


def axis_phase(table_ref, axis, step, move):
    size = jnp.abs(move)
    sign = jnp.where(move < 0, -1.0, 1.0).astype(jnp.float32)
    at = pl.ds(step * SPAN, SPAN)
    return table_ref[2 * axis, size, at, :], table_ref[2 * axis + 1, size, at, :] * sign


def prep_kernel(local, place_ref, near_ref, far_ref, image_near, image_far, table_ref, mine_ref, rest_ref, raw):
    count = near_ref.shape[0]
    listed = near_ref.shape[1] - 2
    rows = image_near.shape[1]
    half = listed // 2
    share = count // 2
    my_cls, my_dom = place_ref[0], place_ref[1]
    core = lax.rem(my_cls, 2)
    raw[...] = jnp.zeros_like(raw)
    lane = lax.broadcasted_iota(jnp.int32, (META_ROWS, LANES), 1)
    for far in range(2):
        record, image_ref = (far_ref, image_far) if far else (near_ref, image_near)
        source_core = 1 - core if far else core
        source = my_cls - core + source_core
        cand = [[record[u, k] for k in range(listed)] for u in range(count)]
        owner = [[lax.div(c, local) for c in row] for row in cand]
        pair = []
        for u in range(count):
            first = owner[u][0]
            second = first
            for k in range(1, listed):
                second = jnp.where(owner[u][k] != first, owner[u][k], second)
            pair.append((first, second))
        for u in range(count):
            entries = [my_dom, pair[u][0], pair[u][1]]
            for side in range(2):
                value = source * (count // 2)
                for v in range(u):
                    lists = (pair[v][0] == pair[u][side]) | (pair[v][1] == pair[u][side])
                    value = value + jnp.where(lists, 1, 0)
                entries.append(value)
            for side in range(2):
                classes = [jnp.int32(0)] * half
                seen = jnp.int32(0)
                for k in range(listed):
                    hit = owner[u][k] == pair[u][side]
                    for j in range(half):
                        classes[j] = jnp.where(hit & (seen == j), cand[u][k] - pair[u][side] * local, classes[j])
                    seen = seen + jnp.where(hit, 1, 0)
                entries += classes
            tile = jnp.zeros((META_ROWS, LANES), jnp.int32)
            for k, value in enumerate(entries):
                tile = jnp.where(lane == k, value, tile)
            values = image_ref[u].astype(jnp.float32)
            for block in range(rows // PIECES):
                at = rows - (block + 1) * PIECES
                raw[at : at + PIECES, :] = values[block * PIECES : (block + 1) * PIECES]
            moved = []
            for step in range(STEP_ANGLES):
                re = raw[pl.ds(2 * step, SPAN, stride=PIECES), :]
                im = raw[pl.ds(2 * step + 1, SPAN, stride=PIECES), :]
                cx, sx = axis_phase(table_ref, 0, step, record[u, listed])
                cy, sy = axis_phase(table_ref, 1, step, record[u, listed + 1])
                cosine = cx * cy - sx * sy
                sine = sx * cy + cx * sy
                moved += [re * cosine + im * sine, im * cosine - re * sine]
            moved = jnp.concatenate(moved, axis=0).astype(mine_ref.dtype)
            tile = tile.astype(jnp.float32).astype(mine_ref.dtype)
            at = source_core * share + u % share
            role = u // share

            @pl.when(core == role)
            def _():
                mine_ref[at, :IMAGE_ROWS, :] = moved
                mine_ref[at, IMAGE_ROWS:, :] = tile

            @pl.when(core != role)
            def _():
                rest_ref[at, :IMAGE_ROWS, :] = moved
                rest_ref[at, IMAGE_ROWS:, :] = tile


SMEM_SPEC = pl.BlockSpec(memory_space=pltpu.SMEM)
VMEM_SPEC = pl.BlockSpec(memory_space=pltpu.VMEM)
HBM_SPEC = pl.BlockSpec(memory_space=pl.ANY)


def prepare(place, near, far, image_near, image_far, tables, local):
    count = near.shape[0]
    shape = jax.ShapeDtypeStruct((count, IMAGE_ROWS + META_ROWS, LANES), image_near.dtype)
    return pl.pallas_call(
        functools.partial(prep_kernel, local),
        out_shape=(shape, shape),
        in_specs=[SMEM_SPEC] * 3 + [VMEM_SPEC] * 3,
        out_specs=(VMEM_SPEC, VMEM_SPEC),
        scratch_shapes=[pltpu.VMEM((IMAGE_ROWS, LANES), jnp.float32)],
        compiler_params=pltpu.CompilerParams(vmem_limit_bytes=VMEM_LIMIT),
        name="prepare",
    )(place, near, far, image_near, image_far, tables)


def read_meta(source, meta_vmem, row):
    meta_vmem[pl.ds(row, 1), :] = source.astype(jnp.float32)[0:1, :].astype(jnp.int32)


def move_metas(meta_vmem, meta, sem):
    copy = pltpu.make_async_copy(meta_vmem, meta, sem)
    copy.start()
    copy.wait()


def side_of(meta, i, my_cls):
    return jnp.where(meta[i, OWNER] == my_cls, 0, 1)


def collect(meta, active, total, my_cls, my_dom=None):
    def look(i, n):
        mine = (meta[i, OWNER] == my_cls) | (meta[i, OWNER + 1] == my_cls)
        if my_dom is not None:
            mine = mine & (meta[i, DOM] == my_dom)
        active[n] = i
        return n + jnp.where(mine, 1, 0)

    return lax.fori_loop(0, total, look, jnp.int32(0), unroll=4)


def step_pieces(values, table_ref, step):
    re = values[2 * step * SPAN : (2 * step + 1) * SPAN]
    im = values[(2 * step + 1) * SPAN : (2 * step + 2) * SPAN]
    at = pl.ds(step * SPAN, SPAN)
    return re, im, [table_ref[k, at, :] for k in range(4)]


def store_moved(moved, step, part, blocks):
    at = pl.ds((2 * step + part) * LANES, LANES)
    pad = jnp.zeros((8, LANES), jnp.float32)
    moved[:LANES, at] = jnp.concatenate([*blocks[:3], pad], axis=0).astype(jnp.bfloat16)
    moved[LANES : LANES + 2 * SPAN, at] = jnp.concatenate(blocks[3:], axis=0).astype(jnp.bfloat16)


def score_kernel(count, place_ref, *refs):
    image_refs = refs[:count]
    (
        refs_ref, table_ref, weight_ref, stat_ref, partner_ref,
        images, moved_a, moved_b, picked_a, picked_b, sums_a, sums_b, meta_vmem, meta, active, image_sem, sem,
    ) = refs[count:]
    total = images.shape[0]
    slots = weight_ref.shape[0]
    classes = picked_a.shape[0] // 48
    my_cls, my_dom = place_ref[0], place_ref[1]
    copies, at = [], 0
    for b, ref in enumerate(image_refs):
        copies.append(pltpu.make_async_copy(ref, images.at[pl.ds(at, ref.shape[0])], image_sem.at[b]))
        at += ref.shape[0]
    for copy in copies:
        copy.start()
    for ref in (moved_a, moved_b, picked_a, picked_b, sums_a, sums_b, weight_ref, stat_ref):
        ref[...] = jnp.zeros_like(ref)
    for slot in range(slots):
        for k in range(3):
            partner_ref[slot, k] = 0
    for copy in copies:
        copy.wait()
    for i in range(total):
        read_meta(images[i, IMAGE_ROWS:, :], meta_vmem, i)
    move_metas(meta_vmem, meta, sem)
    number = collect(meta, active, total, my_cls, my_dom)
    lane = lax.broadcasted_iota(jnp.int32, (SPAN, LANES), 1)

    def one(at, moved, picked, sums):
        index = active[jnp.minimum(at, number - 1)]
        side = side_of(meta, index, my_cls)
        slot = meta[index, SLOT + side]
        partner_ref[slot, FILLED] = 1
        partner_ref[slot, OTHER] = meta[index, OWNER + 1 - side]
        partner_ref[slot, OTHER_SLOT] = meta[index, SLOT + 1 - side]
        for j in range(classes):
            picked[j * 48 : j * 48 + ROT, :] = refs_ref[meta[index, CLASS + side * classes + j]]
        values = images[index, :IMAGE_ROWS, :].astype(jnp.float32)
        for step in range(STEP_ANGLES):
            re, im, (c1, s1, c2, s2) = step_pieces(values, table_ref, step)
            a1, b1, d1, e1 = re * c1, im * s1, im * c1, re * s1
            a2, b2, d2, e2 = re * c2, im * s2, im * c2, re * s2
            store_moved(moved, step, 0, [re, a1 + b1, a1 - b1, a2 + b2, a2 - b2])
            store_moved(moved, step, 1, [im, d1 - e1, d1 + e1, d2 - e2, d2 + e2])
        pairs = lax.dot_general(
            picked[...], moved[...], (((1,), (1,)), ((), ())), preferred_element_type=jnp.float32
        )
        for s in range(SHIFTS):
            half, k = divmod(s, 3)
            for j in range(classes):
                part = pairs[j * 48 : j * 48 + SPAN, half * LANES : (half + 1) * LANES]
                part = jnp.where((lane >= k * SPAN) & (lane < (k + 1) * SPAN), part, 0.0)
                turned = pltpu.roll(part, 0, 1, stride=1, stride_axis=0)
                sums[k, pl.ds(half * classes + j, 1), :] = jnp.sum(turned, axis=0, keepdims=True)
        found = []
        for k in range(3):
            plain = pltpu.roll(sums[k], (LANES - k * SPAN) % LANES, 1) if k else sums[k]
            found.append(SOFTMAX_WARMTH * (plain + pltpu.roll(plain, LANES - ROT, 1)))
        lanes = lax.broadcasted_iota(jnp.int32, found[0].shape, 1)
        lines = lax.broadcasted_iota(jnp.int32, found[0].shape, 0)
        valid = [lanes < ROT, lanes < ROT, (lanes < ROT) & (lines < classes)]
        found = [jnp.where(v, f, NEGATIVE) for v, f in zip(valid, found)]
        peak = jnp.maximum(jnp.maximum(found[0], found[1]), found[2])
        peak = jnp.max(jnp.max(peak, axis=0, keepdims=True), axis=1, keepdims=True)
        w = [jnp.where(v, jnp.exp(f - peak), 0.0) for v, f in zip(valid, found)]
        total = w[0] + w[1] + w[2]
        total = jnp.sum(jnp.sum(total, axis=0, keepdims=True), axis=1, keepdims=True)
        stat_ref[pl.ds(2 * slot, 1), :] = jnp.broadcast_to(peak, (1, LANES))
        stat_ref[pl.ds(2 * slot + 1, 1), :] = jnp.broadcast_to(total, (1, LANES))
        upper = lines < classes
        first = jnp.where(upper, w[0], w[0] + w[1])
        second = jnp.where(upper, w[1] + w[2], w[0] - w[1])
        third = w[1] - w[2]
        third = jnp.where(upper, third, 0.0)
        weight_ref[slot] = first + pltpu.roll(second, SPAN, 1) + pltpu.roll(third, 2 * SPAN, 1)

    def two(step, carry):
        one(2 * step, moved_a, picked_a, sums_a)
        one(2 * step + 1, moved_b, picked_b, sums_b)
        return carry

    lax.fori_loop(0, lax.div(number + 1, 2), two, 0)


def score(place, buffers, refs, tables, slots, classes):
    count, total = len(buffers), sum(buffer.shape[0] for buffer in buffers)
    width = refs.shape[2]
    return pl.pallas_call(
        functools.partial(score_kernel, count),
        out_shape=(
            jax.ShapeDtypeStruct((slots, 2 * classes, LANES), jnp.float32),
            jax.ShapeDtypeStruct((2 * slots, LANES), jnp.float32),
            jax.ShapeDtypeStruct((slots, 3), jnp.int32),
        ),
        in_specs=[SMEM_SPEC] + [HBM_SPEC] * count + [VMEM_SPEC] * 2,
        out_specs=(VMEM_SPEC, VMEM_SPEC, SMEM_SPEC),
        scratch_shapes=[
            pltpu.VMEM((total, IMAGE_ROWS + META_ROWS, LANES), jnp.bfloat16),
            *[pltpu.VMEM((2 * LANES, width), jnp.bfloat16)] * 2,
            *[pltpu.VMEM((48 * classes, width), jnp.bfloat16)] * 2,
            *[pltpu.VMEM((3, 2 * classes, LANES), jnp.float32)] * 2,
            pltpu.VMEM((total, LANES), jnp.int32),
            pltpu.SMEM((total, LANES), jnp.int32),
            pltpu.SMEM((total + 1,), jnp.int32),
            pltpu.SemaphoreType.DMA((count,)),
            pltpu.SemaphoreType.DMA,
        ],
        compiler_params=pltpu.CompilerParams(vmem_limit_bytes=VMEM_LIMIT),
        cost_estimate=pl.CostEstimate(flops=10**10, bytes_accessed=10**7, transcendentals=0),
        name="score",
    )(place, *buffers, refs, tables)


def weight_kernel(flip, place_ref, partner_ref, weight_ref, *refs):
    stat_refs, out_ref = refs[:-1], refs[-1]
    slots, lines, _ = weight_ref.shape
    my_cls = place_ref[0]
    done = []
    for slot in range(slots):
        other, other_slot = partner_ref[slot, OTHER], partner_ref[slot, OTHER_SLOT]
        at = pl.ds(2 * other_slot, 2)
        if flip:
            mine = stat_refs[0][2 * slot : 2 * slot + 2, :]
            theirs = mine
            for k in range(1, len(stat_refs)):
                theirs = jnp.where(jnp.bitwise_xor(other, my_cls) == k, stat_refs[k][at, :], theirs)
        else:
            mine = stat_refs[0][my_cls, 2 * slot : 2 * slot + 2, :]
            theirs = stat_refs[0][other, at, :]
        peak = jnp.maximum(mine[0:1], theirs[0:1])
        gain = jnp.exp(mine[0:1] - peak)
        mass = mine[1:2] * gain + theirs[1:2] * jnp.exp(theirs[0:1] - peak)
        factor = gain / jnp.where(partner_ref[slot, FILLED] > 0, mass, 1.0)
        done.append(weight_ref[slot] * factor)
    out_ref[...] = jnp.concatenate(done, axis=0).astype(out_ref.dtype)


def normalise(flip, place, partners, weights, stats):
    slots, lines, _ = weights.shape
    return pl.pallas_call(
        functools.partial(weight_kernel, flip),
        out_shape=jax.ShapeDtypeStruct((slots * lines, LANES), jnp.bfloat16),
        in_specs=[SMEM_SPEC] * 2 + [VMEM_SPEC] * (1 + len(stats)),
        out_specs=VMEM_SPEC,
        name="normalise",
    )(place, partners, weights, *stats)


def sum_kernel(weight_rows, relative, z_size, y_size, lines, local, width, count, n_weights, first, last, place_ref, *refs):
    refs = list(refs)
    image_refs = [refs.pop(0) for _ in range(count)]
    weight_refs = [refs.pop(0) for _ in range(n_weights)]
    table_ref = refs.pop(0)
    given = None if first else [refs.pop(0), refs.pop(0)]
    out_ref = refs.pop(0) if last else None
    if not last:
        totals, mass = refs.pop(0), refs.pop(0)
    images, weights, moved_a, moved_b, spread_a, spread_b, meta_vmem, meta, active, image_sem, meta_sem = refs[:11]
    if last:
        totals, mass = refs[11:13]
    given_sem = refs[-1]
    depth, wave = images.shape[0], images.shape[1]
    per_row = weight_rows
    chunk = weight_refs[0].shape[0]
    classes = lines // 2
    waves = sum(ref.shape[0] for ref in image_refs) // wave

    def copies(w):
        out, at = [], 0
        for b, ref in enumerate(image_refs):
            size = ref.shape[0]
            low, high = max(at, w * wave), min(at + size, (w + 1) * wave)
            if low < high:
                source = ref.at[pl.ds(low - at, high - low)]
                target = images.at[w % depth, pl.ds(low - w * wave, high - low)]
                out.append(pltpu.make_async_copy(source, target, image_sem.at[w % depth, b]))
            at += size
        return out

    for w in range(min(depth, waves)):
        for copy in copies(w):
            copy.start()
    if first:
        mass[...] = jnp.zeros_like(mass)
        totals[...] = jnp.zeros_like(totals)
    else:
        held = [pltpu.make_async_copy(g, t, given_sem.at[k]) for k, (g, t) in enumerate(zip(given, (totals, mass)))]
        for copy in held:
            copy.start()
    moved_a[...] = jnp.zeros_like(moved_a)
    moved_b[...] = jnp.zeros_like(moved_b)
    for b in range(n_weights):
        weights[b * chunk : (b + 1) * chunk, :] = weight_refs[b][...].astype(jnp.float32)
    my_cls, my_dom = place_ref[0], place_ref[1]
    my_z, my_y = lax.div(my_dom, y_size), lax.rem(my_dom, y_size)
    lane = lax.broadcasted_iota(jnp.int32, (lines, LANES), 1)
    lane_wide = lax.broadcasted_iota(jnp.int32, (SPAN, LANES), 1)

    for w in range(waves):
        for copy in copies(w):
            copy.wait()
        here = images.at[w % depth]
        for i in range(wave):
            read_meta(here[i, IMAGE_ROWS:, :], meta_vmem, i)
        move_metas(meta_vmem, meta, meta_sem)
        number = collect(meta, active, wave, my_cls)
        if w == 0 and not first:
            for copy in held:
                copy.wait()

        def prepare_one(at, moved, spread):
            i = active[jnp.minimum(at, number - 1)]
            share = jnp.where(at < number, 1.0, 0.0).astype(jnp.float32)
            side = side_of(meta, i, my_cls)
            q = meta[i, DOM]
            if relative:
                d_z = lax.rem(my_z - lax.div(q, y_size) + z_size, z_size)
                d_y = lax.rem(my_y - lax.rem(q, y_size) + y_size, y_size)
                q = d_y * z_size + d_z
            at = pl.multiple_of(q * per_row + meta[i, SLOT + side] * lines, lines)
            mine = weights[pl.ds(at, lines), :] * share
            values = here[i, :IMAGE_ROWS, :].astype(jnp.float32)
            for step in range(STEP_ANGLES):
                re, im, (c1, s1, c2, s2) = step_pieces(values, table_ref, step)
                store_moved(moved, step, 0, [re, re * c1, im * s1, re * c2, im * s2])
                store_moved(moved, step, 1, [im, im * c1, -re * s1, im * c2, -re * s2])
            parts = []
            for k in range(3):
                part = jnp.where((lane >= k * SPAN) & (lane < (k + 1) * SPAN), mine, 0.0)
                parts.append(part + pltpu.roll(part, LANES - ROT, 1))
            blocks = []
            for j in range(classes):
                line = []
                for half in range(2):
                    at = half * classes + j
                    turned = [
                        pltpu.roll(
                            jnp.broadcast_to(parts[k][at : at + 1], (SPAN, LANES)), 1, 1, stride=1, stride_axis=0
                        )
                        for k in range(3 - half)
                    ]
                    tile = jnp.where(lane_wide < SPAN, turned[0], turned[1])
                    if half == 0:
                        tile = jnp.where(lane_wide < 2 * SPAN, tile, turned[2])
                    line.append(tile)
                blocks.append(jnp.concatenate(line, axis=1))
            spread[...] = jnp.concatenate(blocks, axis=0).astype(jnp.bfloat16)
            plain = jnp.where(lane < 2 * SPAN, mine, 0.0)
            plain_high = jnp.where(lane < SPAN, mine, 0.0)
            for j in range(classes):
                c = meta[i, CLASS + side * classes + j]
                mass[pl.ds(c, 1), :] += plain[j : j + 1] + plain_high[classes + j : classes + j + 1]

        def add_one(at, added):
            i = active[jnp.minimum(at, number - 1)]
            side = side_of(meta, i, my_cls)
            for j in range(classes):
                c = meta[i, CLASS + side * classes + j]
                for tile in range(width // LANES):
                    to = pl.ds(pl.multiple_of(tile * local * SPAN + c * SPAN, 8), SPAN)
                    totals[to, :] += added[j * SPAN : (j + 1) * SPAN, tile * LANES : (tile + 1) * LANES]

        def two(step, carry):
            at = 2 * step
            added = jnp.dot(spread_a[...], moved_a[...], preferred_element_type=jnp.float32)
            prepare_one(at + 1, moved_b, spread_b)
            add_one(at, added)
            added = jnp.dot(spread_b[...], moved_b[...], preferred_element_type=jnp.float32)
            prepare_one(at + 2, moved_a, spread_a)
            add_one(at + 1, added)
            return carry

        @pl.when(number > 0)
        def _():
            prepare_one(0, moved_a, spread_a)

        lax.fori_loop(0, lax.div(number + 1, 2), two, 0)
        if w + depth < waves:
            for copy in copies(w + depth):
                copy.start()

    if not last:
        return
    scale = 1.0 / (jnp.sum(mass[:local, :], axis=1, keepdims=True) + PRIOR_MASS)
    for turn in range(ROT):
        for tile in range(width // LANES):
            line = totals[pl.ds(tile * local * SPAN + ROT - 1 - turn, local, stride=SPAN), :]
            out_ref[:, pl.ds(turn * width + tile * LANES, LANES)] = (line * scale).astype(out_ref.dtype)


def class_sum(place, buffers, weights, tables, given, last, relative, z_size, y_size, local, width, lines, weight_rows):
    count = len(buffers)
    total = sum(buffer.shape[0] for buffer in buffers)
    wave = total if total <= 128 else math.gcd(total, 128)
    depth = min(2, total // wave)
    totals = (width // LANES * local * SPAN, LANES)
    mass = (-(-local // 8) * 8, LANES)
    first = given is None
    out = jax.ShapeDtypeStruct((local, ROT * width), jnp.bfloat16)
    held = tuple(jax.ShapeDtypeStruct(shape, jnp.float32) for shape in (totals, mass))
    scratch = [
        pltpu.VMEM((depth, wave, IMAGE_ROWS + META_ROWS, LANES), jnp.bfloat16),
        pltpu.VMEM((len(weights) * weights[0].shape[0], LANES), jnp.float32),
        pltpu.VMEM((2 * LANES, width), jnp.bfloat16),
        pltpu.VMEM((2 * LANES, width), jnp.bfloat16),
        pltpu.VMEM((lines // 2 * SPAN, 2 * LANES), jnp.bfloat16),
        pltpu.VMEM((lines // 2 * SPAN, 2 * LANES), jnp.bfloat16),
        pltpu.VMEM((wave, LANES), jnp.int32),
        pltpu.SMEM((wave, LANES), jnp.int32),
        pltpu.SMEM((wave + 1,), jnp.int32),
        pltpu.SemaphoreType.DMA((depth, count)),
        pltpu.SemaphoreType.DMA,
    ]
    if last:
        scratch += [pltpu.VMEM(totals, jnp.float32), pltpu.VMEM(mass, jnp.float32)]
    scratch += [pltpu.SemaphoreType.DMA((2,))]
    return pl.pallas_call(
        functools.partial(
            sum_kernel, weight_rows, relative, z_size, y_size, lines, local, width, count, len(weights), first, last
        ),
        out_shape=out if last else held,
        in_specs=[SMEM_SPEC]
        + [HBM_SPEC] * count
        + [VMEM_SPEC] * (len(weights) + 1)
        + ([] if first else [HBM_SPEC] * 2),
        out_specs=VMEM_SPEC if last else (VMEM_SPEC, VMEM_SPEC),
        scratch_shapes=scratch,
        compiler_params=pltpu.CompilerParams(vmem_limit_bytes=VMEM_LIMIT),
        cost_estimate=pl.CostEstimate(flops=total * 2 * 10**8, bytes_accessed=10**7, transcendentals=0),
        name="class_sum",
    )(place, *buffers, *weights, tables, *([] if first else given))


def shards(x_size, y_size, z_size, particles, references, candidates, offsets):
    groups = lax.axis_size("cls")
    doms = lax.axis_size("dom")
    count, width = particles.shape
    local = references.shape[0]
    classes = candidates.shape[1] // 2
    block_width = width // ROT
    slots = groups * (count // 2)
    tables = trig_tables()
    place = jnp.stack([lax.axis_index("cls"), lax.axis_index("dom")]).astype(jnp.int32)

    def moves(goal):
        out = []
        for cls in range(groups):
            for dom in range(doms):
                x, core, z, y = goal(cls // 2, cls % 2, dom // y_size, dom % y_size)
                to = ((x % x_size) * 2 + core) * doms + (z % z_size) * y_size + y % y_size
                out.append((cls * doms + dom, to))
        return out

    def send(value, goal):
        return lax.ppermute(value, ("cls", "dom"), moves(goal))

    swap = functools.partial(send, goal=lambda x, c, z, y: (x, 1 - c, z, y))
    along_z = functools.partial(send, goal=lambda x, c, z, y: (x, c, z + 1, y))
    back_z = functools.partial(send, goal=lambda x, c, z, y: (x, c, z - 1, y))
    early = functools.partial(send, goal=lambda x, c, z, y: (x + 1 - c, c, z, y + c))
    late = functools.partial(send, goal=lambda x, c, z, y: (x + c, c, z, y + 1 - c))

    images = particles.reshape(count, width // LANES, LANES)
    record = jnp.concatenate([candidates, offsets], axis=1)
    mine, rest = prepare(place, record, swap(record), images, swap(images), jnp.asarray(tables), local)
    refs = lax.optimization_barrier((references, mine))[0].reshape(local, ROT, block_width)
    steps = jnp.asarray(tables[:, 1])
    tuned = x_size == 2 and y_size == 2 and z_size == 4
    if tuned:
        e0, l0, z1, z3 = early(mine), late(mine), along_z(mine), back_z(mine)
        e0, l0, z1, z3, refs = lax.optimization_barrier((e0, l0, z1, z3, refs))
        near = jnp.concatenate([e0, l0])
        row = [mine, rest, near, swap(near)]
        e1, l1, z2, f0 = early(z1), late(z1), along_z(z1), late(e0)
        weights, stats, partners = score(place, row, refs, steps, slots, classes)
        stats = [
            stats,
            swap(stats),
            send(stats, lambda x, c, z, y: (x + 1, c, z, y)),
            send(stats, lambda x, c, z, y: (x + 1, 1 - c, z, y)),
        ]
        z2, z3, e1, l1, f0, *_ = lax.optimization_barrier((z2, z3, e1, l1, f0, *stats))
        z23 = jnp.concatenate([z2, z3])
        f1, e23 = late(e1), early(z23)
        weights = normalise(tuned, place, partners, weights, stats)
        weights = [weights] + [send(weights, lambda x, c, z, y, dz=dz: (x, c, z + dz, y)) for dz in range(1, z_size)]
        weights = jnp.concatenate(weights)
        weights = [weights, send(weights, lambda x, c, z, y: (x, c, z, y + 1))]
        z23, e23, f1, *weights = lax.optimization_barrier((z23, e23, f1, *weights))
        l23, f23 = late(z23), late(e23)
        first = jnp.concatenate([z1, z23, e1, l1, f0])
        second = jnp.concatenate([f1, e23])
        parts = [[*row, first, second], [swap(first), swap(second), l23, f23]]
    else:
        row = lax.all_gather(mine, "cls", axis=0, tiled=True)
        parts = [[lax.all_gather(row, "dom", axis=0, tiled=True)]]
        weights, stats, partners = score(place, [row], refs, steps, slots, classes)
        stats = [lax.all_gather(stats, "cls", axis=0, tiled=False)]
        weights = normalise(tuned, place, partners, weights, stats)
        weights = [lax.all_gather(weights, "dom", axis=0, tiled=True)]
    held = None
    for k, part in enumerate(parts):
        if k:
            *end, _ = lax.optimization_barrier((*part[2:], held[1]))
            part = part[:2] + end + [swap(block) for block in end]
        held = class_sum(
            place, part, weights, steps, held, k == len(parts) - 1, tuned, z_size, y_size, local, block_width, 2 * classes, slots * 2 * classes
        )
    return held


def solution(mesh):
    coords = [device.coords for device in mesh.devices.flat]
    sizes = [len({c[axis] for c in coords}) for axis in range(3)]
    in_specs = (
        P(("cls", "dom"), None),
        P("cls", None),
        P(("cls", "dom"), None),
        P(("cls", "dom"), None),
    )
    out_specs = P("cls", None)
    return jax.shard_map(
        functools.partial(shards, *sizes),
        mesh=mesh,
        in_specs=in_specs,
        out_specs=out_specs,
        check_vma=False,
    )
```

```python
import functools
import math

import jax
import jax.numpy as jnp
import numpy as np
from jax import lax
from jax.experimental import pallas as pl
from jax.experimental.pallas import tpu as pltpu
from jax.sharding import PartitionSpec as P

CYCLES = 128
ANGLES = 144
ROT = 36
SHIFTS = 5
BOX = 256
LANES = 128
SPAN = 40
STEP_ANGLES = ANGLES // ROT
PIECES = 2 * STEP_ANGLES
IMAGE_ROWS = PIECES * SPAN
REACH = 7

SOFTMAX_WARMTH = 2.0
PRIOR_MASS = 1.0
NEGATIVE = -1e30
META_ROWS = 16
VMEM_LIMIT = 60 * 1024 * 1024
DOM, OWNER, SLOT, CLASS = 0, 1, 3, 5
FILLED, OTHER, OTHER_SLOT = 0, 1, 2


def trig_tables():
    theta = 2.0 * np.pi * np.arange(ANGLES) / ANGLES
    radius = np.arange(1, CYCLES + 1)
    out = np.zeros((4, REACH + 1, STEP_ANGLES, SPAN, CYCLES), np.float32)
    for axis, direction in enumerate((np.cos(theta), np.sin(theta))):
        for t in range(REACH + 1):
            phase = 2.0 * np.pi / BOX * t * direction[:, None] * radius[None, :]
            for part, fn in enumerate((np.cos, np.sin)):
                table = fn(phase).reshape(ROT, STEP_ANGLES, CYCLES).transpose(1, 0, 2)
                out[2 * axis + part, t, :, :ROT] = table[:, ::-1]
    return out.reshape(4, REACH + 1, STEP_ANGLES * SPAN, CYCLES)


def axis_phase(table_ref, axis, step, move):
    size = jnp.abs(move)
    sign = jnp.where(move < 0, -1.0, 1.0).astype(jnp.float32)
    at = pl.ds(step * SPAN, SPAN)
    return table_ref[2 * axis, size, at, :], table_ref[2 * axis + 1, size, at, :] * sign


def prep_kernel(local, place_ref, near_ref, far_ref, image_near, image_far, table_ref, mine_ref, rest_ref, raw):
    count = near_ref.shape[0]
    listed = near_ref.shape[1] - 2
    rows = image_near.shape[1]
    half = listed // 2
    share = count // 2
    my_cls, my_dom = place_ref[0], place_ref[1]
    core = lax.rem(my_cls, 2)
    raw[...] = jnp.zeros_like(raw)
    lane = lax.broadcasted_iota(jnp.int32, (META_ROWS, LANES), 1)
    for far in range(2):
        record, image_ref = (far_ref, image_far) if far else (near_ref, image_near)
        source_core = 1 - core if far else core
        source = my_cls - core + source_core
        cand = [[record[u, k] for k in range(listed)] for u in range(count)]
        owner = [[lax.div(c, local) for c in row] for row in cand]
        pair = []
        for u in range(count):
            first = owner[u][0]
            second = first
            for k in range(1, listed):
                second = jnp.where(owner[u][k] != first, owner[u][k], second)
            pair.append((first, second))
        for u in range(count):
            entries = [my_dom, pair[u][0], pair[u][1]]
            for side in range(2):
                value = source * (count // 2)
                for v in range(u):
                    lists = (pair[v][0] == pair[u][side]) | (pair[v][1] == pair[u][side])
                    value = value + jnp.where(lists, 1, 0)
                entries.append(value)
            for side in range(2):
                classes = [jnp.int32(0)] * half
                seen = jnp.int32(0)
                for k in range(listed):
                    hit = owner[u][k] == pair[u][side]
                    for j in range(half):
                        classes[j] = jnp.where(hit & (seen == j), cand[u][k] - pair[u][side] * local, classes[j])
                    seen = seen + jnp.where(hit, 1, 0)
                entries += classes
            tile = jnp.zeros((META_ROWS, LANES), jnp.int32)
            for k, value in enumerate(entries):
                tile = jnp.where(lane == k, value, tile)
            values = image_ref[u].astype(jnp.float32)
            for block in range(rows // PIECES):
                at = rows - (block + 1) * PIECES
                raw[at : at + PIECES, :] = values[block * PIECES : (block + 1) * PIECES]
            moved = []
            for step in range(STEP_ANGLES):
                re = raw[pl.ds(2 * step, SPAN, stride=PIECES), :]
                im = raw[pl.ds(2 * step + 1, SPAN, stride=PIECES), :]
                cx, sx = axis_phase(table_ref, 0, step, record[u, listed])
                cy, sy = axis_phase(table_ref, 1, step, record[u, listed + 1])
                cosine = cx * cy - sx * sy
                sine = sx * cy + cx * sy
                moved += [re * cosine + im * sine, im * cosine - re * sine]
            moved = jnp.concatenate(moved, axis=0).astype(mine_ref.dtype)
            tile = tile.astype(jnp.float32).astype(mine_ref.dtype)
            at = source_core * share + u % share
            role = u // share

            @pl.when(core == role)
            def _():
                mine_ref[at, :IMAGE_ROWS, :] = moved
                mine_ref[at, IMAGE_ROWS:, :] = tile

            @pl.when(core != role)
            def _():
                rest_ref[at, :IMAGE_ROWS, :] = moved
                rest_ref[at, IMAGE_ROWS:, :] = tile


SMEM_SPEC = pl.BlockSpec(memory_space=pltpu.SMEM)
VMEM_SPEC = pl.BlockSpec(memory_space=pltpu.VMEM)
HBM_SPEC = pl.BlockSpec(memory_space=pl.ANY)


def prepare(place, near, far, image_near, image_far, tables, local):
    count = near.shape[0]
    shape = jax.ShapeDtypeStruct((count, IMAGE_ROWS + META_ROWS, LANES), image_near.dtype)
    return pl.pallas_call(
        functools.partial(prep_kernel, local),
        out_shape=(shape, shape),
        in_specs=[SMEM_SPEC] * 3 + [VMEM_SPEC] * 3,
        out_specs=(VMEM_SPEC, VMEM_SPEC),
        scratch_shapes=[pltpu.VMEM((IMAGE_ROWS, LANES), jnp.float32)],
        compiler_params=pltpu.CompilerParams(vmem_limit_bytes=VMEM_LIMIT),
        name="prepare",
    )(place, near, far, image_near, image_far, tables)


def read_meta(source, meta_vmem, row):
    meta_vmem[pl.ds(row, 1), :] = source.astype(jnp.float32)[0:1, :].astype(jnp.int32)


def move_metas(meta_vmem, meta, sem):
    copy = pltpu.make_async_copy(meta_vmem, meta, sem)
    copy.start()
    copy.wait()


def side_of(meta, i, my_cls):
    return jnp.where(meta[i, OWNER] == my_cls, 0, 1)


def collect(meta, active, total, my_cls, my_dom=None):
    def look(i, n):
        mine = (meta[i, OWNER] == my_cls) | (meta[i, OWNER + 1] == my_cls)
        if my_dom is not None:
            mine = mine & (meta[i, DOM] == my_dom)
        active[n] = i
        return n + jnp.where(mine, 1, 0)

    return lax.fori_loop(0, total, look, jnp.int32(0), unroll=4)


def step_pieces(images, i, table_ref, step):
    values = images[i, 2 * step * SPAN : (2 * step + 2) * SPAN, :].astype(jnp.float32)
    re, im = values[:SPAN], values[SPAN:]
    at = pl.ds(step * SPAN, SPAN)
    return re, im, [table_ref[k, at, :] for k in range(4)]


def store_moved(moved, step, part, blocks):
    at = pl.ds((2 * step + part) * LANES, LANES)
    pad = jnp.zeros((8, LANES), jnp.float32)
    moved[:LANES, at] = jnp.concatenate([*blocks[:3], pad], axis=0).astype(jnp.bfloat16)
    moved[LANES : LANES + 2 * SPAN, at] = jnp.concatenate(blocks[3:], axis=0).astype(jnp.bfloat16)


def score_kernel(count, place_ref, *refs):
    image_refs = refs[:count]
    (
        refs_ref, table_ref, weight_ref, stat_ref, partner_ref,
        images, moved_a, moved_b, picked_a, picked_b, sums_a, sums_b, meta_vmem, meta, active, image_sem, sem,
    ) = refs[count:]
    total = images.shape[0]
    slots = weight_ref.shape[0]
    classes = picked_a.shape[0] // 48
    my_cls, my_dom = place_ref[0], place_ref[1]
    copies, at = [], 0
    for b, ref in enumerate(image_refs):
        copies.append(pltpu.make_async_copy(ref, images.at[pl.ds(at, ref.shape[0])], image_sem.at[b]))
        at += ref.shape[0]
    for copy in copies:
        copy.start()
    for ref in (moved_a, moved_b, picked_a, picked_b, sums_a, sums_b, weight_ref, stat_ref):
        ref[...] = jnp.zeros_like(ref)
    for slot in range(slots):
        for k in range(3):
            partner_ref[slot, k] = 0
    for copy in copies:
        copy.wait()
    for i in range(total):
        read_meta(images[i, IMAGE_ROWS:, :], meta_vmem, i)
    move_metas(meta_vmem, meta, sem)
    number = collect(meta, active, total, my_cls, my_dom)
    lane = lax.broadcasted_iota(jnp.int32, (SPAN, LANES), 1)

    def one(at, moved, picked, sums):
        index = active[jnp.minimum(at, number - 1)]
        side = side_of(meta, index, my_cls)
        slot = meta[index, SLOT + side]
        partner_ref[slot, FILLED] = 1
        partner_ref[slot, OTHER] = meta[index, OWNER + 1 - side]
        partner_ref[slot, OTHER_SLOT] = meta[index, SLOT + 1 - side]
        for j in range(classes):
            picked[j * 48 : j * 48 + ROT, :] = refs_ref[meta[index, CLASS + side * classes + j]]
        for step in range(STEP_ANGLES):
            re, im, (c1, s1, c2, s2) = step_pieces(images, index, table_ref, step)
            a1, b1, d1, e1 = re * c1, im * s1, im * c1, re * s1
            a2, b2, d2, e2 = re * c2, im * s2, im * c2, re * s2
            store_moved(moved, step, 0, [re, a1 + b1, a1 - b1, a2 + b2, a2 - b2])
            store_moved(moved, step, 1, [im, d1 - e1, d1 + e1, d2 - e2, d2 + e2])
        for s in range(SHIFTS):
            half, k = divmod(s, 3)
            if k == 0:
                pairs = lax.dot_general(
                    picked[...],
                    moved[half * LANES : (half + 1) * LANES, :],
                    (((1,), (1,)), ((), ())),
                    preferred_element_type=jnp.float32,
                )
            for j in range(classes):
                part = pairs[j * 48 : j * 48 + SPAN]
                part = jnp.where((lane >= k * SPAN) & (lane < (k + 1) * SPAN), part, 0.0)
                turned = pltpu.roll(part, 0, 1, stride=1, stride_axis=0)
                sums[k, pl.ds(half * classes + j, 1), :] = jnp.sum(turned, axis=0, keepdims=True)
        found = []
        for k in range(3):
            plain = pltpu.roll(sums[k], (LANES - k * SPAN) % LANES, 1) if k else sums[k]
            found.append(SOFTMAX_WARMTH * (plain + pltpu.roll(plain, LANES - ROT, 1)))
        lanes = lax.broadcasted_iota(jnp.int32, found[0].shape, 1)
        lines = lax.broadcasted_iota(jnp.int32, found[0].shape, 0)
        valid = [lanes < ROT, lanes < ROT, (lanes < ROT) & (lines < classes)]
        found = [jnp.where(v, f, NEGATIVE) for v, f in zip(valid, found)]
        peak = jnp.maximum(jnp.maximum(found[0], found[1]), found[2])
        peak = jnp.max(jnp.max(peak, axis=0, keepdims=True), axis=1, keepdims=True)
        w = [jnp.where(v, jnp.exp(f - peak), 0.0) for v, f in zip(valid, found)]
        total = w[0] + w[1] + w[2]
        total = jnp.sum(jnp.sum(total, axis=0, keepdims=True), axis=1, keepdims=True)
        stat_ref[pl.ds(2 * slot, 1), :] = jnp.broadcast_to(peak, (1, LANES))
        stat_ref[pl.ds(2 * slot + 1, 1), :] = jnp.broadcast_to(total, (1, LANES))
        upper = lines < classes
        first = jnp.where(upper, w[0], w[0] + w[1])
        second = jnp.where(upper, w[1] + w[2], w[0] - w[1])
        third = w[1] - w[2]
        third = jnp.where(upper, third, 0.0)
        weight_ref[slot] = first + pltpu.roll(second, SPAN, 1) + pltpu.roll(third, 2 * SPAN, 1)

    def two(step, carry):
        one(2 * step, moved_a, picked_a, sums_a)
        one(2 * step + 1, moved_b, picked_b, sums_b)
        return carry

    lax.fori_loop(0, lax.div(number + 1, 2), two, 0)


def score(place, buffers, refs, tables, slots, classes):
    count, total = len(buffers), sum(buffer.shape[0] for buffer in buffers)
    width = refs.shape[2]
    return pl.pallas_call(
        functools.partial(score_kernel, count),
        out_shape=(
            jax.ShapeDtypeStruct((slots, 2 * classes, LANES), jnp.float32),
            jax.ShapeDtypeStruct((2 * slots, LANES), jnp.float32),
            jax.ShapeDtypeStruct((slots, 3), jnp.int32),
        ),
        in_specs=[SMEM_SPEC] + [HBM_SPEC] * count + [VMEM_SPEC] * 2,
        out_specs=(VMEM_SPEC, VMEM_SPEC, SMEM_SPEC),
        scratch_shapes=[
            pltpu.VMEM((total, IMAGE_ROWS + META_ROWS, LANES), jnp.bfloat16),
            *[pltpu.VMEM((2 * LANES, width), jnp.bfloat16)] * 2,
            *[pltpu.VMEM((48 * classes, width), jnp.bfloat16)] * 2,
            *[pltpu.VMEM((3, 2 * classes, LANES), jnp.float32)] * 2,
            pltpu.VMEM((total, LANES), jnp.int32),
            pltpu.SMEM((total, LANES), jnp.int32),
            pltpu.SMEM((total + 1,), jnp.int32),
            pltpu.SemaphoreType.DMA((count,)),
            pltpu.SemaphoreType.DMA,
        ],
        compiler_params=pltpu.CompilerParams(vmem_limit_bytes=VMEM_LIMIT),
        cost_estimate=pl.CostEstimate(flops=10**10, bytes_accessed=10**7, transcendentals=0),
        name="score",
    )(place, *buffers, refs, tables)


def weight_kernel(flip, place_ref, partner_ref, weight_ref, *refs):
    stat_refs, out_ref = refs[:-1], refs[-1]
    slots, lines, _ = weight_ref.shape
    my_cls = place_ref[0]
    done = []
    for slot in range(slots):
        other, other_slot = partner_ref[slot, OTHER], partner_ref[slot, OTHER_SLOT]
        at = pl.ds(2 * other_slot, 2)
        if flip:
            mine = stat_refs[0][2 * slot : 2 * slot + 2, :]
            theirs = mine
            for k in range(1, len(stat_refs)):
                theirs = jnp.where(jnp.bitwise_xor(other, my_cls) == k, stat_refs[k][at, :], theirs)
        else:
            mine = stat_refs[0][my_cls, 2 * slot : 2 * slot + 2, :]
            theirs = stat_refs[0][other, at, :]
        peak = jnp.maximum(mine[0:1], theirs[0:1])
        gain = jnp.exp(mine[0:1] - peak)
        mass = mine[1:2] * gain + theirs[1:2] * jnp.exp(theirs[0:1] - peak)
        factor = gain / jnp.where(partner_ref[slot, FILLED] > 0, mass, 1.0)
        done.append(weight_ref[slot] * factor)
    out_ref[...] = jnp.concatenate(done, axis=0).astype(out_ref.dtype)


def normalise(flip, place, partners, weights, stats):
    slots, lines, _ = weights.shape
    return pl.pallas_call(
        functools.partial(weight_kernel, flip),
        out_shape=jax.ShapeDtypeStruct((slots * lines, LANES), jnp.bfloat16),
        in_specs=[SMEM_SPEC] * 2 + [VMEM_SPEC] * (1 + len(stats)),
        out_specs=VMEM_SPEC,
        name="normalise",
    )(place, partners, weights, *stats)


def sum_kernel(weight_rows, relative, z_size, y_size, lines, local, width, count, n_weights, first, last, place_ref, *refs):
    refs = list(refs)
    image_refs = [refs.pop(0) for _ in range(count)]
    weight_refs = [refs.pop(0) for _ in range(n_weights)]
    table_ref = refs.pop(0)
    given = None if first else [refs.pop(0), refs.pop(0)]
    out_ref = refs.pop(0) if last else None
    if not last:
        totals, mass = refs.pop(0), refs.pop(0)
    images, weights, moved_a, moved_b, spread_a, spread_b, meta_vmem, meta, active, image_sem, meta_sem = refs[:11]
    if last:
        totals, mass = refs[11:13]
    given_sem = refs[-1]
    depth, wave = images.shape[0], images.shape[1]
    per_row = weight_rows
    chunk = weight_refs[0].shape[0]
    classes = lines // 2
    waves = sum(ref.shape[0] for ref in image_refs) // wave

    def copies(w):
        out, at = [], 0
        for b, ref in enumerate(image_refs):
            size = ref.shape[0]
            low, high = max(at, w * wave), min(at + size, (w + 1) * wave)
            if low < high:
                source = ref.at[pl.ds(low - at, high - low)]
                target = images.at[w % depth, pl.ds(low - w * wave, high - low)]
                out.append(pltpu.make_async_copy(source, target, image_sem.at[w % depth, b]))
            at += size
        return out

    for w in range(min(depth, waves)):
        for copy in copies(w):
            copy.start()
    if first:
        mass[...] = jnp.zeros_like(mass)
        totals[...] = jnp.zeros_like(totals)
    else:
        held = [pltpu.make_async_copy(g, t, given_sem.at[k]) for k, (g, t) in enumerate(zip(given, (totals, mass)))]
        for copy in held:
            copy.start()
    moved_a[...] = jnp.zeros_like(moved_a)
    moved_b[...] = jnp.zeros_like(moved_b)
    for b in range(n_weights):
        weights[b * chunk : (b + 1) * chunk, :] = weight_refs[b][...].astype(jnp.float32)
    my_cls, my_dom = place_ref[0], place_ref[1]
    my_z, my_y = lax.div(my_dom, y_size), lax.rem(my_dom, y_size)
    lane = lax.broadcasted_iota(jnp.int32, (lines, LANES), 1)
    lane_wide = lax.broadcasted_iota(jnp.int32, (SPAN, LANES), 1)

    for w in range(waves):
        for copy in copies(w):
            copy.wait()
        here = images.at[w % depth]
        for i in range(wave):
            read_meta(here[i, IMAGE_ROWS:, :], meta_vmem, i)
        move_metas(meta_vmem, meta, meta_sem)
        number = collect(meta, active, wave, my_cls)
        if w == 0 and not first:
            for copy in held:
                copy.wait()

        def prepare_one(at, moved, spread):
            i = active[jnp.minimum(at, number - 1)]
            share = jnp.where(at < number, 1.0, 0.0).astype(jnp.float32)
            side = side_of(meta, i, my_cls)
            q = meta[i, DOM]
            if relative:
                d_z = lax.rem(my_z - lax.div(q, y_size) + z_size, z_size)
                d_y = lax.rem(my_y - lax.rem(q, y_size) + y_size, y_size)
                q = d_y * z_size + d_z
            at = pl.multiple_of(q * per_row + meta[i, SLOT + side] * lines, lines)
            mine = weights[pl.ds(at, lines), :] * share
            parts = []
            for k in range(3):
                part = jnp.where((lane >= k * SPAN) & (lane < (k + 1) * SPAN), mine, 0.0)
                parts.append(part + pltpu.roll(part, LANES - ROT, 1))

            def circulant(j):
                line = []
                for half in range(2):
                    at = half * classes + j
                    turned = [
                        pltpu.roll(
                            jnp.broadcast_to(parts[k][at : at + 1], (SPAN, LANES)), 1, 1, stride=1, stride_axis=0
                        )
                        for k in range(3 - half)
                    ]
                    tile = jnp.where(lane_wide < SPAN, turned[0], turned[1])
                    if half == 0:
                        tile = jnp.where(lane_wide < 2 * SPAN, tile, turned[2])
                    line.append(tile)
                return jnp.concatenate(line, axis=1)

            def one_step(step):
                re, im, (c1, s1, c2, s2) = step_pieces(here, i, table_ref, step)
                store_moved(moved, step, 0, [re, re * c1, im * s1, re * c2, im * s2])
                store_moved(moved, step, 1, [im, im * c1, -re * s1, im * c2, -re * s2])
                for j in range(step * 2, min(step * 2 + 2, classes), 2):
                    both = jnp.concatenate([circulant(j), circulant(j + 1)], axis=0)
                    spread[j * SPAN : (j + 2) * SPAN, :] = both.astype(jnp.bfloat16)
                if step == STEP_ANGLES - 1:
                    plain = jnp.where(lane < 2 * SPAN, mine, 0.0)
                    plain_high = jnp.where(lane < SPAN, mine, 0.0)
                    for j in range(classes):
                        c = meta[i, CLASS + side * classes + j]
                        mass[pl.ds(c, 1), :] += plain[j : j + 1] + plain_high[classes + j : classes + j + 1]

            return one_step

        def add_one(at, moved, spread, one_step):
            i = active[jnp.minimum(at, number - 1)]
            side = side_of(meta, i, my_cls)
            chosen = [meta[i, CLASS + side * classes + j] for j in range(classes)]
            for step in range(STEP_ANGLES):
                columns = pl.ds(2 * step * LANES, 2 * LANES)
                added = jnp.dot(spread[...], moved[:, columns], preferred_element_type=jnp.float32)
                one_step(step)
                for part in range(2):
                    for j in range(classes):
                        start = (2 * step + part) * local * SPAN
                        to = pl.ds(pl.multiple_of(start + chosen[j] * SPAN, 8), SPAN)
                        totals[to, :] += added[j * SPAN : (j + 1) * SPAN, part * LANES : (part + 1) * LANES]

        def two(step, carry):
            at = 2 * step
            add_one(at, moved_a, spread_a, prepare_one(at + 1, moved_b, spread_b))
            add_one(at + 1, moved_b, spread_b, prepare_one(at + 2, moved_a, spread_a))
            return carry

        @pl.when(number > 0)
        def _():
            start = prepare_one(0, moved_a, spread_a)
            for step in range(STEP_ANGLES):
                start(step)

        lax.fori_loop(0, lax.div(number + 1, 2), two, 0)
        if w + depth < waves:
            for copy in copies(w + depth):
                copy.start()

    if not last:
        return
    scale = 1.0 / (jnp.sum(mass[:local, :], axis=1, keepdims=True) + PRIOR_MASS)
    for turn in range(ROT):
        for tile in range(width // LANES):
            line = totals[pl.ds(tile * local * SPAN + ROT - 1 - turn, local, stride=SPAN), :]
            out_ref[:, pl.ds(turn * width + tile * LANES, LANES)] = (line * scale).astype(out_ref.dtype)


def class_sum(place, buffers, weights, tables, given, last, relative, z_size, y_size, local, width, lines, weight_rows):
    count = len(buffers)
    total = sum(buffer.shape[0] for buffer in buffers)
    wave = total if total <= 128 else math.gcd(total, 128)
    depth = min(2, total // wave)
    totals = (width // LANES * local * SPAN, LANES)
    mass = (-(-local // 8) * 8, LANES)
    first = given is None
    out = jax.ShapeDtypeStruct((local, ROT * width), jnp.bfloat16)
    held = tuple(jax.ShapeDtypeStruct(shape, jnp.float32) for shape in (totals, mass))
    scratch = [
        pltpu.VMEM((depth, wave, IMAGE_ROWS + META_ROWS, LANES), jnp.bfloat16),
        pltpu.VMEM((len(weights) * weights[0].shape[0], LANES), jnp.float32),
        pltpu.VMEM((2 * LANES, width), jnp.bfloat16),
        pltpu.VMEM((2 * LANES, width), jnp.bfloat16),
        pltpu.VMEM((lines // 2 * SPAN, 2 * LANES), jnp.bfloat16),
        pltpu.VMEM((lines // 2 * SPAN, 2 * LANES), jnp.bfloat16),
        pltpu.VMEM((wave, LANES), jnp.int32),
        pltpu.SMEM((wave, LANES), jnp.int32),
        pltpu.SMEM((wave + 1,), jnp.int32),
        pltpu.SemaphoreType.DMA((depth, count)),
        pltpu.SemaphoreType.DMA,
    ]
    if last:
        scratch += [pltpu.VMEM(totals, jnp.float32), pltpu.VMEM(mass, jnp.float32)]
    scratch += [pltpu.SemaphoreType.DMA((2,))]
    return pl.pallas_call(
        functools.partial(
            sum_kernel, weight_rows, relative, z_size, y_size, lines, local, width, count, len(weights), first, last
        ),
        out_shape=out if last else held,
        in_specs=[SMEM_SPEC]
        + [HBM_SPEC] * count
        + [VMEM_SPEC] * (len(weights) + 1)
        + ([] if first else [HBM_SPEC] * 2),
        out_specs=VMEM_SPEC if last else (VMEM_SPEC, VMEM_SPEC),
        scratch_shapes=scratch,
        compiler_params=pltpu.CompilerParams(vmem_limit_bytes=VMEM_LIMIT),
        cost_estimate=pl.CostEstimate(flops=total * 2 * 10**8, bytes_accessed=10**7, transcendentals=0),
        name="class_sum",
    )(place, *buffers, *weights, tables, *([] if first else given))


def shards(x_size, y_size, z_size, particles, references, candidates, offsets):
    groups = lax.axis_size("cls")
    doms = lax.axis_size("dom")
    count, width = particles.shape
    local = references.shape[0]
    classes = candidates.shape[1] // 2
    block_width = width // ROT
    slots = groups * (count // 2)
    tables = trig_tables()
    place = jnp.stack([lax.axis_index("cls"), lax.axis_index("dom")]).astype(jnp.int32)

    def moves(goal):
        out = []
        for cls in range(groups):
            for dom in range(doms):
                x, core, z, y = goal(cls // 2, cls % 2, dom // y_size, dom % y_size)
                to = ((x % x_size) * 2 + core) * doms + (z % z_size) * y_size + y % y_size
                out.append((cls * doms + dom, to))
        return out

    def send(value, goal):
        return lax.ppermute(value, ("cls", "dom"), moves(goal))

    swap = functools.partial(send, goal=lambda x, c, z, y: (x, 1 - c, z, y))
    along_z = functools.partial(send, goal=lambda x, c, z, y: (x, c, z + 1, y))
    back_z = functools.partial(send, goal=lambda x, c, z, y: (x, c, z - 1, y))
    early = functools.partial(send, goal=lambda x, c, z, y: (x + 1 - c, c, z, y + c))
    late = functools.partial(send, goal=lambda x, c, z, y: (x + c, c, z, y + 1 - c))

    images = particles.reshape(count, width // LANES, LANES)
    record = jnp.concatenate([candidates, offsets], axis=1)
    mine, rest = prepare(place, record, swap(record), images, swap(images), jnp.asarray(tables), local)
    refs = lax.optimization_barrier((references, mine))[0].reshape(local, ROT, block_width)
    steps = jnp.asarray(tables[:, 1])
    tuned = x_size == 2 and y_size == 2 and z_size == 4
    if tuned:
        e0, l0, z1, z3 = early(mine), late(mine), along_z(mine), back_z(mine)
        e0, l0, z1, z3, refs = lax.optimization_barrier((e0, l0, z1, z3, refs))
        near = jnp.concatenate([e0, l0])
        row = [mine, rest, near, swap(near)]
        e1, l1, z2, f0 = early(z1), late(z1), along_z(z1), late(e0)
        weights, stats, partners = score(place, row, refs, steps, slots, classes)
        stats = [
            stats,
            swap(stats),
            send(stats, lambda x, c, z, y: (x + 1, c, z, y)),
            send(stats, lambda x, c, z, y: (x + 1, 1 - c, z, y)),
        ]
        z2, z3, e1, l1, f0, *_ = lax.optimization_barrier((z2, z3, e1, l1, f0, *stats))
        z23 = jnp.concatenate([z2, z3])
        f1, e23 = late(e1), early(z23)
        weights = normalise(tuned, place, partners, weights, stats)
        weights = [weights] + [send(weights, lambda x, c, z, y, dz=dz: (x, c, z + dz, y)) for dz in range(1, z_size)]
        weights = jnp.concatenate(weights)
        weights = [weights, send(weights, lambda x, c, z, y: (x, c, z, y + 1))]
        z23, e23, f1, *weights = lax.optimization_barrier((z23, e23, f1, *weights))
        l23, f23 = late(z23), late(e23)
        first = jnp.concatenate([z1, z23, e1, l1, f0])
        second = jnp.concatenate([f1, e23])
        parts = [[*row, first, second], [swap(first), swap(second), l23, f23]]
    else:
        row = lax.all_gather(mine, "cls", axis=0, tiled=True)
        parts = [[lax.all_gather(row, "dom", axis=0, tiled=True)]]
        weights, stats, partners = score(place, [row], refs, steps, slots, classes)
        stats = [lax.all_gather(stats, "cls", axis=0, tiled=False)]
        weights = normalise(tuned, place, partners, weights, stats)
        weights = [lax.all_gather(weights, "dom", axis=0, tiled=True)]
    held = None
    for k, part in enumerate(parts):
        if k:
            *end, _ = lax.optimization_barrier((*part[2:], held[1]))
            part = part[:2] + end + [swap(block) for block in end]
        held = class_sum(
            place, part, weights, steps, held, k == len(parts) - 1, tuned, z_size, y_size, local, block_width, 2 * classes, slots * 2 * classes
        )
    return held


def solution(mesh):
    coords = [device.coords for device in mesh.devices.flat]
    sizes = [len({c[axis] for c in coords}) for axis in range(3)]
    in_specs = (
        P(("cls", "dom"), None),
        P("cls", None),
        P(("cls", "dom"), None),
        P(("cls", "dom"), None),
    )
    out_specs = P("cls", None)
    return jax.shard_map(
        functools.partial(shards, *sizes),
        mesh=mesh,
        in_specs=in_specs,
        out_specs=out_specs,
        check_vma=False,
    )
```

```python
import functools
import math

import jax
import jax.numpy as jnp
import numpy as np
from jax import lax
from jax.experimental import pallas as pl
from jax.experimental.pallas import tpu as pltpu
from jax.sharding import PartitionSpec as P

CYCLES = 128
ANGLES = 144
ROT = 36
SHIFTS = 5
BOX = 256
LANES = 128
SPAN = 40
STEP_ANGLES = ANGLES // ROT
PIECES = 2 * STEP_ANGLES
IMAGE_ROWS = PIECES * SPAN
REACH = 7

SOFTMAX_WARMTH = 2.0
PRIOR_MASS = 1.0
NEGATIVE = -1e30
META_ROWS = 16
VMEM_LIMIT = 60 * 1024 * 1024
DOM, OWNER, SLOT, CLASS = 0, 1, 3, 5
FILLED, OTHER, OTHER_SLOT = 0, 1, 2


def trig_tables():
    theta = 2.0 * np.pi * np.arange(ANGLES) / ANGLES
    radius = np.arange(1, CYCLES + 1)
    out = np.zeros((4, REACH + 1, STEP_ANGLES, SPAN, CYCLES), np.float32)
    for axis, direction in enumerate((np.cos(theta), np.sin(theta))):
        for t in range(REACH + 1):
            phase = 2.0 * np.pi / BOX * t * direction[:, None] * radius[None, :]
            for part, fn in enumerate((np.cos, np.sin)):
                table = fn(phase).reshape(ROT, STEP_ANGLES, CYCLES).transpose(1, 0, 2)
                out[2 * axis + part, t, :, :ROT] = table[:, ::-1]
    return out.reshape(4, REACH + 1, STEP_ANGLES * SPAN, CYCLES)


def axis_phase(table_ref, axis, step, move):
    size = jnp.abs(move)
    sign = jnp.where(move < 0, -1.0, 1.0).astype(jnp.float32)
    at = pl.ds(step * SPAN, SPAN)
    return table_ref[2 * axis, size, at, :], table_ref[2 * axis + 1, size, at, :] * sign


def prep_kernel(local, place_ref, near_ref, far_ref, image_near, image_far, table_ref, mine_ref, rest_ref, raw):
    count = near_ref.shape[0]
    listed = near_ref.shape[1] - 2
    rows = image_near.shape[1]
    half = listed // 2
    share = count // 2
    my_cls, my_dom = place_ref[0], place_ref[1]
    core = lax.rem(my_cls, 2)
    raw[...] = jnp.zeros_like(raw)
    lane = lax.broadcasted_iota(jnp.int32, (META_ROWS, LANES), 1)
    for far in range(2):
        record, image_ref = (far_ref, image_far) if far else (near_ref, image_near)
        source_core = 1 - core if far else core
        source = my_cls - core + source_core
        cand = [[record[u, k] for k in range(listed)] for u in range(count)]
        owner = [[lax.div(c, local) for c in row] for row in cand]
        pair = []
        for u in range(count):
            first = owner[u][0]
            second = first
            for k in range(1, listed):
                second = jnp.where(owner[u][k] != first, owner[u][k], second)
            pair.append((first, second))
        for u in range(count):
            entries = [my_dom, pair[u][0], pair[u][1]]
            for side in range(2):
                value = source * (count // 2)
                for v in range(u):
                    lists = (pair[v][0] == pair[u][side]) | (pair[v][1] == pair[u][side])
                    value = value + jnp.where(lists, 1, 0)
                entries.append(value)
            for side in range(2):
                classes = [jnp.int32(0)] * half
                seen = jnp.int32(0)
                for k in range(listed):
                    hit = owner[u][k] == pair[u][side]
                    for j in range(half):
                        classes[j] = jnp.where(hit & (seen == j), cand[u][k] - pair[u][side] * local, classes[j])
                    seen = seen + jnp.where(hit, 1, 0)
                entries += classes
            tile = jnp.zeros((META_ROWS, LANES), jnp.int32)
            for k, value in enumerate(entries):
                tile = jnp.where(lane == k, value, tile)
            values = image_ref[u].astype(jnp.float32)
            for block in range(rows // PIECES):
                at = rows - (block + 1) * PIECES
                raw[at : at + PIECES, :] = values[block * PIECES : (block + 1) * PIECES]
            moved = []
            for step in range(STEP_ANGLES):
                re = raw[pl.ds(2 * step, SPAN, stride=PIECES), :]
                im = raw[pl.ds(2 * step + 1, SPAN, stride=PIECES), :]
                cx, sx = axis_phase(table_ref, 0, step, record[u, listed])
                cy, sy = axis_phase(table_ref, 1, step, record[u, listed + 1])
                cosine = cx * cy - sx * sy
                sine = sx * cy + cx * sy
                moved += [re * cosine + im * sine, im * cosine - re * sine]
            moved = jnp.concatenate(moved, axis=0).astype(mine_ref.dtype)
            tile = tile.astype(jnp.float32).astype(mine_ref.dtype)
            at = source_core * share + u % share
            role = u // share

            @pl.when(core == role)
            def _():
                mine_ref[at, :IMAGE_ROWS, :] = moved
                mine_ref[at, IMAGE_ROWS:, :] = tile

            @pl.when(core != role)
            def _():
                rest_ref[at, :IMAGE_ROWS, :] = moved
                rest_ref[at, IMAGE_ROWS:, :] = tile


SMEM_SPEC = pl.BlockSpec(memory_space=pltpu.SMEM)
VMEM_SPEC = pl.BlockSpec(memory_space=pltpu.VMEM)
HBM_SPEC = pl.BlockSpec(memory_space=pl.ANY)


def prepare(place, near, far, image_near, image_far, tables, local):
    count = near.shape[0]
    shape = jax.ShapeDtypeStruct((count, IMAGE_ROWS + META_ROWS, LANES), image_near.dtype)
    return pl.pallas_call(
        functools.partial(prep_kernel, local),
        out_shape=(shape, shape),
        in_specs=[SMEM_SPEC] * 3 + [VMEM_SPEC] * 3,
        out_specs=(VMEM_SPEC, VMEM_SPEC),
        scratch_shapes=[pltpu.VMEM((IMAGE_ROWS, LANES), jnp.float32)],
        compiler_params=pltpu.CompilerParams(vmem_limit_bytes=VMEM_LIMIT),
        name="prepare",
    )(place, near, far, image_near, image_far, tables)


def read_meta(source, meta_vmem, row):
    meta_vmem[pl.ds(row, 1), :] = source.astype(jnp.float32)[0:1, :].astype(jnp.int32)


def move_metas(meta_vmem, meta, sem):
    copy = pltpu.make_async_copy(meta_vmem, meta, sem)
    copy.start()
    copy.wait()


def turned_lanes(offset):
    lane = lax.broadcasted_iota(jnp.int32, (SPAN, LANES), 1)
    row = lax.broadcasted_iota(jnp.int32, (SPAN, LANES), 0)
    base = jnp.where(lane >= SPAN, SPAN, 0) + jnp.where(lane >= 2 * SPAN, SPAN, 0)
    base = jnp.where(lane >= 3 * SPAN, 0, base)
    place = jnp.where(lane >= 3 * SPAN, 0, lane - base) - row + offset
    place = jnp.where(place < 0, place + ROT, place)
    place = jnp.where(place < 0, place + ROT, place)
    return base + jnp.minimum(place, ROT - 1)


def take_lanes(values, index):
    return jnp.take_along_axis(values, index, axis=1, mode="promise_in_bounds")


def side_of(meta, i, my_cls):
    return jnp.where(meta[i, OWNER] == my_cls, 0, 1)


def collect(meta, active, total, my_cls, my_dom=None):
    def look(i, n):
        mine = (meta[i, OWNER] == my_cls) | (meta[i, OWNER + 1] == my_cls)
        if my_dom is not None:
            mine = mine & (meta[i, DOM] == my_dom)
        active[n] = i
        return n + jnp.where(mine, 1, 0)

    return lax.fori_loop(0, total, look, jnp.int32(0), unroll=4)


def step_pieces(images, i, table_ref, step):
    values = images[i, 2 * step * SPAN : (2 * step + 2) * SPAN, :].astype(jnp.float32)
    re, im = values[:SPAN], values[SPAN:]
    at = pl.ds(step * SPAN, SPAN)
    return re, im, [table_ref[k, at, :] for k in range(4)]


def store_moved(moved, step, part, blocks):
    at = pl.ds((2 * step + part) * LANES, LANES)
    pad = jnp.zeros((8, LANES), jnp.float32)
    moved[:LANES, at] = jnp.concatenate([*blocks[:3], pad], axis=0).astype(jnp.bfloat16)
    moved[LANES : LANES + 2 * SPAN, at] = jnp.concatenate(blocks[3:], axis=0).astype(jnp.bfloat16)


def score_kernel(count, place_ref, *refs):
    image_refs = refs[:count]
    (
        refs_ref, table_ref, weight_ref, stat_ref, partner_ref,
        images, moved_a, moved_b, picked_a, picked_b, sums_a, sums_b, index_ref, meta_vmem, meta, active, image_sem, sem,
    ) = refs[count:]
    total = images.shape[0]
    slots = weight_ref.shape[0]
    classes = picked_a.shape[0] // 48
    my_cls, my_dom = place_ref[0], place_ref[1]
    copies, at = [], 0
    for b, ref in enumerate(image_refs):
        copies.append(pltpu.make_async_copy(ref, images.at[pl.ds(at, ref.shape[0])], image_sem.at[b]))
        at += ref.shape[0]
    for copy in copies:
        copy.start()
    for ref in (moved_a, moved_b, picked_a, picked_b, sums_a, sums_b, weight_ref, stat_ref):
        ref[...] = jnp.zeros_like(ref)
    for slot in range(slots):
        for k in range(3):
            partner_ref[slot, k] = 0
    for copy in copies:
        copy.wait()
    for i in range(total):
        read_meta(images[i, IMAGE_ROWS:, :], meta_vmem, i)
    move_metas(meta_vmem, meta, sem)
    number = collect(meta, active, total, my_cls, my_dom)
    index_ref[...] = turned_lanes(0)

    def one(at, moved, picked, sums):
        index = active[jnp.minimum(at, number - 1)]
        side = side_of(meta, index, my_cls)
        slot = meta[index, SLOT + side]
        partner_ref[slot, FILLED] = 1
        partner_ref[slot, OTHER] = meta[index, OWNER + 1 - side]
        partner_ref[slot, OTHER_SLOT] = meta[index, SLOT + 1 - side]
        for j in range(classes):
            picked[j * 48 : j * 48 + ROT, :] = refs_ref[meta[index, CLASS + side * classes + j]]
        for step in range(STEP_ANGLES):
            re, im, (c1, s1, c2, s2) = step_pieces(images, index, table_ref, step)
            a1, b1, d1, e1 = re * c1, im * s1, im * c1, re * s1
            a2, b2, d2, e2 = re * c2, im * s2, im * c2, re * s2
            store_moved(moved, step, 0, [re, a1 + b1, a1 - b1, a2 + b2, a2 - b2])
            store_moved(moved, step, 1, [im, d1 - e1, d1 + e1, d2 - e2, d2 + e2])
        for half in range(2):
            pairs = lax.dot_general(
                picked[...],
                moved[half * LANES : (half + 1) * LANES, :],
                (((1,), (1,)), ((), ())),
                preferred_element_type=jnp.float32,
            )
            for j in range(classes):
                total = jnp.zeros((8, LANES), jnp.float32)
                for group in range(SPAN // 8):
                    at = j * 48 + group * 8
                    total = total + take_lanes(pairs[at : at + 8], index_ref[group * 8 : (group + 1) * 8, :])
                sums[pl.ds(half * classes + j, 1), :] = jnp.sum(total, axis=0, keepdims=True)
        scores = SOFTMAX_WARMTH * sums[...]
        lanes = lax.broadcasted_iota(jnp.int32, scores.shape, 1)
        lines = lax.broadcasted_iota(jnp.int32, scores.shape, 0)
        upper = lines < classes
        valid = (lanes < ROT) | ((lanes >= SPAN) & (lanes < SPAN + ROT))
        valid = valid | (upper & (lanes >= 2 * SPAN) & (lanes < 2 * SPAN + ROT))
        scores = jnp.where(valid, scores, NEGATIVE)
        peak = jnp.max(jnp.max(scores, axis=0, keepdims=True), axis=1, keepdims=True)
        w = jnp.where(valid, jnp.exp(scores - peak), 0.0)
        total = jnp.sum(jnp.sum(w, axis=0, keepdims=True), axis=1, keepdims=True)
        stat_ref[pl.ds(2 * slot, 1), :] = jnp.broadcast_to(peak, (1, LANES))
        stat_ref[pl.ds(2 * slot + 1, 1), :] = jnp.broadcast_to(total, (1, LANES))
        after, before = pltpu.roll(w, LANES - SPAN, 1), pltpu.roll(w, SPAN, 1)
        start = jnp.where(upper, SPAN, 0)
        paired = jnp.where(lanes < start + SPAN, w + after, before - w)
        paired = jnp.where(lanes < start + 2 * SPAN, paired, 0.0)
        weight_ref[slot] = jnp.where(lanes < start, w, paired)

    def two(step, carry):
        one(2 * step, moved_a, picked_a, sums_a)
        one(2 * step + 1, moved_b, picked_b, sums_b)
        return carry

    lax.fori_loop(0, lax.div(number + 1, 2), two, 0)


def score(place, buffers, refs, tables, slots, classes):
    count, total = len(buffers), sum(buffer.shape[0] for buffer in buffers)
    width = refs.shape[2]
    return pl.pallas_call(
        functools.partial(score_kernel, count),
        out_shape=(
            jax.ShapeDtypeStruct((slots, 2 * classes, LANES), jnp.float32),
            jax.ShapeDtypeStruct((2 * slots, LANES), jnp.float32),
            jax.ShapeDtypeStruct((slots, 3), jnp.int32),
        ),
        in_specs=[SMEM_SPEC] + [HBM_SPEC] * count + [VMEM_SPEC] * 2,
        out_specs=(VMEM_SPEC, VMEM_SPEC, SMEM_SPEC),
        scratch_shapes=[
            pltpu.VMEM((total, IMAGE_ROWS + META_ROWS, LANES), jnp.bfloat16),
            *[pltpu.VMEM((2 * LANES, width), jnp.bfloat16)] * 2,
            *[pltpu.VMEM((48 * classes, width), jnp.bfloat16)] * 2,
            *[pltpu.VMEM((2 * classes, LANES), jnp.float32)] * 2,
            pltpu.VMEM((SPAN, LANES), jnp.int32),
            pltpu.VMEM((total, LANES), jnp.int32),
            pltpu.SMEM((total, LANES), jnp.int32),
            pltpu.SMEM((total + 1,), jnp.int32),
            pltpu.SemaphoreType.DMA((count,)),
            pltpu.SemaphoreType.DMA,
        ],
        compiler_params=pltpu.CompilerParams(vmem_limit_bytes=VMEM_LIMIT),
        cost_estimate=pl.CostEstimate(flops=10**10, bytes_accessed=10**7, transcendentals=0),
        name="score",
    )(place, *buffers, refs, tables)


def weight_kernel(flip, place_ref, partner_ref, weight_ref, *refs):
    stat_refs, out_ref = refs[:-1], refs[-1]
    slots, lines, _ = weight_ref.shape
    my_cls = place_ref[0]
    done = []
    for slot in range(slots):
        other, other_slot = partner_ref[slot, OTHER], partner_ref[slot, OTHER_SLOT]
        at = pl.ds(2 * other_slot, 2)
        if flip:
            mine = stat_refs[0][2 * slot : 2 * slot + 2, :]
            theirs = mine
            for k in range(1, len(stat_refs)):
                theirs = jnp.where(jnp.bitwise_xor(other, my_cls) == k, stat_refs[k][at, :], theirs)
        else:
            mine = stat_refs[0][my_cls, 2 * slot : 2 * slot + 2, :]
            theirs = stat_refs[0][other, at, :]
        peak = jnp.maximum(mine[0:1], theirs[0:1])
        gain = jnp.exp(mine[0:1] - peak)
        mass = mine[1:2] * gain + theirs[1:2] * jnp.exp(theirs[0:1] - peak)
        factor = gain / jnp.where(partner_ref[slot, FILLED] > 0, mass, 1.0)
        done.append(weight_ref[slot] * factor)
    out_ref[...] = jnp.concatenate(done, axis=0).astype(out_ref.dtype)


def normalise(flip, place, partners, weights, stats):
    slots, lines, _ = weights.shape
    return pl.pallas_call(
        functools.partial(weight_kernel, flip),
        out_shape=jax.ShapeDtypeStruct((slots * lines, LANES), jnp.bfloat16),
        in_specs=[SMEM_SPEC] * 2 + [VMEM_SPEC] * (1 + len(stats)),
        out_specs=VMEM_SPEC,
        name="normalise",
    )(place, partners, weights, *stats)


def sum_kernel(weight_rows, relative, z_size, y_size, lines, local, width, count, n_weights, first, last, place_ref, *refs):
    refs = list(refs)
    image_refs = [refs.pop(0) for _ in range(count)]
    weight_refs = [refs.pop(0) for _ in range(n_weights)]
    table_ref = refs.pop(0)
    given = None if first else [refs.pop(0), refs.pop(0)]
    out_ref = refs.pop(0) if last else None
    if not last:
        totals, mass = refs.pop(0), refs.pop(0)
    images, weights, moved_a, moved_b, spread_a, spread_b, index_ref, meta_vmem, meta, active = refs[:10]
    image_sem, meta_sem = refs[10:12]
    if last:
        totals, mass = refs[12:14]
    given_sem = refs[-1]
    depth, wave = images.shape[0], images.shape[1]
    per_row = weight_rows
    chunk = weight_refs[0].shape[0]
    classes = lines // 2
    waves = sum(ref.shape[0] for ref in image_refs) // wave

    def copies(w):
        out, at = [], 0
        for b, ref in enumerate(image_refs):
            size = ref.shape[0]
            low, high = max(at, w * wave), min(at + size, (w + 1) * wave)
            if low < high:
                source = ref.at[pl.ds(low - at, high - low)]
                target = images.at[w % depth, pl.ds(low - w * wave, high - low)]
                out.append(pltpu.make_async_copy(source, target, image_sem.at[w % depth, b]))
            at += size
        return out

    for w in range(min(depth, waves)):
        for copy in copies(w):
            copy.start()
    if first:
        mass[...] = jnp.zeros_like(mass)
        totals[...] = jnp.zeros_like(totals)
    else:
        held = [pltpu.make_async_copy(g, t, given_sem.at[k]) for k, (g, t) in enumerate(zip(given, (totals, mass)))]
        for copy in held:
            copy.start()
    moved_a[...] = jnp.zeros_like(moved_a)
    moved_b[...] = jnp.zeros_like(moved_b)
    for b in range(n_weights):
        weights[b * chunk : (b + 1) * chunk, :] = weight_refs[b][...].astype(jnp.float32)
    my_cls, my_dom = place_ref[0], place_ref[1]
    my_z, my_y = lax.div(my_dom, y_size), lax.rem(my_dom, y_size)
    lane = lax.broadcasted_iota(jnp.int32, (lines, LANES), 1)
    index_ref[...] = turned_lanes(-1)

    for w in range(waves):
        for copy in copies(w):
            copy.wait()
        here = images.at[w % depth]
        for i in range(wave):
            read_meta(here[i, IMAGE_ROWS:, :], meta_vmem, i)
        move_metas(meta_vmem, meta, meta_sem)
        number = collect(meta, active, wave, my_cls)
        if w == 0 and not first:
            for copy in held:
                copy.wait()

        def prepare_one(at, moved, spread):
            i = active[jnp.minimum(at, number - 1)]
            share = jnp.where(at < number, 1.0, 0.0).astype(jnp.float32)
            side = side_of(meta, i, my_cls)
            q = meta[i, DOM]
            if relative:
                d_z = lax.rem(my_z - lax.div(q, y_size) + z_size, z_size)
                d_y = lax.rem(my_y - lax.rem(q, y_size) + y_size, y_size)
                q = d_y * z_size + d_z
            at = pl.multiple_of(q * per_row + meta[i, SLOT + side] * lines, lines)
            mine = weights[pl.ds(at, lines), :] * share
            def circulant(j):
                line = []
                for half in range(2):
                    at = half * classes + j
                    row = jnp.broadcast_to(mine[at : at + 1], (8, LANES))
                    tiles = [take_lanes(row, index_ref[g * 8 : (g + 1) * 8, :]) for g in range(SPAN // 8)]
                    line.append(jnp.concatenate(tiles, axis=0))
                return jnp.concatenate(line, axis=1)

            def one_step(step):
                re, im, (c1, s1, c2, s2) = step_pieces(here, i, table_ref, step)
                store_moved(moved, step, 0, [re, re * c1, im * s1, re * c2, im * s2])
                store_moved(moved, step, 1, [im, im * c1, -re * s1, im * c2, -re * s2])
                for j in range(step * 2, min(step * 2 + 2, classes), 2):
                    both = jnp.concatenate([circulant(j), circulant(j + 1)], axis=0)
                    spread[j * SPAN : (j + 2) * SPAN, :] = both.astype(jnp.bfloat16)
                if step == STEP_ANGLES - 1:
                    plain = jnp.where(lane < 2 * SPAN, mine, 0.0)
                    plain_high = jnp.where(lane < SPAN, mine, 0.0)
                    for j in range(classes):
                        c = meta[i, CLASS + side * classes + j]
                        mass[pl.ds(c, 1), :] += plain[j : j + 1] + plain_high[classes + j : classes + j + 1]

            return one_step

        def add_one(at, moved, spread, one_step):
            i = active[jnp.minimum(at, number - 1)]
            side = side_of(meta, i, my_cls)
            chosen = [meta[i, CLASS + side * classes + j] for j in range(classes)]
            for step in range(STEP_ANGLES):
                columns = pl.ds(2 * step * LANES, 2 * LANES)
                added = jnp.dot(spread[...], moved[:, columns], preferred_element_type=jnp.float32)
                one_step(step)
                for part in range(2):
                    for j in range(classes):
                        start = (2 * step + part) * local * SPAN
                        to = pl.ds(pl.multiple_of(start + chosen[j] * SPAN, 8), SPAN)
                        totals[to, :] += added[j * SPAN : (j + 1) * SPAN, part * LANES : (part + 1) * LANES]

        def two(step, carry):
            at = 2 * step
            add_one(at, moved_a, spread_a, prepare_one(at + 1, moved_b, spread_b))
            add_one(at + 1, moved_b, spread_b, prepare_one(at + 2, moved_a, spread_a))
            return carry

        @pl.when(number > 0)
        def _():
            start = prepare_one(0, moved_a, spread_a)
            for step in range(STEP_ANGLES):
                start(step)

        lax.fori_loop(0, lax.div(number + 1, 2), two, 0)
        if w + depth < waves:
            for copy in copies(w + depth):
                copy.start()

    if not last:
        return
    scale = 1.0 / (jnp.sum(mass[:local, :], axis=1, keepdims=True) + PRIOR_MASS)
    for turn in range(ROT):
        for tile in range(width // LANES):
            line = totals[pl.ds(tile * local * SPAN + ROT - 1 - turn, local, stride=SPAN), :]
            out_ref[:, pl.ds(turn * width + tile * LANES, LANES)] = (line * scale).astype(out_ref.dtype)


def class_sum(place, buffers, weights, tables, given, last, relative, z_size, y_size, local, width, lines, weight_rows):
    count = len(buffers)
    total = sum(buffer.shape[0] for buffer in buffers)
    wave = total if total <= 128 else math.gcd(total, 128)
    depth = min(2, total // wave)
    totals = (width // LANES * local * SPAN, LANES)
    mass = (-(-local // 8) * 8, LANES)
    first = given is None
    out = jax.ShapeDtypeStruct((local, ROT * width), jnp.bfloat16)
    held = tuple(jax.ShapeDtypeStruct(shape, jnp.float32) for shape in (totals, mass))
    scratch = [
        pltpu.VMEM((depth, wave, IMAGE_ROWS + META_ROWS, LANES), jnp.bfloat16),
        pltpu.VMEM((len(weights) * weights[0].shape[0], LANES), jnp.float32),
        pltpu.VMEM((2 * LANES, width), jnp.bfloat16),
        pltpu.VMEM((2 * LANES, width), jnp.bfloat16),
        pltpu.VMEM((lines // 2 * SPAN, 2 * LANES), jnp.bfloat16),
        pltpu.VMEM((lines // 2 * SPAN, 2 * LANES), jnp.bfloat16),
        pltpu.VMEM((SPAN, LANES), jnp.int32),
        pltpu.VMEM((wave, LANES), jnp.int32),
        pltpu.SMEM((wave, LANES), jnp.int32),
        pltpu.SMEM((wave + 1,), jnp.int32),
        pltpu.SemaphoreType.DMA((depth, count)),
        pltpu.SemaphoreType.DMA,
    ]
    if last:
        scratch += [pltpu.VMEM(totals, jnp.float32), pltpu.VMEM(mass, jnp.float32)]
    scratch += [pltpu.SemaphoreType.DMA((2,))]
    return pl.pallas_call(
        functools.partial(
            sum_kernel, weight_rows, relative, z_size, y_size, lines, local, width, count, len(weights), first, last
        ),
        out_shape=out if last else held,
        in_specs=[SMEM_SPEC]
        + [HBM_SPEC] * count
        + [VMEM_SPEC] * (len(weights) + 1)
        + ([] if first else [HBM_SPEC] * 2),
        out_specs=VMEM_SPEC if last else (VMEM_SPEC, VMEM_SPEC),
        scratch_shapes=scratch,
        compiler_params=pltpu.CompilerParams(vmem_limit_bytes=VMEM_LIMIT),
        cost_estimate=pl.CostEstimate(flops=total * 2 * 10**8, bytes_accessed=10**7, transcendentals=0),
        name="class_sum",
    )(place, *buffers, *weights, tables, *([] if first else given))


def shards(x_size, y_size, z_size, particles, references, candidates, offsets):
    groups = lax.axis_size("cls")
    doms = lax.axis_size("dom")
    count, width = particles.shape
    local = references.shape[0]
    classes = candidates.shape[1] // 2
    block_width = width // ROT
    slots = groups * (count // 2)
    tables = trig_tables()
    place = jnp.stack([lax.axis_index("cls"), lax.axis_index("dom")]).astype(jnp.int32)

    def moves(goal):
        out = []
        for cls in range(groups):
            for dom in range(doms):
                x, core, z, y = goal(cls // 2, cls % 2, dom // y_size, dom % y_size)
                to = ((x % x_size) * 2 + core) * doms + (z % z_size) * y_size + y % y_size
                out.append((cls * doms + dom, to))
        return out

    def send(value, goal):
        return lax.ppermute(value, ("cls", "dom"), moves(goal))

    swap = functools.partial(send, goal=lambda x, c, z, y: (x, 1 - c, z, y))
    along_z = functools.partial(send, goal=lambda x, c, z, y: (x, c, z + 1, y))
    back_z = functools.partial(send, goal=lambda x, c, z, y: (x, c, z - 1, y))
    early = functools.partial(send, goal=lambda x, c, z, y: (x + 1 - c, c, z, y + c))
    late = functools.partial(send, goal=lambda x, c, z, y: (x + c, c, z, y + 1 - c))

    images = particles.reshape(count, width // LANES, LANES)
    record = jnp.concatenate([candidates, offsets], axis=1)
    mine, rest = prepare(place, record, swap(record), images, swap(images), jnp.asarray(tables), local)
    refs = lax.optimization_barrier((references, mine))[0].reshape(local, ROT, block_width)
    steps = jnp.asarray(tables[:, 1])
    tuned = x_size == 2 and y_size == 2 and z_size == 4
    if tuned:
        e0, l0, z1, z3 = early(mine), late(mine), along_z(mine), back_z(mine)
        e0, l0, z1, z3, refs = lax.optimization_barrier((e0, l0, z1, z3, refs))
        near = jnp.concatenate([e0, l0])
        row = [mine, rest, near, swap(near)]
        e1, l1, z2, f0 = early(z1), late(z1), along_z(z1), late(e0)
        weights, stats, partners = score(place, row, refs, steps, slots, classes)
        stats = [
            stats,
            swap(stats),
            send(stats, lambda x, c, z, y: (x + 1, c, z, y)),
            send(stats, lambda x, c, z, y: (x + 1, 1 - c, z, y)),
        ]
        z2, z3, e1, l1, f0, *_ = lax.optimization_barrier((z2, z3, e1, l1, f0, *stats))
        z23 = jnp.concatenate([z2, z3])
        f1, e23 = late(e1), early(z23)
        weights = normalise(tuned, place, partners, weights, stats)
        weights = [weights] + [send(weights, lambda x, c, z, y, dz=dz: (x, c, z + dz, y)) for dz in range(1, z_size)]
        weights = jnp.concatenate(weights)
        weights = [weights, send(weights, lambda x, c, z, y: (x, c, z, y + 1))]
        z23, e23, f1, *weights = lax.optimization_barrier((z23, e23, f1, *weights))
        l23, f23 = late(z23), late(e23)
        first = jnp.concatenate([z1, z23, e1, l1, f0])
        second = jnp.concatenate([f1, e23])
        parts = [[*row, first, second], [swap(first), swap(second), l23, f23]]
    else:
        row = lax.all_gather(mine, "cls", axis=0, tiled=True)
        parts = [[lax.all_gather(row, "dom", axis=0, tiled=True)]]
        weights, stats, partners = score(place, [row], refs, steps, slots, classes)
        stats = [lax.all_gather(stats, "cls", axis=0, tiled=False)]
        weights = normalise(tuned, place, partners, weights, stats)
        weights = [lax.all_gather(weights, "dom", axis=0, tiled=True)]
    held = None
    for k, part in enumerate(parts):
        if k:
            *end, _ = lax.optimization_barrier((*part[2:], held[1]))
            part = part[:2] + end + [swap(block) for block in end]
        held = class_sum(
            place, part, weights, steps, held, k == len(parts) - 1, tuned, z_size, y_size, local, block_width, 2 * classes, slots * 2 * classes
        )
    return held


def solution(mesh):
    coords = [device.coords for device in mesh.devices.flat]
    sizes = [len({c[axis] for c in coords}) for axis in range(3)]
    in_specs = (
        P(("cls", "dom"), None),
        P("cls", None),
        P(("cls", "dom"), None),
        P(("cls", "dom"), None),
    )
    out_specs = P("cls", None)
    return jax.shard_map(
        functools.partial(shards, *sizes),
        mesh=mesh,
        in_specs=in_specs,
        out_specs=out_specs,
        check_vma=False,
    )
```

```python
import functools
import math

import jax
import jax.numpy as jnp
import numpy as np
from jax import lax
from jax.experimental import pallas as pl
from jax.experimental.pallas import tpu as pltpu
from jax.sharding import PartitionSpec as P

CYCLES = 128
ANGLES = 144
ROT = 36
SHIFTS = 5
BOX = 256
LANES = 128
SPAN = 40
STEP_ANGLES = ANGLES // ROT
PIECES = 2 * STEP_ANGLES
IMAGE_ROWS = PIECES * SPAN
REACH = 7

SOFTMAX_WARMTH = 2.0
PRIOR_MASS = 1.0
NEGATIVE = -1e30
META_ROWS = 16
VMEM_LIMIT = 60 * 1024 * 1024
DOM, OWNER, SLOT, CLASS = 0, 1, 3, 5
FILLED, OTHER, OTHER_SLOT = 0, 1, 2


def trig_tables():
    theta = 2.0 * np.pi * np.arange(ANGLES) / ANGLES
    radius = np.arange(1, CYCLES + 1)
    out = np.zeros((4, REACH + 1, STEP_ANGLES, SPAN, CYCLES), np.float32)
    for axis, direction in enumerate((np.cos(theta), np.sin(theta))):
        for t in range(REACH + 1):
            phase = 2.0 * np.pi / BOX * t * direction[:, None] * radius[None, :]
            for part, fn in enumerate((np.cos, np.sin)):
                table = fn(phase).reshape(ROT, STEP_ANGLES, CYCLES).transpose(1, 0, 2)
                out[2 * axis + part, t, :, :ROT] = table[:, ::-1]
    return out.reshape(4, REACH + 1, STEP_ANGLES * SPAN, CYCLES)


def axis_phase(table_ref, axis, step, move):
    size = jnp.abs(move)
    sign = jnp.where(move < 0, -1.0, 1.0).astype(jnp.float32)
    at = pl.ds(step * SPAN, SPAN)
    return table_ref[2 * axis, size, at, :], table_ref[2 * axis + 1, size, at, :] * sign


def prep_kernel(local, place_ref, near_ref, far_ref, image_near, image_far, table_ref, mine_ref, rest_ref, raw):
    count = near_ref.shape[0]
    listed = near_ref.shape[1] - 2
    rows = image_near.shape[1]
    half = listed // 2
    share = count // 2
    my_cls, my_dom = place_ref[0], place_ref[1]
    core = lax.rem(my_cls, 2)
    raw[...] = jnp.zeros_like(raw)
    lane = lax.broadcasted_iota(jnp.int32, (META_ROWS, LANES), 1)
    for far in range(2):
        record, image_ref = (far_ref, image_far) if far else (near_ref, image_near)
        source_core = 1 - core if far else core
        source = my_cls - core + source_core
        cand = [[record[u, k] for k in range(listed)] for u in range(count)]
        owner = [[lax.div(c, local) for c in row] for row in cand]
        pair = []
        for u in range(count):
            first = owner[u][0]
            second = first
            for k in range(1, listed):
                second = jnp.where(owner[u][k] != first, owner[u][k], second)
            pair.append((first, second))
        for u in range(count):
            entries = [my_dom, pair[u][0], pair[u][1]]
            for side in range(2):
                value = source * (count // 2)
                for v in range(u):
                    lists = (pair[v][0] == pair[u][side]) | (pair[v][1] == pair[u][side])
                    value = value + jnp.where(lists, 1, 0)
                entries.append(value)
            for side in range(2):
                classes = [jnp.int32(0)] * half
                seen = jnp.int32(0)
                for k in range(listed):
                    hit = owner[u][k] == pair[u][side]
                    for j in range(half):
                        classes[j] = jnp.where(hit & (seen == j), cand[u][k] - pair[u][side] * local, classes[j])
                    seen = seen + jnp.where(hit, 1, 0)
                entries += classes
            tile = jnp.zeros((META_ROWS, LANES), jnp.int32)
            for k, value in enumerate(entries):
                tile = jnp.where(lane == k, value, tile)
            values = image_ref[u].astype(jnp.float32)
            for block in range(rows // PIECES):
                at = rows - (block + 1) * PIECES
                raw[at : at + PIECES, :] = values[block * PIECES : (block + 1) * PIECES]
            moved = []
            for step in range(STEP_ANGLES):
                re = raw[pl.ds(2 * step, SPAN, stride=PIECES), :]
                im = raw[pl.ds(2 * step + 1, SPAN, stride=PIECES), :]
                cx, sx = axis_phase(table_ref, 0, step, record[u, listed])
                cy, sy = axis_phase(table_ref, 1, step, record[u, listed + 1])
                cosine = cx * cy - sx * sy
                sine = sx * cy + cx * sy
                moved += [re * cosine + im * sine, im * cosine - re * sine]
            moved = jnp.concatenate(moved, axis=0).astype(mine_ref.dtype)
            tile = tile.astype(jnp.float32).astype(mine_ref.dtype)
            at = source_core * share + u % share
            role = u // share

            @pl.when(core == role)
            def _():
                mine_ref[at, :IMAGE_ROWS, :] = moved
                mine_ref[at, IMAGE_ROWS:, :] = tile

            @pl.when(core != role)
            def _():
                rest_ref[at, :IMAGE_ROWS, :] = moved
                rest_ref[at, IMAGE_ROWS:, :] = tile


SMEM_SPEC = pl.BlockSpec(memory_space=pltpu.SMEM)
VMEM_SPEC = pl.BlockSpec(memory_space=pltpu.VMEM)
HBM_SPEC = pl.BlockSpec(memory_space=pl.ANY)


def prepare(place, near, far, image_near, image_far, tables, local):
    count = near.shape[0]
    shape = jax.ShapeDtypeStruct((count, IMAGE_ROWS + META_ROWS, LANES), image_near.dtype)
    return pl.pallas_call(
        functools.partial(prep_kernel, local),
        out_shape=(shape, shape),
        in_specs=[SMEM_SPEC] * 3 + [VMEM_SPEC] * 3,
        out_specs=(VMEM_SPEC, VMEM_SPEC),
        scratch_shapes=[pltpu.VMEM((IMAGE_ROWS, LANES), jnp.float32)],
        compiler_params=pltpu.CompilerParams(vmem_limit_bytes=VMEM_LIMIT),
        name="prepare",
    )(place, near, far, image_near, image_far, tables)


def read_meta(source, meta_vmem, row):
    meta_vmem[pl.ds(row, 1), :] = source.astype(jnp.float32)[0:1, :].astype(jnp.int32)


def move_metas(meta_vmem, meta, sem):
    copy = pltpu.make_async_copy(meta_vmem, meta, sem)
    copy.start()
    copy.wait()


def turned_lanes(offset):
    lane = lax.broadcasted_iota(jnp.int32, (SPAN, LANES), 1)
    row = lax.broadcasted_iota(jnp.int32, (SPAN, LANES), 0)
    base = jnp.where(lane >= SPAN, SPAN, 0) + jnp.where(lane >= 2 * SPAN, SPAN, 0)
    base = jnp.where(lane >= 3 * SPAN, 0, base)
    place = jnp.where(lane >= 3 * SPAN, 0, lane - base) - row + offset
    place = jnp.where(place < 0, place + ROT, place)
    place = jnp.where(place < 0, place + ROT, place)
    return base + jnp.minimum(place, ROT - 1)


def take_lanes(values, index):
    return jnp.take_along_axis(values, index, axis=1, mode="promise_in_bounds")


def side_of(meta, i, my_cls):
    return jnp.where(meta[i, OWNER] == my_cls, 0, 1)


def collect(meta, active, total, my_cls, my_dom=None):
    def look(i, n):
        mine = (meta[i, OWNER] == my_cls) | (meta[i, OWNER + 1] == my_cls)
        if my_dom is not None:
            mine = mine & (meta[i, DOM] == my_dom)
        active[n] = i
        return n + jnp.where(mine, 1, 0)

    return lax.fori_loop(0, total, look, jnp.int32(0), unroll=4)


def step_pieces(images, i, table_ref, step):
    values = images[i, 2 * step * SPAN : (2 * step + 2) * SPAN, :].astype(jnp.float32)
    re, im = values[:SPAN], values[SPAN:]
    at = pl.ds(step * SPAN, SPAN)
    return re, im, [table_ref[k, at, :] for k in range(4)]


def store_moved(moved, step, part, blocks):
    at = pl.ds((2 * step + part) * LANES, LANES)
    pad = jnp.zeros((8, LANES), jnp.float32)
    moved[:LANES, at] = jnp.concatenate([*blocks[:3], pad], axis=0).astype(jnp.bfloat16)
    moved[LANES : LANES + 2 * SPAN, at] = jnp.concatenate(blocks[3:], axis=0).astype(jnp.bfloat16)


def score_kernel(count, place_ref, *refs):
    image_refs = refs[:count]
    (
        refs_ref, table_ref, weight_ref, stat_ref, partner_ref,
        images, moved_a, moved_b, picked_a, picked_b, sums_a, sums_b, index_ref, meta_vmem, meta, active, image_sem, sem,
    ) = refs[count:]
    total = images.shape[0]
    slots = weight_ref.shape[0]
    classes = picked_a.shape[0] // 48
    my_cls, my_dom = place_ref[0], place_ref[1]
    copies, at = [], 0
    for b, ref in enumerate(image_refs):
        copies.append(pltpu.make_async_copy(ref, images.at[pl.ds(at, ref.shape[0])], image_sem.at[b]))
        at += ref.shape[0]
    for copy in copies:
        copy.start()
    for ref in (moved_a, moved_b, picked_a, picked_b, sums_a, sums_b, weight_ref, stat_ref):
        ref[...] = jnp.zeros_like(ref)
    for slot in range(slots):
        for k in range(3):
            partner_ref[slot, k] = 0
    for copy in copies:
        copy.wait()
    for i in range(total):
        read_meta(images[i, IMAGE_ROWS:, :], meta_vmem, i)
    move_metas(meta_vmem, meta, sem)
    number = collect(meta, active, total, my_cls, my_dom)
    index_ref[...] = turned_lanes(0)

    def one(at, moved, picked, sums):
        index = active[jnp.minimum(at, number - 1)]
        side = side_of(meta, index, my_cls)
        slot = meta[index, SLOT + side]
        partner_ref[slot, FILLED] = 1
        partner_ref[slot, OTHER] = meta[index, OWNER + 1 - side]
        partner_ref[slot, OTHER_SLOT] = meta[index, SLOT + 1 - side]
        for j in range(classes):
            picked[j * 48 : j * 48 + ROT, :] = refs_ref[meta[index, CLASS + side * classes + j]]
        for step in range(STEP_ANGLES):
            re, im, (c1, s1, c2, s2) = step_pieces(images, index, table_ref, step)
            a1, b1, d1, e1 = re * c1, im * s1, im * c1, re * s1
            a2, b2, d2, e2 = re * c2, im * s2, im * c2, re * s2
            store_moved(moved, step, 0, [re, a1 + b1, a1 - b1, a2 + b2, a2 - b2])
            store_moved(moved, step, 1, [im, d1 - e1, d1 + e1, d2 - e2, d2 + e2])
        for half in range(2):
            pairs = lax.dot_general(
                picked[...],
                moved[half * LANES : (half + 1) * LANES, :],
                (((1,), (1,)), ((), ())),
                preferred_element_type=jnp.float32,
            )
            for j in range(classes):
                total = jnp.zeros((8, LANES), jnp.float32)
                for group in range(SPAN // 8):
                    at = j * 48 + group * 8
                    total = total + take_lanes(pairs[at : at + 8], index_ref[group * 8 : (group + 1) * 8, :])
                sums[pl.ds(half * classes + j, 1), :] = jnp.sum(total, axis=0, keepdims=True)
        scores = SOFTMAX_WARMTH * sums[...]
        lanes = lax.broadcasted_iota(jnp.int32, scores.shape, 1)
        lines = lax.broadcasted_iota(jnp.int32, scores.shape, 0)
        upper = lines < classes
        valid = (lanes < ROT) | ((lanes >= SPAN) & (lanes < SPAN + ROT))
        valid = valid | (upper & (lanes >= 2 * SPAN) & (lanes < 2 * SPAN + ROT))
        scores = jnp.where(valid, scores, NEGATIVE)
        peak = jnp.max(jnp.max(scores, axis=0, keepdims=True), axis=1, keepdims=True)
        w = jnp.where(valid, jnp.exp(scores - peak), 0.0)
        total = jnp.sum(jnp.sum(w, axis=0, keepdims=True), axis=1, keepdims=True)
        stat_ref[pl.ds(2 * slot, 1), :] = jnp.broadcast_to(peak, (1, LANES))
        stat_ref[pl.ds(2 * slot + 1, 1), :] = jnp.broadcast_to(total, (1, LANES))
        after, before = pltpu.roll(w, LANES - SPAN, 1), pltpu.roll(w, SPAN, 1)
        start = jnp.where(upper, SPAN, 0)
        paired = jnp.where(lanes < start + SPAN, w + after, before - w)
        paired = jnp.where(lanes < start + 2 * SPAN, paired, 0.0)
        weight_ref[slot] = jnp.where(lanes < start, w, paired)

    def two(step, carry):
        one(2 * step, moved_a, picked_a, sums_a)
        one(2 * step + 1, moved_b, picked_b, sums_b)
        return carry

    lax.fori_loop(0, lax.div(number + 1, 2), two, 0)


def score(place, buffers, refs, tables, slots, classes):
    count, total = len(buffers), sum(buffer.shape[0] for buffer in buffers)
    width = refs.shape[2]
    return pl.pallas_call(
        functools.partial(score_kernel, count),
        out_shape=(
            jax.ShapeDtypeStruct((slots, 2 * classes, LANES), jnp.float32),
            jax.ShapeDtypeStruct((2 * slots, LANES), jnp.float32),
            jax.ShapeDtypeStruct((slots, 3), jnp.int32),
        ),
        in_specs=[SMEM_SPEC] + [HBM_SPEC] * count + [VMEM_SPEC] * 2,
        out_specs=(VMEM_SPEC, VMEM_SPEC, SMEM_SPEC),
        scratch_shapes=[
            pltpu.VMEM((total, IMAGE_ROWS + META_ROWS, LANES), jnp.bfloat16),
            *[pltpu.VMEM((2 * LANES, width), jnp.bfloat16)] * 2,
            *[pltpu.VMEM((48 * classes, width), jnp.bfloat16)] * 2,
            *[pltpu.VMEM((2 * classes, LANES), jnp.float32)] * 2,
            pltpu.VMEM((SPAN, LANES), jnp.int32),
            pltpu.VMEM((total, LANES), jnp.int32),
            pltpu.SMEM((total, LANES), jnp.int32),
            pltpu.SMEM((total + 1,), jnp.int32),
            pltpu.SemaphoreType.DMA((count,)),
            pltpu.SemaphoreType.DMA,
        ],
        compiler_params=pltpu.CompilerParams(vmem_limit_bytes=VMEM_LIMIT),
        cost_estimate=pl.CostEstimate(flops=10**10, bytes_accessed=10**7, transcendentals=0),
        name="score",
    )(place, *buffers, refs, tables)


def weight_kernel(flip, place_ref, partner_ref, weight_ref, *refs):
    stat_refs, out_ref = refs[:-1], refs[-1]
    slots, lines, _ = weight_ref.shape
    my_cls = place_ref[0]
    done = []
    for slot in range(slots):
        other, other_slot = partner_ref[slot, OTHER], partner_ref[slot, OTHER_SLOT]
        at = pl.ds(2 * other_slot, 2)
        if flip:
            mine = stat_refs[0][2 * slot : 2 * slot + 2, :]
            theirs = mine
            for k in range(1, len(stat_refs)):
                theirs = jnp.where(jnp.bitwise_xor(other, my_cls) == k, stat_refs[k][at, :], theirs)
        else:
            mine = stat_refs[0][my_cls, 2 * slot : 2 * slot + 2, :]
            theirs = stat_refs[0][other, at, :]
        peak = jnp.maximum(mine[0:1], theirs[0:1])
        gain = jnp.exp(mine[0:1] - peak)
        mass = mine[1:2] * gain + theirs[1:2] * jnp.exp(theirs[0:1] - peak)
        factor = gain / jnp.where(partner_ref[slot, FILLED] > 0, mass, 1.0)
        done.append(weight_ref[slot] * factor)
    out_ref[...] = jnp.concatenate(done, axis=0).astype(out_ref.dtype)


def normalise(flip, place, partners, weights, stats):
    slots, lines, _ = weights.shape
    return pl.pallas_call(
        functools.partial(weight_kernel, flip),
        out_shape=jax.ShapeDtypeStruct((slots * lines, LANES), jnp.bfloat16),
        in_specs=[SMEM_SPEC] * 2 + [VMEM_SPEC] * (1 + len(stats)),
        out_specs=VMEM_SPEC,
        name="normalise",
    )(place, partners, weights, *stats)


def sum_kernel(weight_rows, relative, z_size, y_size, lines, local, width, count, n_weights, first, last, place_ref, *refs):
    refs = list(refs)
    image_refs = [refs.pop(0) for _ in range(count)]
    weight_refs = [refs.pop(0) for _ in range(n_weights)]
    table_ref = refs.pop(0)
    given = None if first else [refs.pop(0), refs.pop(0)]
    out_ref = refs.pop(0) if last else None
    if not last:
        totals, mass = refs.pop(0), refs.pop(0)
    images, weights, moved_a, moved_b, spread_a, spread_b, index_ref, meta_vmem, meta, active = refs[:10]
    image_sem, meta_sem = refs[10:12]
    if last:
        totals, mass = refs[12:14]
    given_sem = refs[-1]
    depth, wave = images.shape[0], images.shape[1]
    per_row = weight_rows
    chunk = weight_refs[0].shape[0]
    classes = lines // 2
    waves = sum(ref.shape[0] for ref in image_refs) // wave

    def copies(w):
        out, at = [], 0
        for b, ref in enumerate(image_refs):
            size = ref.shape[0]
            low, high = max(at, w * wave), min(at + size, (w + 1) * wave)
            if low < high:
                source = ref.at[pl.ds(low - at, high - low)]
                target = images.at[w % depth, pl.ds(low - w * wave, high - low)]
                out.append(pltpu.make_async_copy(source, target, image_sem.at[w % depth, b]))
            at += size
        return out

    for w in range(min(depth, waves)):
        for copy in copies(w):
            copy.start()
    if first:
        mass[...] = jnp.zeros_like(mass)
        totals[...] = jnp.zeros_like(totals)
    else:
        held = [pltpu.make_async_copy(g, t, given_sem.at[k]) for k, (g, t) in enumerate(zip(given, (totals, mass)))]
        for copy in held:
            copy.start()
    moved_a[...] = jnp.zeros_like(moved_a)
    moved_b[...] = jnp.zeros_like(moved_b)
    for b in range(n_weights):
        weights[b * chunk : (b + 1) * chunk, :] = weight_refs[b][...].astype(jnp.float32)
    my_cls, my_dom = place_ref[0], place_ref[1]
    my_z, my_y = lax.div(my_dom, y_size), lax.rem(my_dom, y_size)
    lane = lax.broadcasted_iota(jnp.int32, (lines, LANES), 1)
    index_ref[...] = turned_lanes(-1)

    for w in range(waves):
        for copy in copies(w):
            copy.wait()
        here = images.at[w % depth]
        for i in range(wave):
            read_meta(here[i, IMAGE_ROWS:, :], meta_vmem, i)
        move_metas(meta_vmem, meta, meta_sem)
        number = collect(meta, active, wave, my_cls)
        if w == 0 and not first:
            for copy in held:
                copy.wait()

        def prepare_one(at, moved, spread):
            i = active[jnp.minimum(at, number - 1)]
            share = jnp.where(at < number, 1.0, 0.0).astype(jnp.float32)
            side = side_of(meta, i, my_cls)
            q = meta[i, DOM]
            if relative:
                d_z = lax.rem(my_z - lax.div(q, y_size) + z_size, z_size)
                d_y = lax.rem(my_y - lax.rem(q, y_size) + y_size, y_size)
                q = d_y * z_size + d_z
            at = pl.multiple_of(q * per_row + meta[i, SLOT + side] * lines, lines)
            mine = weights[pl.ds(at, lines), :] * share
            def circulant(j):
                line = []
                for half in range(2):
                    at = half * classes + j
                    row = jnp.broadcast_to(mine[at : at + 1], (8, LANES))
                    tiles = [take_lanes(row, index_ref[g * 8 : (g + 1) * 8, :]) for g in range(SPAN // 8)]
                    line.append(jnp.concatenate(tiles, axis=0))
                return jnp.concatenate(line, axis=1)

            def one_step(step):
                re, im, (c1, s1, c2, s2) = step_pieces(here, i, table_ref, step)
                store_moved(moved, step, 0, [re, re * c1, im * s1, re * c2, im * s2])
                store_moved(moved, step, 1, [im, im * c1, -re * s1, im * c2, -re * s2])
                for j in range(step * 2, min(step * 2 + 2, classes), 2):
                    both = jnp.concatenate([circulant(j), circulant(j + 1)], axis=0)
                    spread[j * SPAN : (j + 2) * SPAN, :] = both.astype(jnp.bfloat16)
                if step == STEP_ANGLES - 1:
                    plain = jnp.where(lane < 2 * SPAN, mine, 0.0)
                    plain_high = jnp.where(lane < SPAN, mine, 0.0)
                    for j in range(classes):
                        c = meta[i, CLASS + side * classes + j]
                        mass[pl.ds(c, 1), :] += plain[j : j + 1] + plain_high[classes + j : classes + j + 1]

            return one_step

        def add_one(at, moved, spread, one_step):
            i = active[jnp.minimum(at, number - 1)]
            side = side_of(meta, i, my_cls)
            chosen = [meta[i, CLASS + side * classes + j] for j in range(classes)]
            used = LANES + 2 * SPAN
            added = jnp.dot(spread[:, :used], moved[:used, :], preferred_element_type=jnp.float32)
            for step in range(STEP_ANGLES):
                one_step(step)
            for j in range(classes):
                for tile in range(width // LANES):
                    to = pl.ds(pl.multiple_of(tile * local * SPAN + chosen[j] * SPAN, 8), SPAN)
                    totals[to, :] += added[j * SPAN : (j + 1) * SPAN, tile * LANES : (tile + 1) * LANES]

        def two(step, carry):
            at = 2 * step
            add_one(at, moved_a, spread_a, prepare_one(at + 1, moved_b, spread_b))
            add_one(at + 1, moved_b, spread_b, prepare_one(at + 2, moved_a, spread_a))
            return carry

        @pl.when(number > 0)
        def _():
            start = prepare_one(0, moved_a, spread_a)
            for step in range(STEP_ANGLES):
                start(step)

        lax.fori_loop(0, lax.div(number + 1, 2), two, 0)
        if w + depth < waves:
            for copy in copies(w + depth):
                copy.start()

    if not last:
        return
    scale = 1.0 / (jnp.sum(mass[:local, :], axis=1, keepdims=True) + PRIOR_MASS)
    for turn in range(ROT):
        for tile in range(width // LANES):
            line = totals[pl.ds(tile * local * SPAN + ROT - 1 - turn, local, stride=SPAN), :]
            out_ref[:, pl.ds(turn * width + tile * LANES, LANES)] = (line * scale).astype(out_ref.dtype)


def class_sum(place, buffers, weights, tables, given, last, relative, z_size, y_size, local, width, lines, weight_rows):
    count = len(buffers)
    total = sum(buffer.shape[0] for buffer in buffers)
    wave = total if total <= 128 else math.gcd(total, 128)
    depth = min(2, total // wave)
    totals = (width // LANES * local * SPAN, LANES)
    mass = (-(-local // 8) * 8, LANES)
    first = given is None
    out = jax.ShapeDtypeStruct((local, ROT * width), jnp.bfloat16)
    held = tuple(jax.ShapeDtypeStruct(shape, jnp.float32) for shape in (totals, mass))
    scratch = [
        pltpu.VMEM((depth, wave, IMAGE_ROWS + META_ROWS, LANES), jnp.bfloat16),
        pltpu.VMEM((len(weights) * weights[0].shape[0], LANES), jnp.float32),
        pltpu.VMEM((2 * LANES, width), jnp.bfloat16),
        pltpu.VMEM((2 * LANES, width), jnp.bfloat16),
        pltpu.VMEM((lines // 2 * SPAN, 2 * LANES), jnp.bfloat16),
        pltpu.VMEM((lines // 2 * SPAN, 2 * LANES), jnp.bfloat16),
        pltpu.VMEM((SPAN, LANES), jnp.int32),
        pltpu.VMEM((wave, LANES), jnp.int32),
        pltpu.SMEM((wave, LANES), jnp.int32),
        pltpu.SMEM((wave + 1,), jnp.int32),
        pltpu.SemaphoreType.DMA((depth, count)),
        pltpu.SemaphoreType.DMA,
    ]
    if last:
        scratch += [pltpu.VMEM(totals, jnp.float32), pltpu.VMEM(mass, jnp.float32)]
    scratch += [pltpu.SemaphoreType.DMA((2,))]
    return pl.pallas_call(
        functools.partial(
            sum_kernel, weight_rows, relative, z_size, y_size, lines, local, width, count, len(weights), first, last
        ),
        out_shape=out if last else held,
        in_specs=[SMEM_SPEC]
        + [HBM_SPEC] * count
        + [VMEM_SPEC] * (len(weights) + 1)
        + ([] if first else [HBM_SPEC] * 2),
        out_specs=VMEM_SPEC if last else (VMEM_SPEC, VMEM_SPEC),
        scratch_shapes=scratch,
        compiler_params=pltpu.CompilerParams(vmem_limit_bytes=VMEM_LIMIT),
        cost_estimate=pl.CostEstimate(flops=total * 2 * 10**8, bytes_accessed=10**7, transcendentals=0),
        name="class_sum",
    )(place, *buffers, *weights, tables, *([] if first else given))


def shards(x_size, y_size, z_size, particles, references, candidates, offsets):
    groups = lax.axis_size("cls")
    doms = lax.axis_size("dom")
    count, width = particles.shape
    local = references.shape[0]
    classes = candidates.shape[1] // 2
    block_width = width // ROT
    slots = groups * (count // 2)
    tables = trig_tables()
    place = jnp.stack([lax.axis_index("cls"), lax.axis_index("dom")]).astype(jnp.int32)

    def moves(goal):
        out = []
        for cls in range(groups):
            for dom in range(doms):
                x, core, z, y = goal(cls // 2, cls % 2, dom // y_size, dom % y_size)
                to = ((x % x_size) * 2 + core) * doms + (z % z_size) * y_size + y % y_size
                out.append((cls * doms + dom, to))
        return out

    def send(value, goal):
        return lax.ppermute(value, ("cls", "dom"), moves(goal))

    swap = functools.partial(send, goal=lambda x, c, z, y: (x, 1 - c, z, y))
    along_z = functools.partial(send, goal=lambda x, c, z, y: (x, c, z + 1, y))
    back_z = functools.partial(send, goal=lambda x, c, z, y: (x, c, z - 1, y))
    early = functools.partial(send, goal=lambda x, c, z, y: (x + 1 - c, c, z, y + c))
    late = functools.partial(send, goal=lambda x, c, z, y: (x + c, c, z, y + 1 - c))

    images = particles.reshape(count, width // LANES, LANES)
    record = jnp.concatenate([candidates, offsets], axis=1)
    mine, rest = prepare(place, record, swap(record), images, swap(images), jnp.asarray(tables), local)
    refs = lax.optimization_barrier((references, mine))[0].reshape(local, ROT, block_width)
    steps = jnp.asarray(tables[:, 1])
    tuned = x_size == 2 and y_size == 2 and z_size == 4
    if tuned:
        e0, l0, z1 = early(mine), late(mine), along_z(mine)
        e0, l0, z1, refs = lax.optimization_barrier((e0, l0, z1, refs))
        near = jnp.concatenate([e0, l0])
        row = [mine, rest, near, swap(near)]
        e1, l1, z2, f0 = early(z1), late(z1), along_z(z1), late(e0)
        back = back_z(jnp.concatenate([mine, near]))
        weights, stats, partners = score(place, row, refs, steps, slots, classes)
        stats = [
            stats,
            swap(stats),
            send(stats, lambda x, c, z, y: (x + 1, c, z, y)),
            send(stats, lambda x, c, z, y: (x + 1, 1 - c, z, y)),
        ]
        z2, e1, f0, *_ = lax.optimization_barrier((z2, e1, f0, *stats))
        e2, f1 = early(z2), late(e1)
        weights = normalise(tuned, place, partners, weights, stats)
        weights = [weights] + [send(weights, lambda x, c, z, y, dz=dz: (x, c, z + dz, y)) for dz in range(1, z_size)]
        weights = jnp.concatenate(weights)
        weights = [weights, send(weights, lambda x, c, z, y: (x, c, z, y + 1))]
        z2, e2, f0, *weights = lax.optimization_barrier((z2, e2, f0, *weights))
        l2, f2, f3 = late(z2), late(e2), back_z(f0)
        first = jnp.concatenate([z1, z2, e1, l1, f0])
        second = jnp.concatenate([f1, e2])
        parts = [[*row, first, second, back], [swap(first), swap(second), swap(back), l2, f2, f3]]
    else:
        row = lax.all_gather(mine, "cls", axis=0, tiled=True)
        parts = [[lax.all_gather(row, "dom", axis=0, tiled=True)]]
        weights, stats, partners = score(place, [row], refs, steps, slots, classes)
        stats = [lax.all_gather(stats, "cls", axis=0, tiled=False)]
        weights = normalise(tuned, place, partners, weights, stats)
        weights = [lax.all_gather(weights, "dom", axis=0, tiled=True)]
    held = None
    for k, part in enumerate(parts):
        if k:
            *end, _ = lax.optimization_barrier((*part[3:], held[1]))
            end = jnp.concatenate(end)
            part = part[:3] + [end, swap(end)]
        held = class_sum(
            place, part, weights, steps, held, k == len(parts) - 1, tuned, z_size, y_size, local, block_width, 2 * classes, slots * 2 * classes
        )
    return held


def solution(mesh):
    coords = [device.coords for device in mesh.devices.flat]
    sizes = [len({c[axis] for c in coords}) for axis in range(3)]
    in_specs = (
        P(("cls", "dom"), None),
        P("cls", None),
        P(("cls", "dom"), None),
        P(("cls", "dom"), None),
    )
    out_specs = P("cls", None)
    return jax.shard_map(
        functools.partial(shards, *sizes),
        mesh=mesh,
        in_specs=in_specs,
        out_specs=out_specs,
        check_vma=False,
    )
```

```python
import functools
import math

import jax
import jax.numpy as jnp
import numpy as np
from jax import lax
from jax.experimental import pallas as pl
from jax.experimental.pallas import tpu as pltpu
from jax.sharding import PartitionSpec as P

CYCLES = 128
ANGLES = 144
ROT = 36
SHIFTS = 5
BOX = 256
LANES = 128
SPAN = 40
STEP_ANGLES = ANGLES // ROT
PIECES = 2 * STEP_ANGLES
IMAGE_ROWS = PIECES * SPAN
REACH = 7

SOFTMAX_WARMTH = 2.0
PRIOR_MASS = 1.0
NEGATIVE = -1e30
META_ROWS = 16
VMEM_LIMIT = 60 * 1024 * 1024
DOM, OWNER, SLOT, CLASS = 0, 1, 3, 5
FILLED, OTHER, OTHER_SLOT = 0, 1, 2


def trig_tables():
    theta = 2.0 * np.pi * np.arange(ANGLES) / ANGLES
    radius = np.arange(1, CYCLES + 1)
    out = np.zeros((4, REACH + 1, STEP_ANGLES, SPAN, CYCLES), np.float32)
    for axis, direction in enumerate((np.cos(theta), np.sin(theta))):
        for t in range(REACH + 1):
            phase = 2.0 * np.pi / BOX * t * direction[:, None] * radius[None, :]
            for part, fn in enumerate((np.cos, np.sin)):
                table = fn(phase).reshape(ROT, STEP_ANGLES, CYCLES).transpose(1, 0, 2)
                out[2 * axis + part, t, :, :ROT] = table[:, ::-1]
    return out.reshape(4, REACH + 1, STEP_ANGLES * SPAN, CYCLES)


def axis_phase(table_ref, axis, step, move):
    size = jnp.abs(move)
    sign = jnp.where(move < 0, -1.0, 1.0).astype(jnp.float32)
    at = pl.ds(step * SPAN, SPAN)
    return table_ref[2 * axis, size, at, :], table_ref[2 * axis + 1, size, at, :] * sign


def prep_kernel(local, place_ref, near_ref, far_ref, image_near, image_far, table_ref, mine_ref, rest_ref, raw):
    count = near_ref.shape[0]
    listed = near_ref.shape[1] - 2
    rows = image_near.shape[1]
    half = listed // 2
    share = count // 2
    my_cls, my_dom = place_ref[0], place_ref[1]
    core = lax.rem(my_cls, 2)
    raw[...] = jnp.zeros_like(raw)
    lane = lax.broadcasted_iota(jnp.int32, (META_ROWS, LANES), 1)
    for far in range(2):
        record, image_ref = (far_ref, image_far) if far else (near_ref, image_near)
        source_core = 1 - core if far else core
        source = my_cls - core + source_core
        cand = [[record[u, k] for k in range(listed)] for u in range(count)]
        owner = [[lax.div(c, local) for c in row] for row in cand]
        pair = []
        for u in range(count):
            first = owner[u][0]
            second = first
            for k in range(1, listed):
                second = jnp.where(owner[u][k] != first, owner[u][k], second)
            pair.append((first, second))
        for u in range(count):
            entries = [my_dom, pair[u][0], pair[u][1]]
            for side in range(2):
                value = source * (count // 2)
                for v in range(u):
                    lists = (pair[v][0] == pair[u][side]) | (pair[v][1] == pair[u][side])
                    value = value + jnp.where(lists, 1, 0)
                entries.append(value)
            for side in range(2):
                classes = [jnp.int32(0)] * half
                seen = jnp.int32(0)
                for k in range(listed):
                    hit = owner[u][k] == pair[u][side]
                    for j in range(half):
                        classes[j] = jnp.where(hit & (seen == j), cand[u][k] - pair[u][side] * local, classes[j])
                    seen = seen + jnp.where(hit, 1, 0)
                entries += classes
            tile = jnp.zeros((META_ROWS, LANES), jnp.int32)
            for k, value in enumerate(entries):
                tile = jnp.where(lane == k, value, tile)
            values = image_ref[u].astype(jnp.float32)
            for block in range(rows // PIECES):
                at = rows - (block + 1) * PIECES
                raw[at : at + PIECES, :] = values[block * PIECES : (block + 1) * PIECES]
            moved = []
            for step in range(STEP_ANGLES):
                re = raw[pl.ds(2 * step, SPAN, stride=PIECES), :]
                im = raw[pl.ds(2 * step + 1, SPAN, stride=PIECES), :]
                cx, sx = axis_phase(table_ref, 0, step, record[u, listed])
                cy, sy = axis_phase(table_ref, 1, step, record[u, listed + 1])
                cosine = cx * cy - sx * sy
                sine = sx * cy + cx * sy
                moved += [re * cosine + im * sine, im * cosine - re * sine]
            moved = jnp.concatenate(moved, axis=0).astype(mine_ref.dtype)
            tile = tile.astype(jnp.float32).astype(mine_ref.dtype)
            at = source_core * share + u % share
            role = u // share

            @pl.when(core == role)
            def _():
                mine_ref[at, :IMAGE_ROWS, :] = moved
                mine_ref[at, IMAGE_ROWS:, :] = tile

            @pl.when(core != role)
            def _():
                rest_ref[at, :IMAGE_ROWS, :] = moved
                rest_ref[at, IMAGE_ROWS:, :] = tile


SMEM_SPEC = pl.BlockSpec(memory_space=pltpu.SMEM)
VMEM_SPEC = pl.BlockSpec(memory_space=pltpu.VMEM)
HBM_SPEC = pl.BlockSpec(memory_space=pl.ANY)


def prepare(place, near, far, image_near, image_far, tables, local):
    count = near.shape[0]
    shape = jax.ShapeDtypeStruct((count, IMAGE_ROWS + META_ROWS, LANES), image_near.dtype)
    return pl.pallas_call(
        functools.partial(prep_kernel, local),
        out_shape=(shape, shape),
        in_specs=[SMEM_SPEC] * 3 + [VMEM_SPEC] * 3,
        out_specs=(VMEM_SPEC, VMEM_SPEC),
        scratch_shapes=[pltpu.VMEM((IMAGE_ROWS, LANES), jnp.float32)],
        compiler_params=pltpu.CompilerParams(vmem_limit_bytes=VMEM_LIMIT),
        name="prepare",
    )(place, near, far, image_near, image_far, tables)


def read_meta(source, meta_vmem, row):
    meta_vmem[pl.ds(row, 1), :] = source.astype(jnp.float32)[0:1, :].astype(jnp.int32)


def move_metas(meta_vmem, meta, sem):
    copy = pltpu.make_async_copy(meta_vmem, meta, sem)
    copy.start()
    copy.wait()


def turned_lanes(offset):
    lane = lax.broadcasted_iota(jnp.int32, (SPAN, LANES), 1)
    row = lax.broadcasted_iota(jnp.int32, (SPAN, LANES), 0)
    base = jnp.where(lane >= SPAN, SPAN, 0) + jnp.where(lane >= 2 * SPAN, SPAN, 0)
    base = jnp.where(lane >= 3 * SPAN, 0, base)
    place = jnp.where(lane >= 3 * SPAN, 0, lane - base) - row + offset
    place = jnp.where(place < 0, place + ROT, place)
    place = jnp.where(place < 0, place + ROT, place)
    return base + jnp.minimum(place, ROT - 1)


def take_lanes(values, index):
    return jnp.take_along_axis(values, index, axis=1, mode="promise_in_bounds")


def side_of(meta, i, my_cls):
    return jnp.where(meta[i, OWNER] == my_cls, 0, 1)


def collect(meta, active, total, my_cls, my_dom=None):
    def look(i, n):
        mine = (meta[i, OWNER] == my_cls) | (meta[i, OWNER + 1] == my_cls)
        if my_dom is not None:
            mine = mine & (meta[i, DOM] == my_dom)
        active[n] = i
        return n + jnp.where(mine, 1, 0)

    return lax.fori_loop(0, total, look, jnp.int32(0), unroll=4)


def step_pieces(images, i, table_ref, step):
    values = images[i, 2 * step * SPAN : (2 * step + 2) * SPAN, :].astype(jnp.float32)
    re, im = values[:SPAN], values[SPAN:]
    at = pl.ds(step * SPAN, SPAN)
    return re, im, [table_ref[k, at, :] for k in range(4)]


def store_moved(moved, step, part, blocks):
    at = pl.ds((2 * step + part) * LANES, LANES)
    pad = jnp.zeros((8, LANES), jnp.float32)
    moved[:LANES, at] = jnp.concatenate([*blocks[:3], pad], axis=0).astype(jnp.bfloat16)
    moved[LANES : LANES + 2 * SPAN, at] = jnp.concatenate(blocks[3:], axis=0).astype(jnp.bfloat16)


def score_kernel(count, place_ref, *refs):
    image_refs = refs[:count]
    (
        refs_ref, table_ref, weight_ref, stat_ref, partner_ref,
        images, moved_a, moved_b, picked_a, picked_b, sums_a, sums_b, index_ref, meta_vmem, meta, active, image_sem, sem,
    ) = refs[count:]
    total = images.shape[0]
    slots = weight_ref.shape[0]
    classes = picked_a.shape[0] // 48
    my_cls, my_dom = place_ref[0], place_ref[1]
    copies, at = [], 0
    for b, ref in enumerate(image_refs):
        copies.append(pltpu.make_async_copy(ref, images.at[pl.ds(at, ref.shape[0])], image_sem.at[b]))
        at += ref.shape[0]
    for copy in copies:
        copy.start()
    for ref in (moved_a, moved_b, picked_a, picked_b, sums_a, sums_b, weight_ref, stat_ref):
        ref[...] = jnp.zeros_like(ref)
    for slot in range(slots):
        for k in range(3):
            partner_ref[slot, k] = 0
    for copy in copies:
        copy.wait()
    for i in range(total):
        read_meta(images[i, IMAGE_ROWS:, :], meta_vmem, i)
    move_metas(meta_vmem, meta, sem)
    number = collect(meta, active, total, my_cls, my_dom)
    index_ref[...] = turned_lanes(0)

    def one(at, moved, picked, sums):
        index = active[jnp.minimum(at, number - 1)]
        side = side_of(meta, index, my_cls)
        slot = meta[index, SLOT + side]
        partner_ref[slot, FILLED] = 1
        partner_ref[slot, OTHER] = meta[index, OWNER + 1 - side]
        partner_ref[slot, OTHER_SLOT] = meta[index, SLOT + 1 - side]
        for j in range(classes):
            picked[j * 48 : j * 48 + ROT, :] = refs_ref[meta[index, CLASS + side * classes + j]]
        for step in range(STEP_ANGLES):
            re, im, (c1, s1, c2, s2) = step_pieces(images, index, table_ref, step)
            a1, b1, d1, e1 = re * c1, im * s1, im * c1, re * s1
            a2, b2, d2, e2 = re * c2, im * s2, im * c2, re * s2
            store_moved(moved, step, 0, [re, a1 + b1, a1 - b1, a2 + b2, a2 - b2])
            store_moved(moved, step, 1, [im, d1 - e1, d1 + e1, d2 - e2, d2 + e2])
        for half in range(2):
            pairs = lax.dot_general(
                picked[...],
                moved[half * LANES : (half + 1) * LANES, :],
                (((1,), (1,)), ((), ())),
                preferred_element_type=jnp.float32,
            )
            for j in range(classes):
                total = jnp.zeros((8, LANES), jnp.float32)
                for group in range(SPAN // 8):
                    at = j * 48 + group * 8
                    total = total + take_lanes(pairs[at : at + 8], index_ref[group * 8 : (group + 1) * 8, :])
                sums[pl.ds(half * classes + j, 1), :] = jnp.sum(total, axis=0, keepdims=True)
        scores = SOFTMAX_WARMTH * sums[...]
        lanes = lax.broadcasted_iota(jnp.int32, scores.shape, 1)
        lines = lax.broadcasted_iota(jnp.int32, scores.shape, 0)
        upper = lines < classes
        valid = (lanes < ROT) | ((lanes >= SPAN) & (lanes < SPAN + ROT))
        valid = valid | (upper & (lanes >= 2 * SPAN) & (lanes < 2 * SPAN + ROT))
        scores = jnp.where(valid, scores, NEGATIVE)
        peak = jnp.max(jnp.max(scores, axis=0, keepdims=True), axis=1, keepdims=True)
        w = jnp.where(valid, jnp.exp(scores - peak), 0.0)
        total = jnp.sum(jnp.sum(w, axis=0, keepdims=True), axis=1, keepdims=True)
        stat_ref[pl.ds(2 * slot, 1), :] = jnp.broadcast_to(peak, (1, LANES))
        stat_ref[pl.ds(2 * slot + 1, 1), :] = jnp.broadcast_to(total, (1, LANES))
        after, before = pltpu.roll(w, LANES - SPAN, 1), pltpu.roll(w, SPAN, 1)
        start = jnp.where(upper, SPAN, 0)
        paired = jnp.where(lanes < start + SPAN, w + after, before - w)
        paired = jnp.where(lanes < start + 2 * SPAN, paired, 0.0)
        weight_ref[slot] = jnp.where(lanes < start, w, paired)

    def two(step, carry):
        one(2 * step, moved_a, picked_a, sums_a)
        one(2 * step + 1, moved_b, picked_b, sums_b)
        return carry

    lax.fori_loop(0, lax.div(number + 1, 2), two, 0)


def score(place, buffers, refs, tables, slots, classes):
    count, total = len(buffers), sum(buffer.shape[0] for buffer in buffers)
    width = refs.shape[2]
    return pl.pallas_call(
        functools.partial(score_kernel, count),
        out_shape=(
            jax.ShapeDtypeStruct((slots, 2 * classes, LANES), jnp.float32),
            jax.ShapeDtypeStruct((2 * slots, LANES), jnp.float32),
            jax.ShapeDtypeStruct((slots, 3), jnp.int32),
        ),
        in_specs=[SMEM_SPEC] + [HBM_SPEC] * count + [VMEM_SPEC] * 2,
        out_specs=(VMEM_SPEC, VMEM_SPEC, SMEM_SPEC),
        scratch_shapes=[
            pltpu.VMEM((total, IMAGE_ROWS + META_ROWS, LANES), jnp.bfloat16),
            *[pltpu.VMEM((2 * LANES, width), jnp.bfloat16)] * 2,
            *[pltpu.VMEM((48 * classes, width), jnp.bfloat16)] * 2,
            *[pltpu.VMEM((2 * classes, LANES), jnp.float32)] * 2,
            pltpu.VMEM((SPAN, LANES), jnp.int32),
            pltpu.VMEM((total, LANES), jnp.int32),
            pltpu.SMEM((total, LANES), jnp.int32),
            pltpu.SMEM((total + 1,), jnp.int32),
            pltpu.SemaphoreType.DMA((count,)),
            pltpu.SemaphoreType.DMA,
        ],
        compiler_params=pltpu.CompilerParams(vmem_limit_bytes=VMEM_LIMIT),
        cost_estimate=pl.CostEstimate(flops=10**10, bytes_accessed=10**7, transcendentals=0),
        name="score",
    )(place, *buffers, refs, tables)


def weight_kernel(flip, place_ref, partner_ref, weight_ref, *refs):
    stat_refs, out_ref = refs[:-1], refs[-1]
    slots, lines, _ = weight_ref.shape
    my_cls = place_ref[0]
    done = []
    for slot in range(slots):
        other, other_slot = partner_ref[slot, OTHER], partner_ref[slot, OTHER_SLOT]
        at = pl.ds(2 * other_slot, 2)
        if flip:
            mine = stat_refs[0][2 * slot : 2 * slot + 2, :]
            theirs = mine
            for k in range(1, len(stat_refs)):
                theirs = jnp.where(jnp.bitwise_xor(other, my_cls) == k, stat_refs[k][at, :], theirs)
        else:
            mine = stat_refs[0][my_cls, 2 * slot : 2 * slot + 2, :]
            theirs = stat_refs[0][other, at, :]
        peak = jnp.maximum(mine[0:1], theirs[0:1])
        gain = jnp.exp(mine[0:1] - peak)
        mass = mine[1:2] * gain + theirs[1:2] * jnp.exp(theirs[0:1] - peak)
        factor = gain / jnp.where(partner_ref[slot, FILLED] > 0, mass, 1.0)
        done.append(weight_ref[slot] * factor)
    out_ref[...] = jnp.concatenate(done, axis=0).astype(out_ref.dtype)


def normalise(flip, place, partners, weights, stats):
    slots, lines, _ = weights.shape
    return pl.pallas_call(
        functools.partial(weight_kernel, flip),
        out_shape=jax.ShapeDtypeStruct((slots * lines, LANES), jnp.bfloat16),
        in_specs=[SMEM_SPEC] * 2 + [VMEM_SPEC] * (1 + len(stats)),
        out_specs=VMEM_SPEC,
        name="normalise",
    )(place, partners, weights, *stats)


def sum_kernel(weight_rows, relative, z_size, y_size, lines, local, width, count, n_weights, first, last, place_ref, *refs):
    refs = list(refs)
    image_refs = [refs.pop(0) for _ in range(count)]
    weight_refs = [refs.pop(0) for _ in range(n_weights)]
    table_ref = refs.pop(0)
    given = None if first else [refs.pop(0), refs.pop(0)]
    out_ref = refs.pop(0) if last else None
    if not last:
        totals, mass = refs.pop(0), refs.pop(0)
    images, weights, moved_a, moved_b, spread_a, spread_b, index_ref, meta_vmem, meta, active = refs[:10]
    image_sem, meta_sem = refs[10:12]
    if last:
        totals, mass = refs[12:14]
    given_sem = refs[-1]
    depth, wave = images.shape[0], images.shape[1]
    per_row = weight_rows
    chunk = weight_refs[0].shape[0]
    classes = lines // 2
    waves = sum(ref.shape[0] for ref in image_refs) // wave

    def copies(w):
        out, at = [], 0
        for b, ref in enumerate(image_refs):
            size = ref.shape[0]
            low, high = max(at, w * wave), min(at + size, (w + 1) * wave)
            if low < high:
                source = ref.at[pl.ds(low - at, high - low)]
                target = images.at[w % depth, pl.ds(low - w * wave, high - low)]
                out.append(pltpu.make_async_copy(source, target, image_sem.at[w % depth, b]))
            at += size
        return out

    for w in range(min(depth, waves)):
        for copy in copies(w):
            copy.start()
    if first:
        mass[...] = jnp.zeros_like(mass)
        totals[...] = jnp.zeros_like(totals)
    else:
        held = [pltpu.make_async_copy(g, t, given_sem.at[k]) for k, (g, t) in enumerate(zip(given, (totals, mass)))]
        for copy in held:
            copy.start()
    moved_a[...] = jnp.zeros_like(moved_a)
    moved_b[...] = jnp.zeros_like(moved_b)
    for b in range(n_weights):
        weights[b * chunk : (b + 1) * chunk, :] = weight_refs[b][...].astype(jnp.float32)
    my_cls, my_dom = place_ref[0], place_ref[1]
    my_z, my_y = lax.div(my_dom, y_size), lax.rem(my_dom, y_size)
    lane = lax.broadcasted_iota(jnp.int32, (lines, LANES), 1)
    index_ref[...] = turned_lanes(-1)

    for w in range(waves):
        for copy in copies(w):
            copy.wait()
        here = images.at[w % depth]
        for i in range(wave):
            read_meta(here[i, IMAGE_ROWS:, :], meta_vmem, i)
        move_metas(meta_vmem, meta, meta_sem)
        number = collect(meta, active, wave, my_cls)
        if w == 0 and not first:
            for copy in held:
                copy.wait()

        def prepare_one(at, moved, spread):
            i = active[jnp.minimum(at, number - 1)]
            share = jnp.where(at < number, 1.0, 0.0).astype(jnp.float32)
            side = side_of(meta, i, my_cls)
            q = meta[i, DOM]
            if relative:
                d_z = lax.rem(my_z - lax.div(q, y_size) + z_size, z_size)
                d_y = lax.rem(my_y - lax.rem(q, y_size) + y_size, y_size)
                q = d_y * z_size + d_z
            at = pl.multiple_of(q * per_row + meta[i, SLOT + side] * lines, lines)
            mine = weights[pl.ds(at, lines), :] * share
            def circulant(j):
                line = []
                for half in range(2):
                    at = half * classes + j
                    row = jnp.broadcast_to(mine[at : at + 1], (8, LANES))
                    tiles = [take_lanes(row, index_ref[g * 8 : (g + 1) * 8, :]) for g in range(SPAN // 8)]
                    line.append(jnp.concatenate(tiles, axis=0))
                return jnp.concatenate(line, axis=1)

            def one_step(step):
                re, im, (c1, s1, c2, s2) = step_pieces(here, i, table_ref, step)
                store_moved(moved, step, 0, [re, re * c1, im * s1, re * c2, im * s2])
                store_moved(moved, step, 1, [im, im * c1, -re * s1, im * c2, -re * s2])
                for j in range(step * 2, min(step * 2 + 2, classes), 2):
                    both = jnp.concatenate([circulant(j), circulant(j + 1)], axis=0)
                    spread[j * SPAN : (j + 2) * SPAN, :] = both.astype(jnp.bfloat16)
                if step == STEP_ANGLES - 1:
                    plain = jnp.where(lane < 2 * SPAN, mine, 0.0)
                    plain_high = jnp.where(lane < SPAN, mine, 0.0)
                    for j in range(classes):
                        c = meta[i, CLASS + side * classes + j]
                        mass[pl.ds(c, 1), :] += plain[j : j + 1] + plain_high[classes + j : classes + j + 1]

            return one_step

        def add_one(at, moved, spread, one_step):
            i = active[jnp.minimum(at, number - 1)]
            side = side_of(meta, i, my_cls)
            chosen = [meta[i, CLASS + side * classes + j] for j in range(classes)]
            used = LANES + 2 * SPAN
            added = jnp.dot(spread[:, :used], moved[:used, :], preferred_element_type=jnp.float32)
            for step in range(STEP_ANGLES):
                one_step(step)
            for j in range(classes):
                for tile in range(width // LANES):
                    to = pl.ds(pl.multiple_of(tile * local * SPAN + chosen[j] * SPAN, 8), SPAN)
                    totals[to, :] += added[j * SPAN : (j + 1) * SPAN, tile * LANES : (tile + 1) * LANES]

        def two(step, carry):
            at = 2 * step
            add_one(at, moved_a, spread_a, prepare_one(at + 1, moved_b, spread_b))
            add_one(at + 1, moved_b, spread_b, prepare_one(at + 2, moved_a, spread_a))
            return carry

        @pl.when(number > 0)
        def _():
            start = prepare_one(0, moved_a, spread_a)
            for step in range(STEP_ANGLES):
                start(step)

        lax.fori_loop(0, lax.div(number + 1, 2), two, 0)
        if w + depth < waves:
            for copy in copies(w + depth):
                copy.start()

    if not last:
        return
    scale = 1.0 / (jnp.sum(mass[:local, :], axis=1, keepdims=True) + PRIOR_MASS)
    for turn in range(ROT):
        for tile in range(width // LANES):
            line = totals[pl.ds(tile * local * SPAN + ROT - 1 - turn, local, stride=SPAN), :]
            out_ref[:, pl.ds(turn * width + tile * LANES, LANES)] = (line * scale).astype(out_ref.dtype)


def class_sum(place, buffers, weights, tables, given, last, relative, z_size, y_size, local, width, lines, weight_rows):
    count = len(buffers)
    total = sum(buffer.shape[0] for buffer in buffers)
    wave = total if total <= 128 else math.gcd(total, 128)
    depth = min(2, total // wave)
    totals = (width // LANES * local * SPAN, LANES)
    mass = (-(-local // 8) * 8, LANES)
    first = given is None
    out = jax.ShapeDtypeStruct((local, ROT * width), jnp.bfloat16)
    held = tuple(jax.ShapeDtypeStruct(shape, jnp.float32) for shape in (totals, mass))
    scratch = [
        pltpu.VMEM((depth, wave, IMAGE_ROWS + META_ROWS, LANES), jnp.bfloat16),
        pltpu.VMEM((len(weights) * weights[0].shape[0], LANES), jnp.float32),
        pltpu.VMEM((2 * LANES, width), jnp.bfloat16),
        pltpu.VMEM((2 * LANES, width), jnp.bfloat16),
        pltpu.VMEM((lines // 2 * SPAN, 2 * LANES), jnp.bfloat16),
        pltpu.VMEM((lines // 2 * SPAN, 2 * LANES), jnp.bfloat16),
        pltpu.VMEM((SPAN, LANES), jnp.int32),
        pltpu.VMEM((wave, LANES), jnp.int32),
        pltpu.SMEM((wave, LANES), jnp.int32),
        pltpu.SMEM((wave + 1,), jnp.int32),
        pltpu.SemaphoreType.DMA((depth, count)),
        pltpu.SemaphoreType.DMA,
    ]
    if last:
        scratch += [pltpu.VMEM(totals, jnp.float32), pltpu.VMEM(mass, jnp.float32)]
    scratch += [pltpu.SemaphoreType.DMA((2,))]
    return pl.pallas_call(
        functools.partial(
            sum_kernel, weight_rows, relative, z_size, y_size, lines, local, width, count, len(weights), first, last
        ),
        out_shape=out if last else held,
        in_specs=[SMEM_SPEC]
        + [HBM_SPEC] * count
        + [VMEM_SPEC] * (len(weights) + 1)
        + ([] if first else [HBM_SPEC] * 2),
        out_specs=VMEM_SPEC if last else (VMEM_SPEC, VMEM_SPEC),
        scratch_shapes=scratch,
        compiler_params=pltpu.CompilerParams(vmem_limit_bytes=VMEM_LIMIT),
        cost_estimate=pl.CostEstimate(flops=total * 2 * 10**8, bytes_accessed=10**7, transcendentals=0),
        name="class_sum",
    )(place, *buffers, *weights, tables, *([] if first else given))


def shards(x_size, y_size, z_size, particles, references, candidates, offsets):
    groups = lax.axis_size("cls")
    doms = lax.axis_size("dom")
    count, width = particles.shape
    local = references.shape[0]
    classes = candidates.shape[1] // 2
    block_width = width // ROT
    slots = groups * (count // 2)
    tables = trig_tables()
    place = jnp.stack([lax.axis_index("cls"), lax.axis_index("dom")]).astype(jnp.int32)

    def moves(goal):
        out = []
        for cls in range(groups):
            for dom in range(doms):
                x, core, z, y = goal(cls // 2, cls % 2, dom // y_size, dom % y_size)
                to = ((x % x_size) * 2 + core) * doms + (z % z_size) * y_size + y % y_size
                out.append((cls * doms + dom, to))
        return out

    def send(value, goal):
        return lax.ppermute(value, ("cls", "dom"), moves(goal))

    swap = functools.partial(send, goal=lambda x, c, z, y: (x, 1 - c, z, y))
    along_z = functools.partial(send, goal=lambda x, c, z, y: (x, c, z + 1, y))
    back_z = functools.partial(send, goal=lambda x, c, z, y: (x, c, z - 1, y))
    early = functools.partial(send, goal=lambda x, c, z, y: (x + 1 - c, c, z, y + c))
    late = functools.partial(send, goal=lambda x, c, z, y: (x + c, c, z, y + 1 - c))

    images = particles.reshape(count, width // LANES, LANES)
    record = jnp.concatenate([candidates, offsets], axis=1)
    mine, rest = prepare(place, record, swap(record), images, swap(images), jnp.asarray(tables), local)
    refs = lax.optimization_barrier((references, mine))[0].reshape(local, ROT, block_width)
    steps = jnp.asarray(tables[:, 1])
    tuned = x_size == 2 and y_size == 2 and z_size == 4
    if tuned:
        e0, l0, z1 = early(mine), late(mine), along_z(mine)
        e0, l0, z1, refs = lax.optimization_barrier((e0, l0, z1, refs))
        near = jnp.concatenate([e0, l0])
        row = [mine, rest, near, swap(near)]
        e1, l1, z2, f0 = early(z1), late(z1), along_z(z1), late(e0)
        z3 = back_z(lax.optimization_barrier((mine, z1))[0])
        weights, stats, partners = score(place, row, refs, steps, slots, classes)
        stats = [
            stats,
            swap(stats),
            send(stats, lambda x, c, z, y: (x + 1, c, z, y)),
            send(stats, lambda x, c, z, y: (x + 1, 1 - c, z, y)),
        ]
        z2_late, e1_late, *_ = lax.optimization_barrier((z2, e1, *stats))
        e2, f1 = early(z2_late), late(e1_late)
        weights = normalise(tuned, place, partners, weights, stats)
        *held, weights = lax.optimization_barrier((z1, z2, z3, e1, l1, f0, weights))
        weights = [weights] + [send(weights, lambda x, c, z, y, dz=dz: (x, c, z + dz, y)) for dz in range(1, z_size)]
        weights = jnp.concatenate(weights)
        first = jnp.concatenate(held)
        first_back = swap(first)
        z2_last, e2_last, near_last, f0_last, weights = lax.optimization_barrier((z2, e2, near, f0, weights))
        l2, f2, back = late(z2_last), late(e2_last), back_z(jnp.concatenate([near_last, f0_last]))
        weights = [weights, send(weights, lambda x, c, z, y: (x, c, z, y + 1))]
        second = jnp.concatenate([f1, e2])
        parts = [[*row, first, first_back, second], [swap(second), l2, f2, back]]
    else:
        row = lax.all_gather(mine, "cls", axis=0, tiled=True)
        parts = [[lax.all_gather(row, "dom", axis=0, tiled=True)]]
        weights, stats, partners = score(place, [row], refs, steps, slots, classes)
        stats = [lax.all_gather(stats, "cls", axis=0, tiled=False)]
        weights = normalise(tuned, place, partners, weights, stats)
        weights = [lax.all_gather(weights, "dom", axis=0, tiled=True)]
    held = None
    for k, part in enumerate(parts):
        if k:
            *end, _ = lax.optimization_barrier((*part[1:], held[1]))
            part = part[:1] + end + [swap(block) for block in end]
        held = class_sum(
            place, part, weights, steps, held, k == len(parts) - 1, tuned, z_size, y_size, local, block_width, 2 * classes, slots * 2 * classes
        )
    return held


def solution(mesh):
    coords = [device.coords for device in mesh.devices.flat]
    sizes = [len({c[axis] for c in coords}) for axis in range(3)]
    in_specs = (
        P(("cls", "dom"), None),
        P("cls", None),
        P(("cls", "dom"), None),
        P(("cls", "dom"), None),
    )
    out_specs = P("cls", None)
    return jax.shard_map(
        functools.partial(shards, *sizes),
        mesh=mesh,
        in_specs=in_specs,
        out_specs=out_specs,
        check_vma=False,
    )
```

```python
import functools
import math

import jax
import jax.numpy as jnp
import numpy as np
from jax import lax
from jax.experimental import pallas as pl
from jax.experimental.pallas import tpu as pltpu
from jax.sharding import PartitionSpec as P

CYCLES = 128
ANGLES = 144
ROT = 36
SHIFTS = 5
BOX = 256
LANES = 128
SPAN = 40
STEP_ANGLES = ANGLES // ROT
PIECES = 2 * STEP_ANGLES
IMAGE_ROWS = PIECES * SPAN
REACH = 7

SOFTMAX_WARMTH = 2.0
PRIOR_MASS = 1.0
NEGATIVE = -1e30
META_ROWS = 16
VMEM_LIMIT = 60 * 1024 * 1024
DOM, OWNER, SLOT, CLASS = 0, 1, 3, 5
FILLED, OTHER, OTHER_SLOT = 0, 1, 2


def trig_tables():
    theta = 2.0 * np.pi * np.arange(ANGLES) / ANGLES
    radius = np.arange(1, CYCLES + 1)
    out = np.zeros((4, REACH + 1, STEP_ANGLES, SPAN, CYCLES), np.float32)
    for axis, direction in enumerate((np.cos(theta), np.sin(theta))):
        for t in range(REACH + 1):
            phase = 2.0 * np.pi / BOX * t * direction[:, None] * radius[None, :]
            for part, fn in enumerate((np.cos, np.sin)):
                table = fn(phase).reshape(ROT, STEP_ANGLES, CYCLES).transpose(1, 0, 2)
                out[2 * axis + part, t, :, :ROT] = table[:, ::-1]
    return out.reshape(4, REACH + 1, STEP_ANGLES * SPAN, CYCLES)


def axis_phase(table_ref, axis, step, move):
    size = jnp.abs(move)
    sign = jnp.where(move < 0, -1.0, 1.0).astype(jnp.float32)
    at = pl.ds(step * SPAN, SPAN)
    return table_ref[2 * axis, size, at, :], table_ref[2 * axis + 1, size, at, :] * sign


def prep_kernel(local, place_ref, near_ref, far_ref, image_near, image_far, table_ref, mine_ref, rest_ref, raw):
    count = near_ref.shape[0]
    listed = near_ref.shape[1] - 2
    rows = image_near.shape[1]
    half = listed // 2
    share = count // 2
    my_cls, my_dom = place_ref[0], place_ref[1]
    core = lax.rem(my_cls, 2)
    raw[...] = jnp.zeros_like(raw)
    lane = lax.broadcasted_iota(jnp.int32, (META_ROWS, LANES), 1)
    for far in range(2):
        record, image_ref = (far_ref, image_far) if far else (near_ref, image_near)
        source_core = 1 - core if far else core
        source = my_cls - core + source_core
        cand = [[record[u, k] for k in range(listed)] for u in range(count)]
        owner = [[lax.div(c, local) for c in row] for row in cand]
        pair = []
        for u in range(count):
            first = owner[u][0]
            second = first
            for k in range(1, listed):
                second = jnp.where(owner[u][k] != first, owner[u][k], second)
            pair.append((first, second))
        for u in range(count):
            entries = [my_dom, pair[u][0], pair[u][1]]
            for side in range(2):
                value = source * (count // 2)
                for v in range(u):
                    lists = (pair[v][0] == pair[u][side]) | (pair[v][1] == pair[u][side])
                    value = value + jnp.where(lists, 1, 0)
                entries.append(value)
            for side in range(2):
                classes = [jnp.int32(0)] * half
                seen = jnp.int32(0)
                for k in range(listed):
                    hit = owner[u][k] == pair[u][side]
                    for j in range(half):
                        classes[j] = jnp.where(hit & (seen == j), cand[u][k] - pair[u][side] * local, classes[j])
                    seen = seen + jnp.where(hit, 1, 0)
                entries += classes
            tile = jnp.zeros((META_ROWS, LANES), jnp.int32)
            for k, value in enumerate(entries):
                tile = jnp.where(lane == k, value, tile)
            values = image_ref[u].astype(jnp.float32)
            for block in range(rows // PIECES):
                at = rows - (block + 1) * PIECES
                raw[at : at + PIECES, :] = values[block * PIECES : (block + 1) * PIECES]
            moved = []
            for step in range(STEP_ANGLES):
                re = raw[pl.ds(2 * step, SPAN, stride=PIECES), :]
                im = raw[pl.ds(2 * step + 1, SPAN, stride=PIECES), :]
                cx, sx = axis_phase(table_ref, 0, step, record[u, listed])
                cy, sy = axis_phase(table_ref, 1, step, record[u, listed + 1])
                cosine = cx * cy - sx * sy
                sine = sx * cy + cx * sy
                moved += [re * cosine + im * sine, im * cosine - re * sine]
            moved = jnp.concatenate(moved, axis=0).astype(mine_ref.dtype)
            tile = tile.astype(jnp.float32).astype(mine_ref.dtype)
            at = source_core * share + u % share
            role = u // share

            @pl.when(core == role)
            def _():
                mine_ref[at, :IMAGE_ROWS, :] = moved
                mine_ref[at, IMAGE_ROWS:, :] = tile

            @pl.when(core != role)
            def _():
                rest_ref[at, :IMAGE_ROWS, :] = moved
                rest_ref[at, IMAGE_ROWS:, :] = tile


SMEM_SPEC = pl.BlockSpec(memory_space=pltpu.SMEM)
VMEM_SPEC = pl.BlockSpec(memory_space=pltpu.VMEM)
HBM_SPEC = pl.BlockSpec(memory_space=pl.ANY)


def prepare(place, near, far, image_near, image_far, tables, local):
    count = near.shape[0]
    shape = jax.ShapeDtypeStruct((count, IMAGE_ROWS + META_ROWS, LANES), image_near.dtype)
    return pl.pallas_call(
        functools.partial(prep_kernel, local),
        out_shape=(shape, shape),
        in_specs=[SMEM_SPEC] * 3 + [VMEM_SPEC] * 3,
        out_specs=(VMEM_SPEC, VMEM_SPEC),
        scratch_shapes=[pltpu.VMEM((IMAGE_ROWS, LANES), jnp.float32)],
        compiler_params=pltpu.CompilerParams(vmem_limit_bytes=VMEM_LIMIT),
        name="prepare",
    )(place, near, far, image_near, image_far, tables)


def read_meta(source, meta_vmem, row):
    meta_vmem[pl.ds(row, 1), :] = source.astype(jnp.float32)[0:1, :].astype(jnp.int32)


def move_metas(meta_vmem, meta, sem):
    copy = pltpu.make_async_copy(meta_vmem, meta, sem)
    copy.start()
    copy.wait()


def turned_lanes(offset):
    lane = lax.broadcasted_iota(jnp.int32, (SPAN, LANES), 1)
    row = lax.broadcasted_iota(jnp.int32, (SPAN, LANES), 0)
    base = jnp.where(lane >= SPAN, SPAN, 0) + jnp.where(lane >= 2 * SPAN, SPAN, 0)
    base = jnp.where(lane >= 3 * SPAN, 0, base)
    place = jnp.where(lane >= 3 * SPAN, 0, lane - base) - row + offset
    place = jnp.where(place < 0, place + ROT, place)
    place = jnp.where(place < 0, place + ROT, place)
    return base + jnp.minimum(place, ROT - 1)


def take_lanes(values, index):
    return jnp.take_along_axis(values, index, axis=1, mode="promise_in_bounds")


def side_of(meta, i, my_cls):
    return jnp.where(meta[i, OWNER] == my_cls, 0, 1)


def collect(meta, active, total, my_cls, my_dom=None):
    def look(i, n):
        mine = (meta[i, OWNER] == my_cls) | (meta[i, OWNER + 1] == my_cls)
        if my_dom is not None:
            mine = mine & (meta[i, DOM] == my_dom)
        active[n] = i
        return n + jnp.where(mine, 1, 0)

    return lax.fori_loop(0, total, look, jnp.int32(0), unroll=4)


def step_pieces(images, i, table_ref, step):
    values = images[i, 2 * step * SPAN : (2 * step + 2) * SPAN, :].astype(jnp.float32)
    re, im = values[:SPAN], values[SPAN:]
    at = pl.ds(step * SPAN, SPAN)
    return re, im, [table_ref[k, at, :] for k in range(4)]


def store_moved(moved, step, part, blocks):
    at = pl.ds((2 * step + part) * LANES, LANES)
    pad = jnp.zeros((8, LANES), jnp.float32)
    moved[:LANES, at] = jnp.concatenate([*blocks[:3], pad], axis=0).astype(jnp.bfloat16)
    moved[LANES : LANES + 2 * SPAN, at] = jnp.concatenate(blocks[3:], axis=0).astype(jnp.bfloat16)


def score_kernel(count, place_ref, *refs):
    image_refs = refs[:count]
    (
        refs_ref, table_ref, weight_ref, stat_ref, partner_ref,
        images, moved_a, moved_b, picked_a, picked_b, sums_a, sums_b, index_ref, meta_vmem, meta, active, image_sem, sem,
    ) = refs[count:]
    total = images.shape[0]
    slots = weight_ref.shape[0]
    classes = picked_a.shape[0] // 48
    my_cls, my_dom = place_ref[0], place_ref[1]
    copies, at = [], 0
    for b, ref in enumerate(image_refs):
        copies.append(pltpu.make_async_copy(ref, images.at[pl.ds(at, ref.shape[0])], image_sem.at[b]))
        at += ref.shape[0]
    for copy in copies:
        copy.start()
    for ref in (moved_a, moved_b, picked_a, picked_b, sums_a, sums_b, weight_ref, stat_ref):
        ref[...] = jnp.zeros_like(ref)
    for slot in range(slots):
        for k in range(3):
            partner_ref[slot, k] = 0
    for copy in copies:
        copy.wait()
    for i in range(total):
        read_meta(images[i, IMAGE_ROWS:, :], meta_vmem, i)
    move_metas(meta_vmem, meta, sem)
    number = collect(meta, active, total, my_cls, my_dom)
    index_ref[...] = turned_lanes(0)

    def one(at, moved, picked, sums):
        index = active[jnp.minimum(at, number - 1)]
        side = side_of(meta, index, my_cls)
        slot = meta[index, SLOT + side]
        partner_ref[slot, FILLED] = 1
        partner_ref[slot, OTHER] = meta[index, OWNER + 1 - side]
        partner_ref[slot, OTHER_SLOT] = meta[index, SLOT + 1 - side]
        for j in range(classes):
            picked[j * 48 : j * 48 + ROT, :] = refs_ref[meta[index, CLASS + side * classes + j]]
        for step in range(STEP_ANGLES):
            re, im, (c1, s1, c2, s2) = step_pieces(images, index, table_ref, step)
            a1, b1, d1, e1 = re * c1, im * s1, im * c1, re * s1
            a2, b2, d2, e2 = re * c2, im * s2, im * c2, re * s2
            store_moved(moved, step, 0, [re, a1 + b1, a1 - b1, a2 + b2, a2 - b2])
            store_moved(moved, step, 1, [im, d1 - e1, d1 + e1, d2 - e2, d2 + e2])
        for half in range(2):
            pairs = lax.dot_general(
                picked[...],
                moved[half * LANES : (half + 1) * LANES, :],
                (((1,), (1,)), ((), ())),
                preferred_element_type=jnp.float32,
            )
            for j in range(classes):
                total = jnp.zeros((8, LANES), jnp.float32)
                for group in range(SPAN // 8):
                    at = j * 48 + group * 8
                    total = total + take_lanes(pairs[at : at + 8], index_ref[group * 8 : (group + 1) * 8, :])
                sums[pl.ds(half * classes + j, 1), :] = jnp.sum(total, axis=0, keepdims=True)
        scores = SOFTMAX_WARMTH * sums[...]
        lanes = lax.broadcasted_iota(jnp.int32, scores.shape, 1)
        lines = lax.broadcasted_iota(jnp.int32, scores.shape, 0)
        upper = lines < classes
        valid = (lanes < ROT) | ((lanes >= SPAN) & (lanes < SPAN + ROT))
        valid = valid | (upper & (lanes >= 2 * SPAN) & (lanes < 2 * SPAN + ROT))
        scores = jnp.where(valid, scores, NEGATIVE)
        peak = jnp.max(jnp.max(scores, axis=0, keepdims=True), axis=1, keepdims=True)
        w = jnp.where(valid, jnp.exp(scores - peak), 0.0)
        total = jnp.sum(jnp.sum(w, axis=0, keepdims=True), axis=1, keepdims=True)
        stat_ref[pl.ds(2 * slot, 1), :] = jnp.broadcast_to(peak, (1, LANES))
        stat_ref[pl.ds(2 * slot + 1, 1), :] = jnp.broadcast_to(total, (1, LANES))
        after, before = pltpu.roll(w, LANES - SPAN, 1), pltpu.roll(w, SPAN, 1)
        start = jnp.where(upper, SPAN, 0)
        paired = jnp.where(lanes < start + SPAN, w + after, before - w)
        paired = jnp.where(lanes < start + 2 * SPAN, paired, 0.0)
        weight_ref[slot] = jnp.where(lanes < start, w, paired)

    def two(step, carry):
        one(2 * step, moved_a, picked_a, sums_a)
        one(2 * step + 1, moved_b, picked_b, sums_b)
        return carry

    lax.fori_loop(0, lax.div(number + 1, 2), two, 0)


def score(place, buffers, refs, tables, slots, classes):
    count, total = len(buffers), sum(buffer.shape[0] for buffer in buffers)
    width = refs.shape[2]
    return pl.pallas_call(
        functools.partial(score_kernel, count),
        out_shape=(
            jax.ShapeDtypeStruct((slots, 2 * classes, LANES), jnp.float32),
            jax.ShapeDtypeStruct((2 * slots, LANES), jnp.float32),
            jax.ShapeDtypeStruct((slots, 3), jnp.int32),
        ),
        in_specs=[SMEM_SPEC] + [HBM_SPEC] * count + [VMEM_SPEC] * 2,
        out_specs=(VMEM_SPEC, VMEM_SPEC, SMEM_SPEC),
        scratch_shapes=[
            pltpu.VMEM((total, IMAGE_ROWS + META_ROWS, LANES), jnp.bfloat16),
            *[pltpu.VMEM((2 * LANES, width), jnp.bfloat16)] * 2,
            *[pltpu.VMEM((48 * classes, width), jnp.bfloat16)] * 2,
            *[pltpu.VMEM((2 * classes, LANES), jnp.float32)] * 2,
            pltpu.VMEM((SPAN, LANES), jnp.int32),
            pltpu.VMEM((total, LANES), jnp.int32),
            pltpu.SMEM((total, LANES), jnp.int32),
            pltpu.SMEM((total + 1,), jnp.int32),
            pltpu.SemaphoreType.DMA((count,)),
            pltpu.SemaphoreType.DMA,
        ],
        compiler_params=pltpu.CompilerParams(vmem_limit_bytes=VMEM_LIMIT),
        cost_estimate=pl.CostEstimate(flops=10**10, bytes_accessed=10**7, transcendentals=0),
        name="score",
    )(place, *buffers, refs, tables)


def weight_kernel(flip, place_ref, partner_ref, weight_ref, *refs):
    stat_refs, out_ref = refs[:-1], refs[-1]
    slots, lines, _ = weight_ref.shape
    my_cls = place_ref[0]
    done = []
    for slot in range(slots):
        other, other_slot = partner_ref[slot, OTHER], partner_ref[slot, OTHER_SLOT]
        at = pl.ds(2 * other_slot, 2)
        if flip:
            mine = stat_refs[0][2 * slot : 2 * slot + 2, :]
            theirs = mine
            for k in range(1, len(stat_refs)):
                theirs = jnp.where(jnp.bitwise_xor(other, my_cls) == k, stat_refs[k][at, :], theirs)
        else:
            mine = stat_refs[0][my_cls, 2 * slot : 2 * slot + 2, :]
            theirs = stat_refs[0][other, at, :]
        peak = jnp.maximum(mine[0:1], theirs[0:1])
        gain = jnp.exp(mine[0:1] - peak)
        mass = mine[1:2] * gain + theirs[1:2] * jnp.exp(theirs[0:1] - peak)
        factor = gain / jnp.where(partner_ref[slot, FILLED] > 0, mass, 1.0)
        done.append(weight_ref[slot] * factor)
    out_ref[...] = jnp.concatenate(done, axis=0).astype(out_ref.dtype)


def normalise(flip, place, partners, weights, stats):
    slots, lines, _ = weights.shape
    return pl.pallas_call(
        functools.partial(weight_kernel, flip),
        out_shape=jax.ShapeDtypeStruct((slots * lines, LANES), jnp.bfloat16),
        in_specs=[SMEM_SPEC] * 2 + [VMEM_SPEC] * (1 + len(stats)),
        out_specs=VMEM_SPEC,
        name="normalise",
    )(place, partners, weights, *stats)


def sum_kernel(weight_rows, relative, z_size, y_size, lines, local, width, count, n_weights, first, last, place_ref, *refs):
    refs = list(refs)
    image_refs = [refs.pop(0) for _ in range(count)]
    weight_refs = [refs.pop(0) for _ in range(n_weights)]
    table_ref = refs.pop(0)
    given = None if first else [refs.pop(0), refs.pop(0)]
    out_ref = refs.pop(0) if last else None
    if not last:
        totals, mass = refs.pop(0), refs.pop(0)
    images, weights, moved_a, moved_b, spread_a, spread_b, index_ref, meta_vmem, meta, active = refs[:10]
    image_sem, meta_sem = refs[10:12]
    if last:
        totals, mass = refs[12:14]
    given_sem = refs[-1]
    depth, wave = images.shape[0], images.shape[1]
    per_row = weight_rows
    chunk = weight_refs[0].shape[0]
    classes = lines // 2
    waves = sum(ref.shape[0] for ref in image_refs) // wave

    def copies(w):
        out, at = [], 0
        for b, ref in enumerate(image_refs):
            size = ref.shape[0]
            low, high = max(at, w * wave), min(at + size, (w + 1) * wave)
            if low < high:
                source = ref.at[pl.ds(low - at, high - low)]
                target = images.at[w % depth, pl.ds(low - w * wave, high - low)]
                out.append(pltpu.make_async_copy(source, target, image_sem.at[w % depth, b]))
            at += size
        return out

    for w in range(min(depth, waves)):
        for copy in copies(w):
            copy.start()
    if first:
        mass[...] = jnp.zeros_like(mass)
        totals[...] = jnp.zeros_like(totals)
    else:
        held = [pltpu.make_async_copy(g, t, given_sem.at[k]) for k, (g, t) in enumerate(zip(given, (totals, mass)))]
        for copy in held:
            copy.start()
    moved_a[...] = jnp.zeros_like(moved_a)
    moved_b[...] = jnp.zeros_like(moved_b)
    for b in range(n_weights):
        weights[b * chunk : (b + 1) * chunk, :] = weight_refs[b][...].astype(jnp.float32)
    my_cls, my_dom = place_ref[0], place_ref[1]
    my_z, my_y = lax.div(my_dom, y_size), lax.rem(my_dom, y_size)
    lane = lax.broadcasted_iota(jnp.int32, (lines, LANES), 1)
    index_ref[...] = turned_lanes(-1)

    for w in range(waves):
        for copy in copies(w):
            copy.wait()
        here = images.at[w % depth]
        for i in range(wave):
            read_meta(here[i, IMAGE_ROWS:, :], meta_vmem, i)
        move_metas(meta_vmem, meta, meta_sem)
        number = collect(meta, active, wave, my_cls)
        if w == 0 and not first:
            for copy in held:
                copy.wait()

        def prepare_one(at, moved, spread):
            i = active[jnp.minimum(at, number - 1)]
            share = jnp.where(at < number, 1.0, 0.0).astype(jnp.float32)
            side = side_of(meta, i, my_cls)
            q = meta[i, DOM]
            if relative:
                d_z = lax.rem(my_z - lax.div(q, y_size) + z_size, z_size)
                d_y = lax.rem(my_y - lax.rem(q, y_size) + y_size, y_size)
                q = d_y * z_size + d_z
            at = pl.multiple_of(q * per_row + meta[i, SLOT + side] * lines, lines)
            mine = weights[pl.ds(at, lines), :] * share
            def circulant(j):
                line = []
                for half in range(2):
                    at = half * classes + j
                    row = jnp.broadcast_to(mine[at : at + 1], (8, LANES))
                    tiles = [take_lanes(row, index_ref[g * 8 : (g + 1) * 8, :]) for g in range(SPAN // 8)]
                    line.append(jnp.concatenate(tiles, axis=0))
                return jnp.concatenate(line, axis=1)

            def one_step(step):
                re, im, (c1, s1, c2, s2) = step_pieces(here, i, table_ref, step)
                store_moved(moved, step, 0, [re, re * c1, im * s1, re * c2, im * s2])
                store_moved(moved, step, 1, [im, im * c1, -re * s1, im * c2, -re * s2])
                for j in range(step * 2, min(step * 2 + 2, classes), 2):
                    both = jnp.concatenate([circulant(j), circulant(j + 1)], axis=0)
                    spread[j * SPAN : (j + 2) * SPAN, :] = both.astype(jnp.bfloat16)
                if step == STEP_ANGLES - 1:
                    plain = jnp.where(lane < 2 * SPAN, mine, 0.0)
                    plain_high = jnp.where(lane < SPAN, mine, 0.0)
                    for j in range(classes):
                        c = meta[i, CLASS + side * classes + j]
                        mass[pl.ds(c, 1), :] += plain[j : j + 1] + plain_high[classes + j : classes + j + 1]

            return one_step

        def add_one(at, moved, spread, one_step):
            i = active[jnp.minimum(at, number - 1)]
            side = side_of(meta, i, my_cls)
            chosen = [meta[i, CLASS + side * classes + j] for j in range(classes)]
            used = LANES + 2 * SPAN
            added = jnp.dot(spread[:, :used], moved[:used, :], preferred_element_type=jnp.float32)
            for step in range(STEP_ANGLES):
                one_step(step)
            for j in range(classes):
                for tile in range(width // LANES):
                    to = pl.ds(pl.multiple_of(tile * local * SPAN + chosen[j] * SPAN, 8), SPAN)
                    totals[to, :] += added[j * SPAN : (j + 1) * SPAN, tile * LANES : (tile + 1) * LANES]

        def two(step, carry):
            at = 2 * step
            add_one(at, moved_a, spread_a, prepare_one(at + 1, moved_b, spread_b))
            add_one(at + 1, moved_b, spread_b, prepare_one(at + 2, moved_a, spread_a))
            return carry

        @pl.when(number > 0)
        def _():
            start = prepare_one(0, moved_a, spread_a)
            for step in range(STEP_ANGLES):
                start(step)

        lax.fori_loop(0, lax.div(number + 1, 2), two, 0)
        if w + depth < waves:
            for copy in copies(w + depth):
                copy.start()

    if not last:
        return
    scale = 1.0 / (jnp.sum(mass[:local, :], axis=1, keepdims=True) + PRIOR_MASS)
    for turn in range(ROT):
        for tile in range(width // LANES):
            line = totals[pl.ds(tile * local * SPAN + ROT - 1 - turn, local, stride=SPAN), :]
            out_ref[:, pl.ds(turn * width + tile * LANES, LANES)] = (line * scale).astype(out_ref.dtype)


def class_sum(place, buffers, weights, tables, given, last, relative, z_size, y_size, local, width, lines, weight_rows):
    count = len(buffers)
    total = sum(buffer.shape[0] for buffer in buffers)
    wave = total if total <= 128 else math.gcd(total, 128)
    depth = min(2, total // wave)
    totals = (width // LANES * local * SPAN, LANES)
    mass = (-(-local // 8) * 8, LANES)
    first = given is None
    out = jax.ShapeDtypeStruct((local, ROT * width), jnp.bfloat16)
    held = tuple(jax.ShapeDtypeStruct(shape, jnp.float32) for shape in (totals, mass))
    scratch = [
        pltpu.VMEM((depth, wave, IMAGE_ROWS + META_ROWS, LANES), jnp.bfloat16),
        pltpu.VMEM((len(weights) * weights[0].shape[0], LANES), jnp.float32),
        pltpu.VMEM((2 * LANES, width), jnp.bfloat16),
        pltpu.VMEM((2 * LANES, width), jnp.bfloat16),
        pltpu.VMEM((lines // 2 * SPAN, 2 * LANES), jnp.bfloat16),
        pltpu.VMEM((lines // 2 * SPAN, 2 * LANES), jnp.bfloat16),
        pltpu.VMEM((SPAN, LANES), jnp.int32),
        pltpu.VMEM((wave, LANES), jnp.int32),
        pltpu.SMEM((wave, LANES), jnp.int32),
        pltpu.SMEM((wave + 1,), jnp.int32),
        pltpu.SemaphoreType.DMA((depth, count)),
        pltpu.SemaphoreType.DMA,
    ]
    if last:
        scratch += [pltpu.VMEM(totals, jnp.float32), pltpu.VMEM(mass, jnp.float32)]
    scratch += [pltpu.SemaphoreType.DMA((2,))]
    return pl.pallas_call(
        functools.partial(
            sum_kernel, weight_rows, relative, z_size, y_size, lines, local, width, count, len(weights), first, last
        ),
        out_shape=out if last else held,
        in_specs=[SMEM_SPEC]
        + [HBM_SPEC] * count
        + [VMEM_SPEC] * (len(weights) + 1)
        + ([] if first else [HBM_SPEC] * 2),
        out_specs=VMEM_SPEC if last else (VMEM_SPEC, VMEM_SPEC),
        scratch_shapes=scratch,
        compiler_params=pltpu.CompilerParams(vmem_limit_bytes=VMEM_LIMIT),
        cost_estimate=pl.CostEstimate(flops=total * 2 * 10**8, bytes_accessed=10**7, transcendentals=0),
        name="class_sum",
    )(place, *buffers, *weights, tables, *([] if first else given))


def shards(x_size, y_size, z_size, particles, references, candidates, offsets):
    groups = lax.axis_size("cls")
    doms = lax.axis_size("dom")
    count, width = particles.shape
    local = references.shape[0]
    classes = candidates.shape[1] // 2
    block_width = width // ROT
    slots = groups * (count // 2)
    tables = trig_tables()
    place = jnp.stack([lax.axis_index("cls"), lax.axis_index("dom")]).astype(jnp.int32)

    def moves(goal):
        out = []
        for cls in range(groups):
            for dom in range(doms):
                x, core, z, y = goal(cls // 2, cls % 2, dom // y_size, dom % y_size)
                to = ((x % x_size) * 2 + core) * doms + (z % z_size) * y_size + y % y_size
                out.append((cls * doms + dom, to))
        return out

    def send(value, goal):
        return lax.ppermute(value, ("cls", "dom"), moves(goal))

    swap = functools.partial(send, goal=lambda x, c, z, y: (x, 1 - c, z, y))
    along_z = functools.partial(send, goal=lambda x, c, z, y: (x, c, z + 1, y))
    back_z = functools.partial(send, goal=lambda x, c, z, y: (x, c, z - 1, y))
    early = functools.partial(send, goal=lambda x, c, z, y: (x + 1 - c, c, z, y + c))
    late = functools.partial(send, goal=lambda x, c, z, y: (x + c, c, z, y + 1 - c))

    images = particles.reshape(count, width // LANES, LANES)
    record = jnp.concatenate([candidates, offsets], axis=1)
    mine, rest = prepare(place, record, swap(record), images, swap(images), jnp.asarray(tables), local)
    refs = lax.optimization_barrier((references, mine))[0].reshape(local, ROT, block_width)
    steps = jnp.asarray(tables[:, 1])
    tuned = x_size == 2 and y_size == 2 and z_size == 4
    if tuned:
        e0, l0, z1 = early(mine), late(mine), along_z(mine)
        e0, l0, z1, refs = lax.optimization_barrier((e0, l0, z1, refs))
        near = jnp.concatenate([e0, l0])
        row = [mine, rest, near, swap(near)]
        e1, l1, z2, f0 = early(z1), late(z1), along_z(z1), late(e0)
        z3 = back_z(lax.optimization_barrier((mine, z1))[0])
        weights, stats, partners = score(place, row, refs, steps, slots, classes)
        stats, z2, z3, e1, l1, f0 = lax.optimization_barrier((stats, z2, z3, e1, l1, f0))
        stats = [
            stats,
            swap(stats),
            send(stats, lambda x, c, z, y: (x + 1, c, z, y)),
            send(stats, lambda x, c, z, y: (x + 1, 1 - c, z, y)),
        ]
        z2_late, e1_late, *_ = lax.optimization_barrier((z2, e1, *stats))
        e2, f1 = early(z2_late), late(e1_late)
        weights = normalise(tuned, place, partners, weights, stats)
        *held, weights = lax.optimization_barrier((z1, z2, z3, e1, l1, f0, weights))
        weights = [weights] + [send(weights, lambda x, c, z, y, dz=dz: (x, c, z + dz, y)) for dz in range(1, z_size)]
        weights = jnp.concatenate(weights)
        first = jnp.concatenate(held)
        first_back = swap(first)
        z2_last, e2_last, near_last, f0_last, weights = lax.optimization_barrier((z2, e2, near, f0, weights))
        l2, f2, back = late(z2_last), late(e2_last), back_z(jnp.concatenate([near_last, f0_last]))
        weights = [weights, send(weights, lambda x, c, z, y: (x, c, z, y + 1))]
        second = jnp.concatenate([f1, e2])
        parts = [[*row, first, first_back, second], [swap(second), l2, f2, back]]
    else:
        row = lax.all_gather(mine, "cls", axis=0, tiled=True)
        parts = [[lax.all_gather(row, "dom", axis=0, tiled=True)]]
        weights, stats, partners = score(place, [row], refs, steps, slots, classes)
        stats = [lax.all_gather(stats, "cls", axis=0, tiled=False)]
        weights = normalise(tuned, place, partners, weights, stats)
        weights = [lax.all_gather(weights, "dom", axis=0, tiled=True)]
    held = None
    for k, part in enumerate(parts):
        if k:
            *end, _ = lax.optimization_barrier((*part[1:], held[1]))
            part = part[:1] + end + [swap(block) for block in end]
        held = class_sum(
            place, part, weights, steps, held, k == len(parts) - 1, tuned, z_size, y_size, local, block_width, 2 * classes, slots * 2 * classes
        )
    return held


def solution(mesh):
    coords = [device.coords for device in mesh.devices.flat]
    sizes = [len({c[axis] for c in coords}) for axis in range(3)]
    in_specs = (
        P(("cls", "dom"), None),
        P("cls", None),
        P(("cls", "dom"), None),
        P(("cls", "dom"), None),
    )
    out_specs = P("cls", None)
    return jax.shard_map(
        functools.partial(shards, *sizes),
        mesh=mesh,
        in_specs=in_specs,
        out_specs=out_specs,
        check_vma=False,
    )
```

```python
import functools
import math

import jax
import jax.numpy as jnp
import numpy as np
from jax import lax
from jax.experimental import pallas as pl
from jax.experimental.pallas import tpu as pltpu
from jax.sharding import PartitionSpec as P

CYCLES = 128
ANGLES = 144
ROT = 36
SHIFTS = 5
BOX = 256
LANES = 128
SPAN = 40
STEP_ANGLES = ANGLES // ROT
PIECES = 2 * STEP_ANGLES
IMAGE_ROWS = PIECES * SPAN
REACH = 7

SOFTMAX_WARMTH = 2.0
PRIOR_MASS = 1.0
NEGATIVE = -1e30
META_ROWS = 16
VMEM_LIMIT = 60 * 1024 * 1024
DOM, OWNER, SLOT, CLASS = 0, 1, 3, 5
FILLED, OTHER, OTHER_SLOT = 0, 1, 2


def trig_tables():
    theta = 2.0 * np.pi * np.arange(ANGLES) / ANGLES
    radius = np.arange(1, CYCLES + 1)
    out = np.zeros((4, REACH + 1, STEP_ANGLES, SPAN, CYCLES), np.float32)
    for axis, direction in enumerate((np.cos(theta), np.sin(theta))):
        for t in range(REACH + 1):
            phase = 2.0 * np.pi / BOX * t * direction[:, None] * radius[None, :]
            for part, fn in enumerate((np.cos, np.sin)):
                table = fn(phase).reshape(ROT, STEP_ANGLES, CYCLES).transpose(1, 0, 2)
                out[2 * axis + part, t, :, :ROT] = table[:, ::-1]
    return out.reshape(4, REACH + 1, STEP_ANGLES * SPAN, CYCLES)


def axis_phase(table_ref, axis, step, move):
    size = jnp.abs(move)
    sign = jnp.where(move < 0, -1.0, 1.0).astype(jnp.float32)
    at = pl.ds(step * SPAN, SPAN)
    return table_ref[2 * axis, size, at, :], table_ref[2 * axis + 1, size, at, :] * sign


def prep_kernel(
    local, near_ref, near_off, far_ref, far_off, image_near, image_far, table_ref, mine_ref, rest_ref, raw
):
    count, listed = near_ref.shape
    rows = image_near.shape[1]
    half = listed // 2
    share = count // 2
    my_cls, my_dom = lax.axis_index("cls"), lax.axis_index("dom")
    core = lax.rem(my_cls, 2)
    raw[...] = jnp.zeros_like(raw)
    lane = lax.broadcasted_iota(jnp.int32, (META_ROWS, LANES), 1)
    for far in range(2):
        record, prior, image_ref = (far_ref, far_off, image_far) if far else (near_ref, near_off, image_near)
        source_core = 1 - core if far else core
        source = my_cls - core + source_core
        cand = [[record[u, k] for k in range(listed)] for u in range(count)]
        owner = [[lax.div(c, local) for c in row] for row in cand]
        pair = []
        for u in range(count):
            first = owner[u][0]
            second = first
            for k in range(1, listed):
                second = jnp.where(owner[u][k] != first, owner[u][k], second)
            pair.append((first, second))
        for u in range(count):
            entries = [my_dom, pair[u][0], pair[u][1]]
            for side in range(2):
                value = source * (count // 2)
                for v in range(u):
                    lists = (pair[v][0] == pair[u][side]) | (pair[v][1] == pair[u][side])
                    value = value + jnp.where(lists, 1, 0)
                entries.append(value)
            for side in range(2):
                classes = [jnp.int32(0)] * half
                seen = jnp.int32(0)
                for k in range(listed):
                    hit = owner[u][k] == pair[u][side]
                    for j in range(half):
                        classes[j] = jnp.where(hit & (seen == j), cand[u][k] - pair[u][side] * local, classes[j])
                    seen = seen + jnp.where(hit, 1, 0)
                entries += classes
            tile = jnp.zeros((META_ROWS, LANES), jnp.int32)
            for k, value in enumerate(entries):
                tile = jnp.where(lane == k, value, tile)
            values = image_ref[u].astype(jnp.float32)
            for block in range(rows // PIECES):
                at = rows - (block + 1) * PIECES
                raw[at : at + PIECES, :] = values[block * PIECES : (block + 1) * PIECES]
            moved = []
            for step in range(STEP_ANGLES):
                re = raw[pl.ds(2 * step, SPAN, stride=PIECES), :]
                im = raw[pl.ds(2 * step + 1, SPAN, stride=PIECES), :]
                cx, sx = axis_phase(table_ref, 0, step, prior[u, 0])
                cy, sy = axis_phase(table_ref, 1, step, prior[u, 1])
                cosine = cx * cy - sx * sy
                sine = sx * cy + cx * sy
                moved += [re * cosine + im * sine, im * cosine - re * sine]
            moved = jnp.concatenate(moved, axis=0).astype(mine_ref.dtype)
            tile = tile.astype(jnp.float32).astype(mine_ref.dtype)
            at = source_core * share + u % share
            role = u // share

            @pl.when(core == role)
            def _():
                mine_ref[at, :IMAGE_ROWS, :] = moved
                mine_ref[at, IMAGE_ROWS:, :] = tile

            @pl.when(core != role)
            def _():
                rest_ref[at, :IMAGE_ROWS, :] = moved
                rest_ref[at, IMAGE_ROWS:, :] = tile


SMEM_SPEC = pl.BlockSpec(memory_space=pltpu.SMEM)
VMEM_SPEC = pl.BlockSpec(memory_space=pltpu.VMEM)
HBM_SPEC = pl.BlockSpec(memory_space=pl.ANY)


def prepare(near, far, image_near, image_far, tables, local):
    count = image_near.shape[0]
    shape = jax.ShapeDtypeStruct((count, IMAGE_ROWS + META_ROWS, LANES), image_near.dtype)
    return pl.pallas_call(
        functools.partial(prep_kernel, local),
        out_shape=(shape, shape),
        in_specs=[SMEM_SPEC] * 4 + [VMEM_SPEC] * 3,
        out_specs=(VMEM_SPEC, VMEM_SPEC),
        scratch_shapes=[pltpu.VMEM((IMAGE_ROWS, LANES), jnp.float32)],
        compiler_params=pltpu.CompilerParams(vmem_limit_bytes=VMEM_LIMIT),
        name="prepare",
    )(*near, *far, image_near, image_far, tables)


def read_meta(source, meta_vmem, row):
    meta_vmem[pl.ds(row, 1), :] = source.astype(jnp.float32)[0:1, :].astype(jnp.int32)


def move_metas(meta_vmem, meta, sem):
    copy = pltpu.make_async_copy(meta_vmem, meta, sem)
    copy.start()
    copy.wait()


def turned_lanes(offset):
    lane = lax.broadcasted_iota(jnp.int32, (SPAN, LANES), 1)
    row = lax.broadcasted_iota(jnp.int32, (SPAN, LANES), 0)
    base = jnp.where(lane >= SPAN, SPAN, 0) + jnp.where(lane >= 2 * SPAN, SPAN, 0)
    base = jnp.where(lane >= 3 * SPAN, 0, base)
    place = jnp.where(lane >= 3 * SPAN, 0, lane - base) - row + offset
    place = jnp.where(place < 0, place + ROT, place)
    place = jnp.where(place < 0, place + ROT, place)
    return base + jnp.minimum(place, ROT - 1)


def take_lanes(values, index):
    return jnp.take_along_axis(values, index, axis=1, mode="promise_in_bounds")


def side_of(meta, i, my_cls):
    return jnp.where(meta[i, OWNER] == my_cls, 0, 1)


def collect(meta, active, total, my_cls, my_dom=None):
    def look(i, n):
        mine = (meta[i, OWNER] == my_cls) | (meta[i, OWNER + 1] == my_cls)
        if my_dom is not None:
            mine = mine & (meta[i, DOM] == my_dom)
        active[n] = i
        return n + jnp.where(mine, 1, 0)

    return lax.fori_loop(0, total, look, jnp.int32(0), unroll=4)


def step_pieces(images, i, table_ref, step):
    values = images[i, 2 * step * SPAN : (2 * step + 2) * SPAN, :].astype(jnp.float32)
    re, im = values[:SPAN], values[SPAN:]
    at = pl.ds(step * SPAN, SPAN)
    return re, im, [table_ref[k, at, :] for k in range(4)]


def store_moved(moved, step, part, blocks):
    at = pl.ds((2 * step + part) * LANES, LANES)
    pad = jnp.zeros((8, LANES), jnp.float32)
    moved[:LANES, at] = jnp.concatenate([*blocks[:3], pad], axis=0).astype(jnp.bfloat16)
    moved[LANES : LANES + 2 * SPAN, at] = jnp.concatenate(blocks[3:], axis=0).astype(jnp.bfloat16)


def score_kernel(count, *refs):
    image_refs = refs[:count]
    (
        refs_ref, table_ref, weight_ref, stat_ref, partner_ref,
        images, moved_a, moved_b, picked_a, picked_b, sums_a, sums_b, index_ref, meta_vmem, meta, active, image_sem, sem,
    ) = refs[count:]
    total = images.shape[0]
    slots = weight_ref.shape[0]
    classes = picked_a.shape[0] // 48
    my_cls, my_dom = lax.axis_index("cls"), lax.axis_index("dom")
    copies, at = [], 0
    for b, ref in enumerate(image_refs):
        copies.append(pltpu.make_async_copy(ref, images.at[pl.ds(at, ref.shape[0])], image_sem.at[b]))
        at += ref.shape[0]
    for copy in copies:
        copy.start()
    for ref in (moved_a, moved_b, picked_a, picked_b, sums_a, sums_b, weight_ref, stat_ref):
        ref[...] = jnp.zeros_like(ref)
    for slot in range(slots):
        for k in range(3):
            partner_ref[slot, k] = 0
    for copy in copies:
        copy.wait()
    for i in range(total):
        read_meta(images[i, IMAGE_ROWS:, :], meta_vmem, i)
    move_metas(meta_vmem, meta, sem)
    number = collect(meta, active, total, my_cls, my_dom)
    index_ref[...] = turned_lanes(0)

    def one(at, moved, picked, sums):
        index = active[jnp.minimum(at, number - 1)]
        side = side_of(meta, index, my_cls)
        slot = meta[index, SLOT + side]
        partner_ref[slot, FILLED] = 1
        partner_ref[slot, OTHER] = meta[index, OWNER + 1 - side]
        partner_ref[slot, OTHER_SLOT] = meta[index, SLOT + 1 - side]
        for j in range(classes):
            picked[j * 48 : j * 48 + ROT, :] = refs_ref[meta[index, CLASS + side * classes + j]]
        for step in range(STEP_ANGLES):
            re, im, (c1, s1, c2, s2) = step_pieces(images, index, table_ref, step)
            a1, b1, d1, e1 = re * c1, im * s1, im * c1, re * s1
            a2, b2, d2, e2 = re * c2, im * s2, im * c2, re * s2
            store_moved(moved, step, 0, [re, a1 + b1, a1 - b1, a2 + b2, a2 - b2])
            store_moved(moved, step, 1, [im, d1 - e1, d1 + e1, d2 - e2, d2 + e2])
        for half in range(2):
            pairs = lax.dot_general(
                picked[...],
                moved[half * LANES : (half + 1) * LANES, :],
                (((1,), (1,)), ((), ())),
                preferred_element_type=jnp.float32,
            )
            for j in range(classes):
                total = jnp.zeros((8, LANES), jnp.float32)
                for group in range(SPAN // 8):
                    at = j * 48 + group * 8
                    total = total + take_lanes(pairs[at : at + 8], index_ref[group * 8 : (group + 1) * 8, :])
                sums[pl.ds(half * classes + j, 1), :] = jnp.sum(total, axis=0, keepdims=True)
        scores = SOFTMAX_WARMTH * sums[...]
        lanes = lax.broadcasted_iota(jnp.int32, scores.shape, 1)
        lines = lax.broadcasted_iota(jnp.int32, scores.shape, 0)
        upper = lines < classes
        valid = (lanes < ROT) | ((lanes >= SPAN) & (lanes < SPAN + ROT))
        valid = valid | (upper & (lanes >= 2 * SPAN) & (lanes < 2 * SPAN + ROT))
        scores = jnp.where(valid, scores, NEGATIVE)
        peak = jnp.max(jnp.max(scores, axis=0, keepdims=True), axis=1, keepdims=True)
        w = jnp.where(valid, jnp.exp(scores - peak), 0.0)
        total = jnp.sum(jnp.sum(w, axis=0, keepdims=True), axis=1, keepdims=True)
        stat_ref[pl.ds(2 * slot, 1), :] = jnp.broadcast_to(peak, (1, LANES))
        stat_ref[pl.ds(2 * slot + 1, 1), :] = jnp.broadcast_to(total, (1, LANES))
        after, before = pltpu.roll(w, LANES - SPAN, 1), pltpu.roll(w, SPAN, 1)
        start = jnp.where(upper, SPAN, 0)
        paired = jnp.where(lanes < start + SPAN, w + after, before - w)
        paired = jnp.where(lanes < start + 2 * SPAN, paired, 0.0)
        weight_ref[slot] = jnp.where(lanes < start, w, paired)

    def two(step, carry):
        one(2 * step, moved_a, picked_a, sums_a)
        one(2 * step + 1, moved_b, picked_b, sums_b)
        return carry

    lax.fori_loop(0, lax.div(number + 1, 2), two, 0)


def score(buffers, refs, tables, slots, classes):
    count, total = len(buffers), sum(buffer.shape[0] for buffer in buffers)
    width = refs.shape[2]
    return pl.pallas_call(
        functools.partial(score_kernel, count),
        out_shape=(
            jax.ShapeDtypeStruct((slots, 2 * classes, LANES), jnp.float32),
            jax.ShapeDtypeStruct((2 * slots, LANES), jnp.float32),
            jax.ShapeDtypeStruct((slots, 3), jnp.int32),
        ),
        in_specs=[HBM_SPEC] * count + [VMEM_SPEC] * 2,
        out_specs=(VMEM_SPEC, VMEM_SPEC, SMEM_SPEC),
        scratch_shapes=[
            pltpu.VMEM((total, IMAGE_ROWS + META_ROWS, LANES), jnp.bfloat16),
            *[pltpu.VMEM((2 * LANES, width), jnp.bfloat16)] * 2,
            *[pltpu.VMEM((48 * classes, width), jnp.bfloat16)] * 2,
            *[pltpu.VMEM((2 * classes, LANES), jnp.float32)] * 2,
            pltpu.VMEM((SPAN, LANES), jnp.int32),
            pltpu.VMEM((total, LANES), jnp.int32),
            pltpu.SMEM((total, LANES), jnp.int32),
            pltpu.SMEM((total + 1,), jnp.int32),
            pltpu.SemaphoreType.DMA((count,)),
            pltpu.SemaphoreType.DMA,
        ],
        compiler_params=pltpu.CompilerParams(vmem_limit_bytes=VMEM_LIMIT),
        cost_estimate=pl.CostEstimate(flops=10**10, bytes_accessed=10**7, transcendentals=0),
        name="score",
    )(*buffers, refs, tables)


def weight_kernel(flip, partner_ref, weight_ref, *refs):
    stat_refs, out_ref = refs[:-1], refs[-1]
    slots, lines, _ = weight_ref.shape
    my_cls = lax.axis_index("cls")
    done = []
    for slot in range(slots):
        other, other_slot = partner_ref[slot, OTHER], partner_ref[slot, OTHER_SLOT]
        at = pl.ds(2 * other_slot, 2)
        if flip:
            mine = stat_refs[0][2 * slot : 2 * slot + 2, :]
            theirs = mine
            for k in range(1, len(stat_refs)):
                theirs = jnp.where(jnp.bitwise_xor(other, my_cls) == k, stat_refs[k][at, :], theirs)
        else:
            mine = stat_refs[0][my_cls, 2 * slot : 2 * slot + 2, :]
            theirs = stat_refs[0][other, at, :]
        peak = jnp.maximum(mine[0:1], theirs[0:1])
        gain = jnp.exp(mine[0:1] - peak)
        mass = mine[1:2] * gain + theirs[1:2] * jnp.exp(theirs[0:1] - peak)
        factor = gain / jnp.where(partner_ref[slot, FILLED] > 0, mass, 1.0)
        done.append(weight_ref[slot] * factor)
    out_ref[...] = jnp.concatenate(done, axis=0).astype(out_ref.dtype)


def normalise(flip, partners, weights, stats):
    slots, lines, _ = weights.shape
    return pl.pallas_call(
        functools.partial(weight_kernel, flip),
        out_shape=jax.ShapeDtypeStruct((slots * lines, LANES), jnp.bfloat16),
        in_specs=[SMEM_SPEC] + [VMEM_SPEC] * (1 + len(stats)),
        out_specs=VMEM_SPEC,
        name="normalise",
    )(partners, weights, *stats)


def sum_kernel(weight_rows, relative, z_size, y_size, lines, local, width, count, n_weights, first, last, *refs):
    refs = list(refs)
    image_refs = [refs.pop(0) for _ in range(count)]
    weight_refs = [refs.pop(0) for _ in range(n_weights)]
    table_ref = refs.pop(0)
    given = None if first else [refs.pop(0), refs.pop(0)]
    out_ref = refs.pop(0) if last else None
    if not last:
        totals, mass = refs.pop(0), refs.pop(0)
    images, weights, moved_a, moved_b, spread_a, spread_b, index_ref, meta_vmem, meta, active = refs[:10]
    image_sem, meta_sem = refs[10:12]
    if last:
        totals, mass = refs[12:14]
    given_sem = refs[-1]
    depth, wave = images.shape[0], images.shape[1]
    per_row = weight_rows
    chunk = weight_refs[0].shape[0]
    classes = lines // 2
    waves = sum(ref.shape[0] for ref in image_refs) // wave

    def copies(w):
        out, at = [], 0
        for b, ref in enumerate(image_refs):
            size = ref.shape[0]
            low, high = max(at, w * wave), min(at + size, (w + 1) * wave)
            if low < high:
                source = ref.at[pl.ds(low - at, high - low)]
                target = images.at[w % depth, pl.ds(low - w * wave, high - low)]
                out.append(pltpu.make_async_copy(source, target, image_sem.at[w % depth, b]))
            at += size
        return out

    for w in range(min(depth, waves)):
        for copy in copies(w):
            copy.start()
    if first:
        mass[...] = jnp.zeros_like(mass)
        totals[...] = jnp.zeros_like(totals)
    else:
        held = [pltpu.make_async_copy(g, t, given_sem.at[k]) for k, (g, t) in enumerate(zip(given, (totals, mass)))]
        for copy in held:
            copy.start()
    moved_a[...] = jnp.zeros_like(moved_a)
    moved_b[...] = jnp.zeros_like(moved_b)
    for b in range(n_weights):
        weights[b * chunk : (b + 1) * chunk, :] = weight_refs[b][...].astype(jnp.float32)
    my_cls, my_dom = lax.axis_index("cls"), lax.axis_index("dom")
    my_z, my_y = lax.div(my_dom, y_size), lax.rem(my_dom, y_size)
    lane = lax.broadcasted_iota(jnp.int32, (lines, LANES), 1)
    index_ref[...] = turned_lanes(-1)

    for w in range(waves):
        for copy in copies(w):
            copy.wait()
        here = images.at[w % depth]
        for i in range(wave):
            read_meta(here[i, IMAGE_ROWS:, :], meta_vmem, i)
        move_metas(meta_vmem, meta, meta_sem)
        number = collect(meta, active, wave, my_cls)
        if w == 0 and not first:
            for copy in held:
                copy.wait()

        def prepare_one(at, moved, spread):
            i = active[jnp.minimum(at, number - 1)]
            share = jnp.where(at < number, 1.0, 0.0).astype(jnp.float32)
            side = side_of(meta, i, my_cls)
            q = meta[i, DOM]
            if relative:
                d_z = lax.rem(my_z - lax.div(q, y_size) + z_size, z_size)
                d_y = lax.rem(my_y - lax.rem(q, y_size) + y_size, y_size)
                q = d_y * z_size + d_z
            at = pl.multiple_of(q * per_row + meta[i, SLOT + side] * lines, lines)
            mine = weights[pl.ds(at, lines), :] * share
            def circulant(j):
                line = []
                for half in range(2):
                    at = half * classes + j
                    row = jnp.broadcast_to(mine[at : at + 1], (8, LANES))
                    tiles = [take_lanes(row, index_ref[g * 8 : (g + 1) * 8, :]) for g in range(SPAN // 8)]
                    line.append(jnp.concatenate(tiles, axis=0))
                return jnp.concatenate(line, axis=1)

            def one_step(step):
                re, im, (c1, s1, c2, s2) = step_pieces(here, i, table_ref, step)
                store_moved(moved, step, 0, [re, re * c1, im * s1, re * c2, im * s2])
                store_moved(moved, step, 1, [im, im * c1, -re * s1, im * c2, -re * s2])
                for j in range(step * 2, min(step * 2 + 2, classes), 2):
                    both = jnp.concatenate([circulant(j), circulant(j + 1)], axis=0)
                    spread[j * SPAN : (j + 2) * SPAN, :] = both.astype(jnp.bfloat16)
                if step == STEP_ANGLES - 1:
                    plain = jnp.where(lane < 2 * SPAN, mine, 0.0)
                    plain_high = jnp.where(lane < SPAN, mine, 0.0)
                    for j in range(classes):
                        c = meta[i, CLASS + side * classes + j]
                        mass[pl.ds(c, 1), :] += plain[j : j + 1] + plain_high[classes + j : classes + j + 1]

            return one_step

        def add_one(at, moved, spread, one_step):
            i = active[jnp.minimum(at, number - 1)]
            side = side_of(meta, i, my_cls)
            chosen = [meta[i, CLASS + side * classes + j] for j in range(classes)]
            used = LANES + 2 * SPAN
            added = jnp.dot(spread[:, :used], moved[:used, :], preferred_element_type=jnp.float32)
            for step in range(STEP_ANGLES):
                one_step(step)
            for j in range(classes):
                for tile in range(width // LANES):
                    to = pl.ds(pl.multiple_of(tile * local * SPAN + chosen[j] * SPAN, 8), SPAN)
                    totals[to, :] += added[j * SPAN : (j + 1) * SPAN, tile * LANES : (tile + 1) * LANES]

        def two(step, carry):
            at = 2 * step
            add_one(at, moved_a, spread_a, prepare_one(at + 1, moved_b, spread_b))
            add_one(at + 1, moved_b, spread_b, prepare_one(at + 2, moved_a, spread_a))
            return carry

        @pl.when(number > 0)
        def _():
            start = prepare_one(0, moved_a, spread_a)
            for step in range(STEP_ANGLES):
                start(step)

        lax.fori_loop(0, lax.div(number + 1, 2), two, 0)
        if w + depth < waves:
            for copy in copies(w + depth):
                copy.start()

    if not last:
        return
    scale = 1.0 / (jnp.sum(mass[:local, :], axis=1, keepdims=True) + PRIOR_MASS)
    for turn in range(ROT):
        for tile in range(width // LANES):
            line = totals[pl.ds(tile * local * SPAN + ROT - 1 - turn, local, stride=SPAN), :]
            out_ref[:, pl.ds(turn * width + tile * LANES, LANES)] = (line * scale).astype(out_ref.dtype)


def class_sum(buffers, weights, tables, given, last, relative, z_size, y_size, local, width, lines, weight_rows):
    count = len(buffers)
    total = sum(buffer.shape[0] for buffer in buffers)
    wave = total if total <= 128 else math.gcd(total, 128)
    depth = min(2, total // wave)
    totals = (width // LANES * local * SPAN, LANES)
    mass = (-(-local // 8) * 8, LANES)
    first = given is None
    out = jax.ShapeDtypeStruct((local, ROT * width), jnp.bfloat16)
    held = tuple(jax.ShapeDtypeStruct(shape, jnp.float32) for shape in (totals, mass))
    scratch = [
        pltpu.VMEM((depth, wave, IMAGE_ROWS + META_ROWS, LANES), jnp.bfloat16),
        pltpu.VMEM((len(weights) * weights[0].shape[0], LANES), jnp.float32),
        pltpu.VMEM((2 * LANES, width), jnp.bfloat16),
        pltpu.VMEM((2 * LANES, width), jnp.bfloat16),
        pltpu.VMEM((lines // 2 * SPAN, 2 * LANES), jnp.bfloat16),
        pltpu.VMEM((lines // 2 * SPAN, 2 * LANES), jnp.bfloat16),
        pltpu.VMEM((SPAN, LANES), jnp.int32),
        pltpu.VMEM((wave, LANES), jnp.int32),
        pltpu.SMEM((wave, LANES), jnp.int32),
        pltpu.SMEM((wave + 1,), jnp.int32),
        pltpu.SemaphoreType.DMA((depth, count)),
        pltpu.SemaphoreType.DMA,
    ]
    if last:
        scratch += [pltpu.VMEM(totals, jnp.float32), pltpu.VMEM(mass, jnp.float32)]
    scratch += [pltpu.SemaphoreType.DMA((2,))]
    return pl.pallas_call(
        functools.partial(
            sum_kernel, weight_rows, relative, z_size, y_size, lines, local, width, count, len(weights), first, last
        ),
        out_shape=out if last else held,
        in_specs=[HBM_SPEC] * count
        + [VMEM_SPEC] * (len(weights) + 1)
        + ([] if first else [HBM_SPEC] * 2),
        out_specs=VMEM_SPEC if last else (VMEM_SPEC, VMEM_SPEC),
        scratch_shapes=scratch,
        compiler_params=pltpu.CompilerParams(vmem_limit_bytes=VMEM_LIMIT),
        cost_estimate=pl.CostEstimate(flops=total * 2 * 10**8, bytes_accessed=10**7, transcendentals=0),
        name="class_sum",
    )(*buffers, *weights, tables, *([] if first else given))


def shards(x_size, y_size, z_size, particles, references, candidates, offsets):
    groups = lax.axis_size("cls")
    doms = lax.axis_size("dom")
    count, width = particles.shape
    local = references.shape[0]
    classes = candidates.shape[1] // 2
    block_width = width // ROT
    slots = groups * (count // 2)
    tables = trig_tables()

    def moves(goal):
        out = []
        for cls in range(groups):
            for dom in range(doms):
                x, core, z, y = goal(cls // 2, cls % 2, dom // y_size, dom % y_size)
                to = ((x % x_size) * 2 + core) * doms + (z % z_size) * y_size + y % y_size
                out.append((cls * doms + dom, to))
        return out

    def send(value, goal):
        return lax.ppermute(value, ("cls", "dom"), moves(goal))

    swap = functools.partial(send, goal=lambda x, c, z, y: (x, 1 - c, z, y))
    along_z = functools.partial(send, goal=lambda x, c, z, y: (x, c, z + 1, y))
    back_z = functools.partial(send, goal=lambda x, c, z, y: (x, c, z - 1, y))
    early = functools.partial(send, goal=lambda x, c, z, y: (x + 1 - c, c, z, y + c))
    late = functools.partial(send, goal=lambda x, c, z, y: (x + c, c, z, y + 1 - c))

    images = particles.reshape(count, width // LANES, LANES)
    near, far = (candidates, offsets), (swap(candidates), swap(offsets))
    mine, rest = prepare(near, far, images, swap(images), jnp.asarray(tables), local)
    refs = lax.optimization_barrier((references, mine))[0].reshape(local, ROT, block_width)
    steps = jnp.asarray(tables[:, 1])
    tuned = x_size == 2 and y_size == 2 and z_size == 4
    if tuned:
        z1, e0, l0 = along_z(mine), early(mine), late(mine)
        e0, l0, z1, refs = lax.optimization_barrier((e0, l0, z1, refs))
        near = jnp.concatenate([e0, l0])
        row = [mine, rest, near, swap(near)]
        e1, l1, z2, f0 = early(z1), late(z1), along_z(z1), late(e0)
        z3 = back_z(lax.optimization_barrier((mine, z1))[0])
        weights, stats, partners = score(row, refs, steps, slots, classes)
        stats, z2, z3, e1, l1, f0 = lax.optimization_barrier((stats, z2, z3, e1, l1, f0))
        stats = [
            stats,
            swap(stats),
            send(stats, lambda x, c, z, y: (x + 1, c, z, y)),
            send(stats, lambda x, c, z, y: (x + 1, 1 - c, z, y)),
        ]
        z2_late, e1_late, *_ = lax.optimization_barrier((z2, e1, *stats))
        e2, f1 = early(z2_late), late(e1_late)
        weights = normalise(tuned, partners, weights, stats)
        *held, weights = lax.optimization_barrier((z1, z2, z3, e1, l1, f0, weights))
        weights = [weights] + [send(weights, lambda x, c, z, y, dz=dz: (x, c, z + dz, y)) for dz in range(1, z_size)]
        weights = jnp.concatenate(weights)
        first = jnp.concatenate(held)
        first_back = swap(first)
        z2_last, e2_last, near_last, f0_last, weights = lax.optimization_barrier((z2, e2, near, f0, weights))
        l2, f2, back = late(z2_last), late(e2_last), back_z(jnp.concatenate([near_last, f0_last]))
        weights = [weights, send(weights, lambda x, c, z, y: (x, c, z, y + 1))]
        second = jnp.concatenate([f1, e2])
        parts = [[*row, first, first_back, second], [swap(second), l2, f2, back]]
    else:
        row = lax.all_gather(mine, "cls", axis=0, tiled=True)
        parts = [[lax.all_gather(row, "dom", axis=0, tiled=True)]]
        weights, stats, partners = score([row], refs, steps, slots, classes)
        stats = [lax.all_gather(stats, "cls", axis=0, tiled=False)]
        weights = normalise(tuned, partners, weights, stats)
        weights = [lax.all_gather(weights, "dom", axis=0, tiled=True)]
    held = None
    for k, part in enumerate(parts):
        if k:
            *end, _ = lax.optimization_barrier((*part[1:], held[1]))
            part = part[:1] + end + [swap(block) for block in end]
        held = class_sum(
            part, weights, steps, held, k == len(parts) - 1, tuned, z_size, y_size, local, block_width, 2 * classes, slots * 2 * classes
        )
    return held


def solution(mesh):
    coords = [device.coords for device in mesh.devices.flat]
    sizes = [len({c[axis] for c in coords}) for axis in range(3)]
    in_specs = (
        P(("cls", "dom"), None),
        P("cls", None),
        P(("cls", "dom"), None),
        P(("cls", "dom"), None),
    )
    out_specs = P("cls", None)
    return jax.shard_map(
        functools.partial(shards, *sizes),
        mesh=mesh,
        in_specs=in_specs,
        out_specs=out_specs,
        check_vma=False,
    )
```
